32 devices in a mesh: aux: 8 (over z, x), vir: 4 (over y, core).
Axes of the slice: x: 2, y: 2, z: 4, core: 2. Of those that a mesh axis runs over, the one named last changes fastest.
Arguments:
- factors: bfloat16 [2048, 1024, 128], P('aux', 'vir'), may hold values from -0.125 to 0.125
- trials: float32 [1, 1024, 128], P(None, 'vir', 'aux'), may hold values from -6 to 6
- occ_energy: float32 [128], replicated, may hold values from -3 to -0.5
- vir_energy: float32 [1024], P('vir'), may hold values from 0.5 to 3
Outputs:
- trial_out: float32 [1, 1024, 128], P(None, 'vir', 'aux')
- shifts: float32 [2, 1], replicated
The draws below stay inside these ranges and needn't reach their ends.
All inputs are finite; a program needn't handle non-finite values.
Results may differ from the reference program's by a relative error of at most 0.0075.
Values may be sent and summed in bfloat16 or wider, within the bound.
No kernel may reach another device: no remote copies, remote signals or barrier semaphores. Data moves between devices by JAX's collectives and lax.ppermute only.
A program may use at most 128 MiB of HBM per device.

```python
import jax
import jax.numpy as jnp
from jax import lax

P_SIZE = 2048
OCC = 128
VIR = 1024
NT = 1
ITERS = 2


def block_scale(rng, extent, split, smallest, top_value):
    def one(axis_at, parts):
        heights = jax.random.uniform(jax.random.fold_in(jax.random.fold_in(rng, 6), axis_at), (parts,), jnp.float32, smallest / len(split), top_value / len(split))
        return jnp.repeat(jnp.exp(heights), extent[axis_at] // parts).reshape((-1,) + (1,) * (len(extent) - axis_at - 1))

    level = one(*split[0])
    for cut in split[1:]:
        level = level * one(*cut)
    return level


def noise(stream_key, shape, spread, most, cuts=(), held_as=jnp.bfloat16):
    values = spread * jax.random.normal(stream_key, shape, jnp.float32)
    if cuts:
        values = values * block_scale(stream_key, shape, cuts, -0.22, 0.18)
    return jnp.clip(values, -most, most).astype(held_as)


def setup_inputs(seed: int = 0) -> dict:
    key_of = jax.random.split(jax.random.key(seed), 5)
    return {
        "factors": noise(key_of[0], (P_SIZE, VIR, OCC), ((P_SIZE * VIR * OCC) ** -0.25), 0.125, ((0, 8), (1, 4))),
        "trials": noise(key_of[1], (NT, VIR, OCC), 1.0, 6.0, ((1, 4), (2, 8)), jnp.float32),
        "occ_energy": jnp.clip(jax.random.uniform(key_of[2], (OCC,), jnp.float32, -3.0, -0.5), -3.0, -0.5),
        "vir_energy": jnp.clip(0.5 + 2.5 * jax.random.uniform(key_of[3], (VIR,), jnp.float32) ** block_scale(key_of[3], (VIR,), ((0, 4),), -0.2, 0.2), 0.5, 3.0),
    }


def hold_round(values):
    return lax.optimization_barrier(values.astype(jnp.bfloat16)).astype(jnp.float32)

def coupling_of(factors, rounded):
    block_size = 128 if P_SIZE % 128 == 0 else P_SIZE
    blocked = factors.reshape(P_SIZE // block_size, block_size, VIR, OCC)
    rounded_wide = rounded.astype(jnp.float32)

    def add_block(running, factor_block):
        block_wide = factor_block.astype(jnp.float32)
        density = hold_round(jnp.einsum('pai,nai->np', block_wide, rounded_wide))
        pairs = hold_round(jnp.einsum('pai,naj->npij', block_wide, rounded_wide))
        partial_value = 2.0 * jnp.einsum('pai,np->nai', block_wide, density) - jnp.einsum('paj,npij->nai', block_wide, pairs)
        return (running + partial_value, None)
    start_sum = jnp.zeros((NT, VIR, OCC), jnp.float32)
    coupling, ignored = lax.scan(add_block, start_sum, blocked)
    return coupling

def reference(factors, trials, occ_energy, vir_energy):
    energy_gap = vir_energy[:, None] - occ_energy[None, :]
    trial = trials
    shift_list = []
    for iteration in range(ITERS):
        rounded = lax.optimization_barrier(trial.astype(jnp.bfloat16))
        coupling = coupling_of(factors, rounded)
        image = energy_gap[None] * rounded.astype(jnp.float32) + coupling
        quotient = lax.optimization_barrier(jnp.sum(trial * image, axis=(1, 2))) / lax.optimization_barrier(jnp.sum(trial * trial, axis=(1, 2)))
        update = trial - (image - quotient[:, None, None] * trial) / energy_gap[None]
        mean_square = lax.optimization_barrier(jnp.mean(update * update, axis=(1, 2)))
        trial = update * lax.rsqrt(mean_square + 1e-06)[:, None, None]
        shift_list.append(quotient)
    return (trial, jnp.stack(shift_list))
```

```python
import functools

import jax
import jax.numpy as jnp
from jax import lax
from jax.experimental import pallas as pl
from jax.experimental.pallas import tpu as pltpu
from jax.sharding import PartitionSpec as P

ITERS = 2
EVERY = ("aux", "vir")


def contract_body(nv, counts, block, group, order_ref, xt_ref, *refs):
    f_refs, out_ref, acc_ref = refs[:-2], refs[-2], refs[-1]
    step = pl.program_id(0)
    occ, width = xt_ref.shape[1:]
    share = out_ref.shape[2]

    @pl.when(step == 0)
    def _():
        acc_ref[...] = jnp.zeros_like(acc_ref)

    xt = jnp.concatenate([xt_ref[order_ref[k]] for k in range(nv)], axis=1)
    eye = lax.broadcasted_iota(jnp.int32, (occ, occ), 0) == lax.broadcasted_iota(
        jnp.int32, (occ, occ), 1
    )

    def work(blocks):
        for first in range(0, block, group):
            tall = jnp.concatenate(
                [
                    jnp.concatenate([blocks[k][first + q] for q in range(group)], axis=1)
                    for k in range(nv)
                ],
                axis=0,
            )
            pairs = jnp.dot(xt, tall, preferred_element_type=jnp.float32)
            mixes = []
            for q in range(group):
                pair = pairs[:, q * occ : (q + 1) * occ]
                density = jnp.sum(jnp.where(eye, pair, 0.0), keepdims=True)
                density = density.astype(jnp.bfloat16).astype(jnp.float32)
                pair = pair.astype(jnp.bfloat16).astype(jnp.float32)
                mixes.append((jnp.where(eye, 2.0 * density, 0.0) - pair).astype(jnp.bfloat16))
            mix = jnp.concatenate(mixes, axis=0)
            acc_ref[...] += jnp.dot(tall, mix, preferred_element_type=jnp.float32)

    start = 0
    for c, n in enumerate(counts):

        @pl.when((step >= start) & (step < start + n))
        def _(c=c):
            work(f_refs[c * nv : (c + 1) * nv])

        start += n

    @pl.when(step == start - 1)
    def _():
        for k in range(nv):
            turned = acc_ref[k * width : (k + 1) * width, :].T
            for r in range(occ // share):
                out_ref[r, order_ref[k]] = turned[r * share : (r + 1) * share, :].astype(out_ref.dtype)


def contract(order, xt, chunks, aux_count, block, group):
    nv, occ, width = xt.shape
    counts = [chunk[0].shape[0] // block for chunk in chunks]
    specs = [
        pl.BlockSpec(memory_space=pltpu.SMEM),
        pl.BlockSpec((nv, occ, width), lambda g: (0, 0, 0)),
    ]
    start = 0
    for n in counts:
        place = functools.partial(lambda s, m, g: (jnp.clip(g - s, 0, m - 1), 0, 0), start, n)
        specs += [pl.BlockSpec((block, width, occ), place)] * nv
        start += n
    shape = (aux_count, nv, occ // aux_count, width)
    pairs_total = start * block
    return pl.pallas_call(
        functools.partial(contract_body, nv, counts, block, group),
        grid=(start,),
        in_specs=specs,
        out_specs=pl.BlockSpec(shape, lambda g: (0, 0, 0, 0)),
        out_shape=jax.ShapeDtypeStruct(shape, jnp.float32),
        scratch_shapes=[pltpu.VMEM((nv * width, occ), jnp.float32)],
        compiler_params=pltpu.CompilerParams(vmem_limit_bytes=48 * 2**20),
        cost_estimate=pl.CostEstimate(
            flops=4 * pairs_total * nv * width * occ * occ,
            bytes_accessed=2 * pairs_total * nv * width * occ,
            transcendentals=0,
        ),
    )(order, xt, *[part for chunk in chunks for part in chunk])


def spread(share, count):
    copies = jnp.broadcast_to(share[None], (count,) + share.shape)
    return lax.all_to_all(copies, EVERY, 0, 0, tiled=True)


def local(factors, trials, occ_energy, vir_energy):
    na, nv = lax.axis_size("aux"), lax.axis_size("vir")
    count = na * nv
    aux_at, vir_at = lax.axis_index("aux"), lax.axis_index("vir")
    p_count, width, occ = factors.shape
    own = p_count // nv
    share = occ // na
    total = occ * width * nv
    paired = nv & (nv - 1) == 0

    def partner(at, k):
        return at ^ k if paired else (at + k) % nv

    def source(at, k):
        return at ^ k if paired else (at - k) % nv

    block = next(n for n in (8, 4, 2, 1) if own % n == 0)
    tail = max(block, own // 4 // block * block)
    cuts = [(0, own - tail), (own - tail, own)] if own > tail else [(0, own)]

    chunks = []
    for low, high in cuts:
        parts = []
        for k in range(nv):
            piece = lax.dynamic_slice_in_dim(factors, partner(vir_at, k) * own + low, high - low, 0)
            if k:
                piece = lax.ppermute(piece, "vir", [(at, partner(at, k)) for at in range(nv)])
            parts.append(piece)
        chunks.append(parts)
    order = jnp.stack([source(vir_at, k) for k in range(nv)]).astype(jnp.int32)

    trial_own = trials[0].T
    begin = spread(jnp.concatenate([trial_own, vir_energy[None]], axis=0), count)
    begin = begin.reshape(na, nv, share + 1, width)
    trial = begin[:, :, :share]
    gap = begin[:, :, share:] - occ_energy.reshape(na, 1, share, 1)
    gap_own = vir_energy[None, :] - lax.dynamic_slice_in_dim(occ_energy, aux_at * share, share)[:, None]

    def reduce_to_share(partial):
        terms = lax.all_to_all(
            partial.astype(jnp.bfloat16).reshape(count, share, width), EVERY, 0, 0, tiled=True
        )
        return jnp.sum(terms.astype(jnp.float32), axis=0)

    shift_list = []
    for iteration in range(ITERS):
        rounded = trial.astype(jnp.bfloat16)
        xt = rounded.transpose(1, 0, 2, 3).reshape(nv, occ, width)
        if iteration == 0:
            partial = None
            for chunk in chunks:
                part = contract(order, xt, [chunk], na, block, block)
                partial = part if partial is None else partial + part
        else:
            partial = contract(order, xt, chunks, na, block, block)
        coupling = reduce_to_share(partial)
        last = iteration == ITERS - 1
        if last:
            trial_now = lax.dynamic_slice(
                trial, (aux_at, vir_at, 0, 0), (1, 1, share, width)
            ).reshape(share, width)
            gap_now = gap_own
        else:
            trial_now, gap_now = trial, gap
            coupling = spread(coupling.astype(jnp.bfloat16), count).astype(jnp.float32)
            coupling = coupling.reshape(na, nv, share, width)
        image = gap_now * trial_now.astype(jnp.bfloat16).astype(jnp.float32) + coupling
        scaled_trial = trial_now / gap_now
        scaled_diff = trial_now - image / gap_now
        sums = jnp.stack(
            [
                jnp.sum(trial_now * image),
                jnp.sum(trial_now * trial_now),
                jnp.sum(scaled_diff * scaled_diff),
                jnp.sum(scaled_diff * scaled_trial),
                jnp.sum(scaled_trial * scaled_trial),
            ]
        )
        if last:
            sums = jnp.sum(spread(jnp.pad(sums, (0, 3)), count), axis=0)
        shift = sums[0] / sums[1]
        mean_square = (sums[2] + 2.0 * shift * sums[3] + shift * shift * sums[4]) / total
        trial = (scaled_diff + shift * scaled_trial) * lax.rsqrt(mean_square + 1e-06)
        shift_list.append(shift)
    return (trial.T[None], jnp.stack(shift_list)[:, None])


def solution(mesh):
    placed = (P("aux", "vir", None), P(None, "vir", "aux"), P(), P("vir"))
    return jax.shard_map(
        local, mesh=mesh, in_specs=placed, out_specs=(P(None, "vir", "aux"), P()), check_vma=False
    )
```

```python
import functools

import jax
import jax.numpy as jnp
from jax import lax
from jax.experimental import pallas as pl
from jax.experimental.pallas import tpu as pltpu
from jax.sharding import PartitionSpec as P

ITERS = 2
EVERY = ("aux", "vir")


def contract_body(nv, counts, block, group, order_ref, xt_ref, carry_ref, *refs):
    f_refs, out_ref, acc_ref = refs[:-2], refs[-2], refs[-1]
    step = pl.program_id(0)
    occ, width = xt_ref.shape[1:]

    @pl.when(step == 0)
    def _():
        acc_ref[...] = jnp.zeros_like(acc_ref) if carry_ref is None else carry_ref[...]

    xt = jnp.concatenate([xt_ref[order_ref[k]] for k in range(nv)], axis=1)
    eye = lax.broadcasted_iota(jnp.int32, (occ, occ), 0) == lax.broadcasted_iota(
        jnp.int32, (occ, occ), 1
    )

    def work(blocks):
        for first in range(0, block, group):
            tall = jnp.concatenate(
                [
                    jnp.concatenate([blocks[k][first + q] for q in range(group)], axis=1)
                    for k in range(nv)
                ],
                axis=0,
            )
            pairs = jnp.dot(xt, tall, preferred_element_type=jnp.float32)
            mixes = []
            for q in range(group):
                pair = pairs[:, q * occ : (q + 1) * occ]
                density = jnp.sum(jnp.where(eye, pair, 0.0), keepdims=True)
                density = density.astype(jnp.bfloat16).astype(jnp.float32)
                pair = pair.astype(jnp.bfloat16).astype(jnp.float32)
                mixes.append((jnp.where(eye, 2.0 * density, 0.0) - pair).astype(jnp.bfloat16))
            mix = jnp.concatenate(mixes, axis=0)
            acc_ref[...] += jnp.dot(tall, mix, preferred_element_type=jnp.float32)

    start = 0
    for c, n in enumerate(counts):

        @pl.when((step >= start) & (step < start + n))
        def _(c=c):
            work(f_refs[c * nv : (c + 1) * nv])

        start += n

    @pl.when(step == start - 1)
    def _():
        if len(out_ref.shape) == 2:
            out_ref[...] = acc_ref[...]
            return
        share = out_ref.shape[2]
        for k in range(nv):
            turned = acc_ref[k * width : (k + 1) * width, :].T
            for r in range(occ // share):
                rows = turned[r * share : (r + 1) * share, :]
                out_ref[r, order_ref[k]] = rows.astype(out_ref.dtype)


def contract(order, xt, chunks, bounds, block, carry=None, aux_count=None):
    nv, occ, width = xt.shape
    counts = [(high - low) // block for low, high in bounds]
    whole = pl.BlockSpec((nv * width, occ), lambda g, order: (0, 0))
    specs = [pl.BlockSpec((nv, occ, width), lambda g, order: (0, 0, 0))]
    if carry is not None:
        specs.append(whole)
    start = 0
    for n, (low, high) in zip(counts, bounds):

        def near(g, order, s=start, m=n, skip=low // block):
            return (order[nv] + skip + jnp.clip(g - s, 0, m - 1), 0, 0)

        def far(g, order, s=start, m=n):
            return (jnp.clip(g - s, 0, m - 1), 0, 0)

        specs.append(pl.BlockSpec((block, width, occ), near))
        specs += [pl.BlockSpec((block, width, occ), far)] * (nv - 1)
        start += n
    body = functools.partial(contract_body, nv, counts, block, block)
    if carry is None:
        body = functools.partial(lambda f, o, x, *refs: f(o, x, None, *refs), body)
    if aux_count is None:
        out_spec, out = whole, jax.ShapeDtypeStruct((nv * width, occ), jnp.float32)
    else:
        shape = (aux_count, nv, occ // aux_count, width)
        out_spec = pl.BlockSpec(shape, lambda g, order: (0, 0, 0, 0))
        out = jax.ShapeDtypeStruct(shape, jnp.bfloat16)
    return pl.pallas_call(
        body,
        grid_spec=pltpu.PrefetchScalarGridSpec(
            num_scalar_prefetch=1,
            grid=(start,),
            in_specs=specs,
            out_specs=out_spec,
            scratch_shapes=[pltpu.VMEM((nv * width, occ), jnp.float32)],
        ),
        out_shape=out,
        compiler_params=pltpu.CompilerParams(vmem_limit_bytes=48 * 2**20),
        cost_estimate=pl.CostEstimate(
            flops=4 * start * block * nv * width * occ * occ,
            bytes_accessed=2 * start * block * nv * width * occ,
            transcendentals=0,
        ),
    )(order, xt, *([] if carry is None else [carry]), *[part for chunk in chunks for part in chunk])


def five_sums(trial, gap, coupling):
    rounded = trial.astype(jnp.bfloat16).astype(jnp.float32)
    image = gap * rounded + coupling
    scaled_trial = trial / gap
    scaled_diff = trial - image / gap

    def total(values):
        return jnp.sum(values, keepdims=True)

    sums = (
        total(trial * image),
        total(trial * trial),
        total(scaled_diff * scaled_diff),
        total(scaled_diff * scaled_trial),
        total(scaled_trial * scaled_trial),
    )
    return scaled_diff, scaled_trial, sums


def finish(scaled_diff, scaled_trial, sums, count):
    cross_sum, self_sum, diff_sum, mixed_sum, scaled_sum = sums
    shift = cross_sum / self_sum
    mean_square = (diff_sum + 2.0 * shift * mixed_sum + shift * shift * scaled_sum) / count
    return (scaled_diff + shift * scaled_trial) * lax.rsqrt(mean_square + 1e-06), shift


def step_whole(coupling_shares, trial, gap, aux_count):
    nv, occ, width = trial.shape
    share = occ // aux_count

    def body(shares_ref, trial_ref, gap_ref, next_ref, xt_ref, shift_ref, coupling_ref):
        for r in range(aux_count):
            for v in range(nv):
                rows = shares_ref[r * nv + v].astype(jnp.float32)
                coupling_ref[v * occ + r * share : v * occ + (r + 1) * share, :] = rows
        diff, scaled, sums = five_sums(
            trial_ref[...].reshape(nv * occ, width), gap_ref[...].reshape(nv * occ, width), coupling_ref[...]
        )
        fresh, shift = finish(diff, scaled, sums, nv * occ * width)
        fresh = fresh.reshape(nv, occ, width)
        next_ref[...] = fresh
        xt_ref[...] = fresh.astype(jnp.bfloat16)
        shift_ref[...] = jnp.broadcast_to(shift, shift_ref.shape)

    return pl.pallas_call(
        body,
        out_shape=(
            jax.ShapeDtypeStruct(trial.shape, jnp.float32),
            jax.ShapeDtypeStruct(trial.shape, jnp.bfloat16),
            jax.ShapeDtypeStruct((1, 128), jnp.float32),
        ),
        scratch_shapes=[pltpu.VMEM((nv * occ, width), jnp.float32)],
        compiler_params=pltpu.CompilerParams(vmem_limit_bytes=24 * 2**20),
    )(coupling_shares, trial, gap)


def share_sums(terms, trial, gap):
    count = terms.shape[0]

    def body(terms_ref, trial_ref, gap_ref, diff_ref, scaled_ref, sums_ref):
        coupling = jnp.sum(terms_ref[...].astype(jnp.float32), axis=0)
        diff, scaled, sums = five_sums(trial_ref[...], gap_ref[...], coupling)
        diff_ref[...] = diff
        scaled_ref[...] = scaled
        lane = lax.broadcasted_iota(jnp.int32, (1, 128), 1)
        row = jnp.zeros((1, 128), jnp.float32)
        for at, value in enumerate(sums):
            row = jnp.where(lane == at, value, row)
        sums_ref[...] = jnp.broadcast_to(row[None], sums_ref.shape)

    like = jax.ShapeDtypeStruct(trial.shape, jnp.float32)
    return pl.pallas_call(
        body,
        out_shape=(like, like, jax.ShapeDtypeStruct((count, 1, 128), jnp.float32)),
        compiler_params=pltpu.CompilerParams(vmem_limit_bytes=24 * 2**20),
    )(terms, trial, gap)


def step_share(diff, scaled, all_sums, total):
    def body(diff_ref, scaled_ref, sums_ref, next_ref, shift_ref):
        row = jnp.sum(sums_ref[...], axis=0)
        fresh, shift = finish(
            diff_ref[...], scaled_ref[...], [row[:, at : at + 1] for at in range(5)], total
        )
        next_ref[...] = fresh
        shift_ref[...] = jnp.broadcast_to(shift, shift_ref.shape)

    return pl.pallas_call(
        body,
        out_shape=(
            jax.ShapeDtypeStruct(diff.shape, jnp.float32),
            jax.ShapeDtypeStruct((1, 128), jnp.float32),
        ),
    )(diff, scaled, all_sums)


def spread(share, count):
    copies = jnp.broadcast_to(share[None], (count,) + share.shape)
    return lax.all_to_all(copies, EVERY, 0, 0, tiled=True)


def local(factors, trials, occ_energy, vir_energy):
    na, nv = lax.axis_size("aux"), lax.axis_size("vir")
    count = na * nv
    aux_at, vir_at = lax.axis_index("aux"), lax.axis_index("vir")
    p_count, width, occ = factors.shape
    own = p_count // nv
    share = occ // na
    total = occ * width * nv
    paired = nv & (nv - 1) == 0

    def partner(at, k):
        return at ^ k if paired else (at + k) % nv

    def source(at, k):
        return at ^ k if paired else (at - k) % nv

    block = next(n for n in (8, 4, 2, 1) if own % n == 0)
    cuts = [0, own]
    if own >= 8 * block:
        cuts = [0, 2 * block, own - block, own]
    bounds = list(zip(cuts, cuts[1:]))

    message = jnp.concatenate([trials[0].T, vir_energy[None]], axis=0)
    begin = spread(message, count)
    chunks = []
    for at, (low, high) in enumerate(bounds):
        parts = [factors]
        for k in range(1, nv):
            piece = lax.dynamic_slice_in_dim(
                factors, partner(vir_at, k) * own + low, high - low, 0
            )
            if at:
                piece, chunks[-1][k] = lax.optimization_barrier((piece, chunks[-1][k]))
            pairs = [(one, partner(one, k)) for one in range(nv)]
            parts.append(lax.ppermute(piece, "vir", pairs))
        chunks.append(parts)
    order = jnp.stack([source(vir_at, k) for k in range(nv)] + [vir_at * (own // block)])
    order = order.astype(jnp.int32)

    begin = begin.reshape(na, nv, share + 1, width)
    trial = begin[:, :, :share].transpose(1, 0, 2, 3).reshape(nv, occ, width)
    gap = begin[0, :, share:] - occ_energy[None, :, None]
    gap_own = vir_energy[None, :] - lax.dynamic_slice_in_dim(occ_energy, aux_at * share, share)[:, None]
    xt = trial.astype(jnp.bfloat16)

    shift_list = []
    for iteration in range(ITERS):
        if iteration == 0:
            carry = None
            for chunk, bound in zip(chunks[:-1], bounds[:-1]):
                carry = contract(order, xt, [chunk], [bound], block, carry)
            partial = contract(order, xt, chunks[-1:], bounds[-1:], block, carry, na)
        else:
            partial = contract(order, xt, chunks, bounds, block, None, na)
        terms = lax.all_to_all(partial.reshape(count, share, width), EVERY, 0, 0, tiled=True)
        if iteration < ITERS - 1:
            coupling = jnp.sum(terms.astype(jnp.float32), axis=0).astype(jnp.bfloat16)
            trial, xt, shift = step_whole(spread(coupling, count), trial, gap, na)
        else:
            trial_own = lax.dynamic_slice(
                trial, (vir_at, aux_at * share, 0), (1, share, width)
            ).reshape(share, width)
            diff, scaled, sums = share_sums(terms, trial_own, gap_own)
            sums = lax.all_to_all(sums, EVERY, 0, 0, tiled=True)
            fresh, shift = step_share(diff, scaled, sums, total)
        shift_list.append(shift[:, :1])
    return (fresh.T[None], jnp.concatenate(shift_list, axis=0))


def solution(mesh):
    placed = (P("aux", "vir", None), P(None, "vir", "aux"), P(), P("vir"))
    return jax.shard_map(
        local, mesh=mesh, in_specs=placed, out_specs=(P(None, "vir", "aux"), P()), check_vma=False
    )
```

```python
import functools

import jax
import jax.numpy as jnp
from jax import lax
from jax.experimental import pallas as pl
from jax.experimental.pallas import tpu as pltpu
from jax.sharding import PartitionSpec as P

ITERS = 2
EVERY = ("aux", "vir")


def diagonal(occ):
    rows = lax.broadcasted_iota(jnp.int32, (occ, occ), 0)
    return rows == lax.broadcasted_iota(jnp.int32, (occ, occ), 1)


def coulomb_and_exchange(pair, eye):
    density = jnp.sum(jnp.where(eye, pair, 0.0), keepdims=True)
    density = density.astype(jnp.bfloat16).astype(jnp.float32)
    pair = pair.astype(jnp.bfloat16).astype(jnp.float32)
    return (jnp.where(eye, 2.0 * density, 0.0) - pair).astype(jnp.bfloat16)


def side_by_side(blocks, count):
    return jnp.concatenate([blocks[q] for q in range(count)], axis=1)


def contract_body(nv, bounds, own, carried, slots, order_ref, xt_ref, *refs):
    carry_ref = refs[0] if carried else None
    f_refs, (out_ref, acc_ref, held, sems) = refs[carried:-4], refs[-4:]
    occ, width = xt_ref.shape[1:]
    near_start = order_ref[nv] * own

    def copies(step):
        low, high = bounds[step]
        slot = step % slots
        made = []
        for k in range(nv):
            ref = f_refs[step * nv + k]
            if k == 0:
                ref = ref.at[pl.ds(near_start + low, high - low)]
            into = held.at[slot, k, pl.ds(0, high - low)]
            made.append(pltpu.make_async_copy(ref, into, sems.at[slot, k]))
        return made

    for step in range(min(slots, len(bounds))):
        for copy in copies(step):
            copy.start()
    acc_ref[...] = carry_ref[...] if carried else jnp.zeros_like(acc_ref)
    xt = jnp.concatenate([xt_ref[k] for k in range(nv)], axis=1)
    eye = diagonal(occ)
    for step, (low, high) in enumerate(bounds):
        for copy in copies(step):
            copy.wait()
        block = high - low
        tall = jnp.concatenate(
            [side_by_side(held.at[step % slots, k], block) for k in range(nv)], axis=0
        )
        pairs = jnp.dot(xt, tall, preferred_element_type=jnp.float32)
        mix = jnp.concatenate(
            [coulomb_and_exchange(pairs[:, q * occ : (q + 1) * occ], eye) for q in range(block)],
            axis=0,
        )
        acc_ref[...] += jnp.dot(tall, mix, preferred_element_type=jnp.float32)
        if step + slots < len(bounds):
            for copy in copies(step + slots):
                copy.start()
    if len(out_ref.shape) == 2:
        out_ref[...] = acc_ref[...]
        return
    share = out_ref.shape[2]
    for k in range(nv):
        turned = acc_ref[k * width : (k + 1) * width, :].T
        for r in range(occ // share):
            out_ref[r, order_ref[k]] = turned[r * share : (r + 1) * share, :].astype(out_ref.dtype)


def contract(order, xt, chunks, bounds, own, carry=None, aux_count=None):
    nv, occ, width = xt.shape
    carried = carry is not None
    slots = 3
    largest = max(high - low for low, high in bounds)
    count = sum(high - low for low, high in bounds)
    if aux_count is None:
        out = jax.ShapeDtypeStruct((nv * width, occ), jnp.float32)
    else:
        out = jax.ShapeDtypeStruct((aux_count, nv, occ // aux_count, width), jnp.bfloat16)
    in_vmem, anywhere = pl.BlockSpec(memory_space=pltpu.VMEM), pl.BlockSpec(memory_space=pl.ANY)
    return pl.pallas_call(
        functools.partial(contract_body, nv, bounds, own, carried, slots),
        in_specs=[pl.BlockSpec(memory_space=pltpu.SMEM)]
        + [in_vmem] * (1 + carried)
        + [anywhere] * (nv * len(chunks)),
        out_specs=in_vmem,
        out_shape=out,
        scratch_shapes=[
            pltpu.VMEM((nv * width, occ), jnp.float32),
            pltpu.VMEM((slots, nv, largest, width, occ), jnp.bfloat16),
            pltpu.SemaphoreType.DMA((slots, nv)),
        ],
        compiler_params=pltpu.CompilerParams(vmem_limit_bytes=40 * 2**20),
        cost_estimate=pl.CostEstimate(flops=0, bytes_accessed=0, transcendentals=0),
    )(order, xt, *([carry] if carried else []), *[part for chunk in chunks for part in chunk])


def partial_pairs(factors, xt_own, own, kept, unit):
    p_count, width, occ = factors.shape
    nv, per = p_count // own, kept // unit

    def body(xt_ref, f_ref, out_ref):
        wide = side_by_side(f_ref, unit)
        pairs = jnp.dot(xt_ref[...], wide, preferred_element_type=jnp.float32)
        for q in range(unit):
            out_ref[q] = pairs[:, q * occ : (q + 1) * occ].astype(jnp.bfloat16)

    return pl.pallas_call(
        body,
        grid=(nv, per),
        in_specs=[
            pl.BlockSpec((occ, width), lambda b, t: (0, 0)),
            pl.BlockSpec((unit, width, occ), lambda b, t: (b * (own // unit) + (own - kept) // unit + t, 0, 0)),
        ],
        out_specs=pl.BlockSpec((unit, occ, occ), lambda b, t: (b * per + t, 0, 0)),
        out_shape=jax.ShapeDtypeStruct((nv * kept, occ, occ), jnp.bfloat16),
        cost_estimate=pl.CostEstimate(flops=0, bytes_accessed=0, transcendentals=0),
    )(xt_own, factors)


def contract_pairs(order, factors, mine, other, carry, own, kept, unit):
    p_count, width, occ = factors.shape
    nv, per = p_count // own, kept // unit
    half = nv * per // 2

    def body(order_ref, mine_ref, other_ref, f_ref, carry_ref, out_ref):
        step = pl.program_id(0)

        @pl.when(step == 0)
        def _():
            out_ref[...] = carry_ref[...]

        eye = diagonal(occ)
        is_mine = step < half
        mix = jnp.concatenate(
            [
                coulomb_and_exchange(
                    jnp.where(is_mine, mine_ref[q].astype(jnp.float32), other_ref[q].astype(jnp.float32)), eye
                )
                for q in range(unit)
            ],
            axis=0,
        )
        wide = side_by_side(f_ref, unit)
        out_ref[0:width, :] += jnp.dot(wide, mix, preferred_element_type=jnp.float32)

    def place(g, order):
        core = order[nv + 1]
        at = jnp.where(g < half, core * half + g, (1 - core) * half + g - half)
        return (lax.div(at, per) * (own // unit) + (own - kept) // unit + lax.rem(at, per), 0, 0)

    whole = pl.BlockSpec((nv * width, occ), lambda g, order: (0, 0))
    return pl.pallas_call(
        body,
        grid_spec=pltpu.PrefetchScalarGridSpec(
            num_scalar_prefetch=1,
            grid=(2 * half,),
            in_specs=[
                pl.BlockSpec((unit, occ, occ), lambda g, order: (jnp.minimum(g, half - 1), 0, 0)),
                pl.BlockSpec((unit, occ, occ), lambda g, order: (jnp.maximum(g - half, 0), 0, 0)),
                pl.BlockSpec((unit, width, occ), place),
                whole,
            ],
            out_specs=whole,
        ),
        out_shape=jax.ShapeDtypeStruct((nv * width, occ), jnp.float32),
        cost_estimate=pl.CostEstimate(flops=0, bytes_accessed=0, transcendentals=0),
    )(order, mine, other, factors, carry)


def five_sums(trial, gap, coupling):
    rounded = trial.astype(jnp.bfloat16).astype(jnp.float32)
    image = gap * rounded + coupling
    scaled_trial = trial / gap
    scaled_diff = trial - image / gap

    def total(values):
        return jnp.sum(values, keepdims=True)

    sums = (
        total(trial * image),
        total(trial * trial),
        total(scaled_diff * scaled_diff),
        total(scaled_diff * scaled_trial),
        total(scaled_trial * scaled_trial),
    )
    return scaled_diff, scaled_trial, sums


def finish(scaled_diff, scaled_trial, sums, count):
    cross_sum, self_sum, diff_sum, mixed_sum, scaled_sum = sums
    shift = cross_sum / self_sum
    mean_square = (diff_sum + 2.0 * shift * mixed_sum + shift * shift * scaled_sum) / count
    return (scaled_diff + shift * scaled_trial) * lax.rsqrt(mean_square + 1e-06), shift


def step_whole(order, coupling_shares, trial, gap, aux_count):
    nv, occ, width = trial.shape
    share = occ // aux_count

    def body(order_ref, shares_ref, trial_ref, gap_ref, next_ref, xt_ref, shift_ref, coupling_ref):
        for r in range(aux_count):
            for v in range(nv):
                rows = shares_ref[r * nv + order_ref[v]].astype(jnp.float32)
                coupling_ref[v * occ + r * share : v * occ + (r + 1) * share, :] = rows
        diff, scaled, sums = five_sums(
            trial_ref[...].reshape(nv * occ, width), gap_ref[...].reshape(nv * occ, width), coupling_ref[...]
        )
        fresh, shift = finish(diff, scaled, sums, nv * occ * width)
        fresh = fresh.reshape(nv, occ, width)
        next_ref[...] = fresh
        xt_ref[...] = fresh.astype(jnp.bfloat16)
        shift_ref[...] = jnp.broadcast_to(shift, shift_ref.shape)

    return pl.pallas_call(
        body,
        out_shape=(
            jax.ShapeDtypeStruct(trial.shape, jnp.float32),
            jax.ShapeDtypeStruct(trial.shape, jnp.bfloat16),
            jax.ShapeDtypeStruct((1, 128), jnp.float32),
        ),
        in_specs=[pl.BlockSpec(memory_space=pltpu.SMEM)] + [pl.BlockSpec(memory_space=pltpu.VMEM)] * 3,
        scratch_shapes=[pltpu.VMEM((nv * occ, width), jnp.float32)],
        compiler_params=pltpu.CompilerParams(vmem_limit_bytes=24 * 2**20),
    )(order, coupling_shares, trial, gap)


def share_sums(terms, trial, gap):
    count = terms.shape[0]

    def body(terms_ref, trial_ref, gap_ref, diff_ref, scaled_ref, sums_ref):
        coupling = jnp.sum(terms_ref[...].astype(jnp.float32), axis=0)
        diff, scaled, sums = five_sums(trial_ref[...], gap_ref[...], coupling)
        diff_ref[...] = diff
        scaled_ref[...] = scaled
        lane = lax.broadcasted_iota(jnp.int32, (1, 128), 1)
        row = jnp.zeros((1, 128), jnp.float32)
        for at, value in enumerate(sums):
            row = jnp.where(lane == at, value, row)
        sums_ref[...] = jnp.broadcast_to(row[None], sums_ref.shape)

    like = jax.ShapeDtypeStruct(trial.shape, jnp.float32)
    return pl.pallas_call(
        body,
        out_shape=(like, like, jax.ShapeDtypeStruct((count, 1, 128), jnp.float32)),
        compiler_params=pltpu.CompilerParams(vmem_limit_bytes=24 * 2**20),
    )(terms, trial, gap)


def step_share(diff, scaled, all_sums, total):
    def body(diff_ref, scaled_ref, sums_ref, next_ref, shift_ref):
        row = jnp.sum(sums_ref[...], axis=0)
        fresh, shift = finish(
            diff_ref[...], scaled_ref[...], [row[:, at : at + 1] for at in range(5)], total
        )
        next_ref[...] = fresh
        shift_ref[...] = jnp.broadcast_to(shift, shift_ref.shape)

    return pl.pallas_call(
        body,
        out_shape=(
            jax.ShapeDtypeStruct(diff.shape, jnp.float32),
            jax.ShapeDtypeStruct((1, 128), jnp.float32),
        ),
    )(diff, scaled, all_sums)


def spread(share, count, axes=EVERY):
    copies = jnp.broadcast_to(share[None], (count,) + share.shape)
    return lax.all_to_all(copies, axes, 0, 0, tiled=True)


def local(factors, trials, occ_energy, vir_energy):
    na, nv = lax.axis_size("aux"), lax.axis_size("vir")
    count = na * nv
    aux_at, vir_at = lax.axis_index("aux"), lax.axis_index("vir")
    p_count, width, occ = factors.shape
    own = p_count // nv
    share = occ // na
    total = occ * width * nv
    paired = nv & (nv - 1) == 0

    def partner(at, k):
        return at ^ k if paired else (at + k) % nv

    def source(at, k):
        return at ^ k if paired else (at - k) % nv

    def send(value, k):
        return lax.ppermute(value, "vir", [(one, partner(one, k)) for one in range(nv)])

    order = [source(vir_at, k) for k in range(nv)] + [vir_at, vir_at & 1]
    order = jnp.stack(order).astype(jnp.int32)

    early, late = [(0, own)], []
    unit = own // 16
    if paired and nv >= 4 and own % 16 == 0 and unit >= 4:
        cuts = [0, 2 * unit, 6 * unit, 10 * unit, 12 * unit, 13 * unit, 14 * unit, own]
        bounds = list(zip(cuts, cuts[1:]))
        early, late = bounds[:-2], bounds[-2:]
    kept = own - early[-1][1]

    def pieces_of(bound, after):
        low, high = bound
        pieces = []
        for k in range(1, nv):
            place = partner(vir_at, k) * own + low
            pieces.append(lax.dynamic_slice_in_dim(after, place, high - low, 0))
        return pieces

    def send_pieces(pieces):
        return [factors] + [send(piece, k) for k, piece in enumerate(pieces, 1)]

    chunks = [send_pieces(pieces_of(early[0], factors))]
    later_factors = factors
    if kept:
        later_factors, trials, chunks[0][1] = lax.optimization_barrier(
            (factors, trials, chunks[0][1])
        )

    gathered = spread(trials[0].T, na, "aux").reshape(occ, width)
    gathered = jnp.concatenate([gathered, vir_energy[None]], axis=0)
    if paired:
        state = {0: gathered}
        bit = nv // 2
        while bit:
            names = sorted(state)
            if kept and bit in (1, 2):
                at = 4 - bit if bit == 1 else bit
                state[0], chunks[0][at] = lax.optimization_barrier((state[0], chunks[0][at]))
            came = send(jnp.stack([state[k] for k in names]), bit)
            state.update({k ^ bit: came[at] for at, k in enumerate(names)})
            bit //= 2
    else:
        state = {k: send(gathered, k) if k else gathered for k in range(nv)}
    state = jnp.stack([state[k] for k in range(nv)])
    trial = state[:, :occ]
    gap = state[:, occ:] - occ_energy[None, :, None]
    gap_own = vir_energy[None, :] - lax.dynamic_slice_in_dim(occ_energy, aux_at * share, share)[:, None]
    xt = trial.astype(jnp.bfloat16)

    carry, carried = None, 0
    for at in range(1, len(early)):
        pieces = pieces_of(early[at], later_factors)
        if at == len(early) - 1:
            while carried < at - 1:
                carry = contract(order, xt, [chunks[carried]], [early[carried]], own, carry)
                carried += 1
            pieces, carry = lax.optimization_barrier((pieces, carry))
        pieces, chunks[-1][2] = lax.optimization_barrier((pieces, chunks[-1][2]))
        chunks.append(send_pieces(pieces))

    if kept:
        half = nv * kept // 2
        core = vir_at & 1
        sums = partial_pairs(factors, xt[0], own, kept, unit)
        mine = lax.dynamic_slice_in_dim(sums, core * half, half, 0)
        other = lax.dynamic_slice_in_dim(sums, (1 - core) * half, half, 0)

        def add(one, two):
            return (one.astype(jnp.float32) + two.astype(jnp.float32)).astype(jnp.bfloat16)

        mine = add(mine, send(other, 1))
        bit = 2
        while bit < nv:
            mine = add(mine, send(mine, bit))
            bit *= 2
        other = send(mine, 1)

    shift_list = []
    for iteration in range(ITERS):
        last = iteration == ITERS - 1
        if iteration == 0:
            while carried < len(early) - 1:
                carry = contract(order, xt, [chunks[carried]], [early[carried]], own, carry)
                carried += 1
            if kept:
                carry = contract_pairs(order, factors, mine, other, carry, own, kept, unit)
            partial = contract(order, xt, chunks[-1:], early[-1:], own, carry, na)
        else:
            bounds = early + late
            if late:
                carry = contract(order, xt, chunks[:-1], bounds[:-1], own)
                partial = contract(order, xt, chunks[-1:], bounds[-1:], own, carry, na)
            else:
                partial = contract(order, xt, chunks, bounds, own, None, na)
        if iteration == 0 and late:
            pieces, partial = lax.optimization_barrier((pieces_of(late[0], later_factors), partial))
            parts = send_pieces(pieces)
        terms = lax.all_to_all(partial.reshape(count, share, width), EVERY, 0, 0, tiled=True)
        if not last:
            coupling = jnp.sum(terms.astype(jnp.float32), axis=0).astype(jnp.bfloat16)
            if iteration == 0 and late:
                parts[1:], coupling = lax.optimization_barrier((parts[1:], coupling))
                chunks.append(parts)
                pieces, coupling = lax.optimization_barrier(
                    (pieces_of(late[1], later_factors), coupling)
                )
                chunks.append(send_pieces(pieces))
            trial, xt, shift = step_whole(order, spread(coupling, count), trial, gap, na)
        else:
            trial_own = lax.dynamic_slice_in_dim(trial[0], aux_at * share, share, 0)
            diff, scaled, sums = share_sums(terms, trial_own, gap_own)
            sums = lax.all_to_all(sums, EVERY, 0, 0, tiled=True)
            fresh, shift = step_share(diff, scaled, sums, total)
        shift_list.append(shift[:, :1])
    return (fresh.T[None], jnp.concatenate(shift_list, axis=0))


def solution(mesh):
    placed = (P("aux", "vir", None), P(None, "vir", "aux"), P(), P("vir"))
    return jax.shard_map(
        local, mesh=mesh, in_specs=placed, out_specs=(P(None, "vir", "aux"), P()), check_vma=False
    )
```

```python
import functools

import jax
import jax.numpy as jnp
from jax import lax
from jax.experimental import pallas as pl
from jax.experimental.pallas import tpu as pltpu
from jax.sharding import PartitionSpec as P

ITERS = 2
EVERY = ("aux", "vir")


def diagonal(occ):
    rows = lax.broadcasted_iota(jnp.int32, (occ, occ), 0)
    return rows == lax.broadcasted_iota(jnp.int32, (occ, occ), 1)


def coulomb_and_exchange(pair, eye):
    density = jnp.sum(jnp.where(eye, pair, 0.0), keepdims=True)
    density = density.astype(jnp.bfloat16).astype(jnp.float32)
    pair = pair.astype(jnp.bfloat16).astype(jnp.float32)
    return (jnp.where(eye, 2.0 * density, 0.0) - pair).astype(jnp.bfloat16)


def side_by_side(blocks, count):
    return jnp.concatenate([blocks[q] for q in range(count)], axis=1)


def contract_body(nv, steps, own, carried, slots, order_ref, xt_ref, *refs):
    carry_ref = refs[0] if carried else None
    f_refs, (out_ref, acc_ref, held, sems) = refs[carried:-4], refs[-4:]
    occ, width = xt_ref.shape[1:]
    near_start = order_ref[nv] * own

    def copies(step):
        low, high, places = steps[step]
        slot = step % slots
        made = []
        for k, (at, offset) in enumerate(places):
            first = near_start + low if k == 0 else offset
            part = f_refs[at].at[pl.ds(first, high - low)]
            into = held.at[slot, k, pl.ds(0, high - low)]
            made.append(pltpu.make_async_copy(part, into, sems.at[slot, k]))
        return made

    for step in range(min(slots, len(steps))):
        for copy in copies(step):
            copy.start()
    acc_ref[...] = carry_ref[...] if carried else jnp.zeros_like(acc_ref)
    xt = jnp.concatenate([xt_ref[k] for k in range(nv)], axis=1)
    eye = diagonal(occ)
    for step, (low, high, places) in enumerate(steps):
        for copy in copies(step):
            copy.wait()
        block = high - low
        tall = jnp.concatenate(
            [side_by_side(held.at[step % slots, k], block) for k in range(nv)], axis=0
        )
        pairs = jnp.dot(xt, tall, preferred_element_type=jnp.float32)
        mix = jnp.concatenate(
            [coulomb_and_exchange(pairs[:, q * occ : (q + 1) * occ], eye) for q in range(block)],
            axis=0,
        )
        acc_ref[...] += jnp.dot(tall, mix, preferred_element_type=jnp.float32)
        if step + slots < len(steps):
            for copy in copies(step + slots):
                copy.start()
    if len(out_ref.shape) == 2:
        out_ref[...] = acc_ref[...]
        return
    share = out_ref.shape[2]
    for k in range(nv):
        turned = acc_ref[k * width : (k + 1) * width, :].T
        for r in range(occ // share):
            out_ref[r, order_ref[k]] = turned[r * share : (r + 1) * share, :].astype(out_ref.dtype)


def contract(order, xt, factors, sources, bounds, own, carry=None, aux_count=None):
    nv, occ, width = xt.shape
    carried = carry is not None
    slots = 3
    largest = max(high - low for low, high in bounds)
    count = sum(high - low for low, high in bounds)
    arrays, steps = [factors], []
    for low, high in bounds:
        places = [(0, 0)]
        for k in range(1, nv):
            start, array = next((a, x) for a, b, x in sources[k] if a <= low and high <= b)
            at = next((n for n, x in enumerate(arrays) if x is array), len(arrays))
            if at == len(arrays):
                arrays.append(array)
            places.append((at, low - start))
        steps.append((low, high, places))
    if aux_count is None:
        out = jax.ShapeDtypeStruct((nv * width, occ), jnp.float32)
    else:
        out = jax.ShapeDtypeStruct((aux_count, nv, occ // aux_count, width), jnp.bfloat16)
    in_vmem, anywhere = pl.BlockSpec(memory_space=pltpu.VMEM), pl.BlockSpec(memory_space=pl.ANY)
    return pl.pallas_call(
        functools.partial(contract_body, nv, steps, own, carried, slots),
        in_specs=[pl.BlockSpec(memory_space=pltpu.SMEM)]
        + [in_vmem] * (1 + carried)
        + [anywhere] * len(arrays),
        out_specs=in_vmem,
        out_shape=out,
        scratch_shapes=[
            pltpu.VMEM((nv * width, occ), jnp.float32),
            pltpu.VMEM((slots, nv, largest, width, occ), jnp.bfloat16),
            pltpu.SemaphoreType.DMA((slots, nv)),
        ],
        compiler_params=pltpu.CompilerParams(vmem_limit_bytes=40 * 2**20),
        cost_estimate=pl.CostEstimate(flops=0, bytes_accessed=0, transcendentals=0),
    )(order, xt, *([carry] if carried else []), *arrays)


def five_sums(trial, gap, coupling):
    rounded = trial.astype(jnp.bfloat16).astype(jnp.float32)
    image = gap * rounded + coupling
    scaled_trial = trial / gap
    scaled_diff = trial - image / gap

    def total(values):
        return jnp.sum(values, keepdims=True)

    sums = (
        total(trial * image),
        total(trial * trial),
        total(scaled_diff * scaled_diff),
        total(scaled_diff * scaled_trial),
        total(scaled_trial * scaled_trial),
    )
    return scaled_diff, scaled_trial, sums


def finish(scaled_diff, scaled_trial, sums, count):
    cross_sum, self_sum, diff_sum, mixed_sum, scaled_sum = sums
    shift = cross_sum / self_sum
    mean_square = (diff_sum + 2.0 * shift * mixed_sum + shift * shift * scaled_sum) / count
    return (scaled_diff + shift * scaled_trial) * lax.rsqrt(mean_square + 1e-06), shift


def step_whole(order, coupling_shares, trial, gap, aux_count):
    nv, occ, width = trial.shape
    share = occ // aux_count

    def body(order_ref, shares_ref, trial_ref, gap_ref, next_ref, xt_ref, shift_ref, coupling_ref):
        for r in range(aux_count):
            for v in range(nv):
                rows = shares_ref[r * nv + order_ref[v]].astype(jnp.float32)
                coupling_ref[v * occ + r * share : v * occ + (r + 1) * share, :] = rows
        diff, scaled, sums = five_sums(
            trial_ref[...].reshape(nv * occ, width), gap_ref[...].reshape(nv * occ, width), coupling_ref[...]
        )
        fresh, shift = finish(diff, scaled, sums, nv * occ * width)
        fresh = fresh.reshape(nv, occ, width)
        next_ref[...] = fresh
        xt_ref[...] = fresh.astype(jnp.bfloat16)
        shift_ref[...] = jnp.broadcast_to(shift, shift_ref.shape)

    return pl.pallas_call(
        body,
        out_shape=(
            jax.ShapeDtypeStruct(trial.shape, jnp.float32),
            jax.ShapeDtypeStruct(trial.shape, jnp.bfloat16),
            jax.ShapeDtypeStruct((1, 128), jnp.float32),
        ),
        in_specs=[pl.BlockSpec(memory_space=pltpu.SMEM)] + [pl.BlockSpec(memory_space=pltpu.VMEM)] * 3,
        scratch_shapes=[pltpu.VMEM((nv * occ, width), jnp.float32)],
        compiler_params=pltpu.CompilerParams(vmem_limit_bytes=24 * 2**20),
    )(order, coupling_shares, trial, gap)


def share_sums(terms, trial, gap):
    count = terms.shape[0]

    def body(terms_ref, trial_ref, gap_ref, diff_ref, scaled_ref, sums_ref):
        coupling = jnp.sum(terms_ref[...].astype(jnp.float32), axis=0)
        diff, scaled, sums = five_sums(trial_ref[...], gap_ref[...], coupling)
        diff_ref[...] = diff
        scaled_ref[...] = scaled
        lane = lax.broadcasted_iota(jnp.int32, (1, 128), 1)
        row = jnp.zeros((1, 128), jnp.float32)
        for at, value in enumerate(sums):
            row = jnp.where(lane == at, value, row)
        sums_ref[...] = jnp.broadcast_to(row[None], sums_ref.shape)

    like = jax.ShapeDtypeStruct(trial.shape, jnp.float32)
    return pl.pallas_call(
        body,
        out_shape=(like, like, jax.ShapeDtypeStruct((count, 1, 128), jnp.float32)),
        compiler_params=pltpu.CompilerParams(vmem_limit_bytes=24 * 2**20),
    )(terms, trial, gap)


def step_share(diff, scaled, all_sums, total):
    def body(diff_ref, scaled_ref, sums_ref, next_ref, shift_ref):
        row = jnp.sum(sums_ref[...], axis=0)
        fresh, shift = finish(
            diff_ref[...], scaled_ref[...], [row[:, at : at + 1] for at in range(5)], total
        )
        next_ref[...] = fresh
        shift_ref[...] = jnp.broadcast_to(shift, shift_ref.shape)

    return pl.pallas_call(
        body,
        out_shape=(
            jax.ShapeDtypeStruct(diff.shape, jnp.float32),
            jax.ShapeDtypeStruct((1, 128), jnp.float32),
        ),
    )(diff, scaled, all_sums)


def spread(share, count, axes=EVERY):
    copies = jnp.broadcast_to(share[None], (count,) + share.shape)
    return lax.all_to_all(copies, axes, 0, 0, tiled=True)


def local(factors, trials, occ_energy, vir_energy):
    na, nv = lax.axis_size("aux"), lax.axis_size("vir")
    count = na * nv
    aux_at, vir_at = lax.axis_index("aux"), lax.axis_index("vir")
    p_count, width, occ = factors.shape
    own = p_count // nv
    share = occ // na
    total = occ * width * nv
    paired = nv & (nv - 1) == 0

    def partner(at, k):
        return at ^ k if paired else (at + k) % nv

    def source(at, k):
        return at ^ k if paired else (at - k) % nv

    def send(value, k):
        return lax.ppermute(value, "vir", [(one, partner(one, k)) for one in range(nv)])

    order = [source(vir_at, k) for k in range(nv)] + [vir_at]
    order = jnp.stack(order).astype(jnp.int32)

    unit = own // 16
    cut_up = unit >= 4 and own % 16 == 0
    sources = {k: [] for k in range(1, nv)}

    def piece(k, low, high, whole=factors):
        return lax.dynamic_slice_in_dim(whole, partner(vir_at, k) * own + low, high - low, 0)

    def exchange(k, low, high, part):
        sources[k].append((low, high, send(part, k)))

    def after_newest(k, *values):
        low, high, array = sources[k][-1]
        *values, array = lax.optimization_barrier((*values, array))
        sources[k][-1] = (low, high, array)
        return values

    marks = [0, own]
    if cut_up:
        marks = [0, 3 * unit, 15 * unit, own]
    for k in range(1, nv):
        exchange(k, 0, marks[1], piece(k, 0, marks[1]))
    later_factors = factors
    if cut_up:
        later_factors, trials = after_newest(1, factors, trials)

    gathered = spread(trials[0].T, na, "aux").reshape(occ, width)
    gathered = jnp.concatenate([gathered, vir_energy[None]], axis=0)
    if paired:
        state = {0: gathered}
        bit = nv // 2
        while bit:
            names = sorted(state)
            if cut_up and bit <= 2:
                state[0], = after_newest(4 - bit if bit == 1 else bit, state[0])
            came = send(jnp.stack([state[k] for k in names]), bit)
            if cut_up and bit == 2:
                large = [piece(k, *marks[1:3], later_factors) for k in range(1, nv)]
                large, came = lax.optimization_barrier((large, came))
            state.update({k ^ bit: came[at] for at, k in enumerate(names)})
            bit //= 2
    else:
        state = {k: send(gathered, k) if k else gathered for k in range(nv)}
    state = jnp.stack([state[k] for k in range(nv)])
    trial = state[:, :occ]
    gap_own = vir_energy[None, :] - lax.dynamic_slice_in_dim(occ_energy, aux_at * share, share)[:, None]
    xt = trial.astype(jnp.bfloat16)

    for low, high in zip(marks[1:], marks[2:]):
        for k in range(nv - 1, 0, -1):
            if low == marks[1]:
                exchange(k, low, high, large[k - 1])
            else:
                cut = piece(k, low, high, later_factors)
                exchange(k, low, high, *after_newest(min(k, 2), cut))

    early, ending = [], [(0, own)]
    if cut_up:
        steps = [0, 3 * unit, 7 * unit, 11 * unit, 15 * unit]
        early, ending = list(zip(steps, steps[1:])), [(15 * unit, own)]

    shift_list = []
    for iteration in range(ITERS):
        last = iteration == ITERS - 1
        call = functools.partial(contract, order, xt, factors, sources)
        if early and iteration == 0:
            partial = call(ending, own, call(early, own), na)
        else:
            partial = call(early + ending, own, None, na)
        if not last:
            energy, partial = lax.optimization_barrier((occ_energy, partial))
            gap = state[:, occ:] - energy[None, :, None]
        terms = lax.all_to_all(partial.reshape(count, share, width), EVERY, 0, 0, tiled=True)
        if not last:
            coupling = jnp.sum(terms.astype(jnp.float32), axis=0).astype(jnp.bfloat16)
            coupling, gap = lax.optimization_barrier((coupling, gap))
            trial, xt, shift = step_whole(order, spread(coupling, count), trial, gap, na)
        else:
            trial_own = lax.dynamic_slice_in_dim(trial[0], aux_at * share, share, 0)
            diff, scaled, sums = share_sums(terms, trial_own, gap_own)
            sums = lax.all_to_all(sums, EVERY, 0, 0, tiled=True)
            fresh, shift = step_share(diff, scaled, sums, total)
        shift_list.append(shift[:, :1])
    return (fresh.T[None], jnp.concatenate(shift_list, axis=0))


def solution(mesh):
    placed = (P("aux", "vir", None), P(None, "vir", "aux"), P(), P("vir"))
    return jax.shard_map(
        local, mesh=mesh, in_specs=placed, out_specs=(P(None, "vir", "aux"), P()), check_vma=False
    )
```

```python
import functools

import jax
import jax.numpy as jnp
from jax import lax
from jax.experimental import pallas as pl
from jax.experimental.pallas import tpu as pltpu
from jax.sharding import PartitionSpec as P

ITERS = 2
EVERY = ("aux", "vir")


def diagonal(occ):
    rows = lax.broadcasted_iota(jnp.int32, (occ, occ), 0)
    return rows == lax.broadcasted_iota(jnp.int32, (occ, occ), 1)


def coulomb_and_exchange(pair, eye):
    density = jnp.sum(jnp.where(eye, pair, 0.0), keepdims=True)
    density = density.astype(jnp.bfloat16).astype(jnp.float32)
    pair = pair.astype(jnp.bfloat16).astype(jnp.float32)
    return (jnp.where(eye, 2.0 * density, 0.0) - pair).astype(jnp.bfloat16)


def side_by_side(blocks, count):
    return jnp.concatenate([blocks[q] for q in range(count)], axis=1)


def contract_body(nv, steps, own, carried, slots, order_ref, xt_ref, *refs):
    carry_ref = refs[0] if carried else None
    f_refs, (out_ref, acc_ref, held, sems) = refs[carried:-4], refs[-4:]
    occ, width = xt_ref.shape[1:]
    near_start = order_ref[nv] * own

    def copies(step):
        low, high, places = steps[step]
        slot = step % slots
        made = []
        for k, (at, offset) in enumerate(places):
            first = near_start + low if k == 0 else offset
            part = f_refs[at].at[pl.ds(first, high - low)]
            into = held.at[slot, k, pl.ds(0, high - low)]
            made.append(pltpu.make_async_copy(part, into, sems.at[slot, k]))
        return made

    for step in range(min(slots, len(steps))):
        for copy in copies(step):
            copy.start()
    acc_ref[...] = carry_ref[...] if carried else jnp.zeros_like(acc_ref)
    xt = jnp.concatenate([xt_ref[k] for k in range(nv)], axis=1)
    eye = diagonal(occ)
    for step, (low, high, places) in enumerate(steps):
        for copy in copies(step):
            copy.wait()
        block = high - low
        tall = jnp.concatenate(
            [side_by_side(held.at[step % slots, k], block) for k in range(nv)], axis=0
        )
        pairs = jnp.dot(xt, tall, preferred_element_type=jnp.float32)
        mix = jnp.concatenate(
            [coulomb_and_exchange(pairs[:, q * occ : (q + 1) * occ], eye) for q in range(block)],
            axis=0,
        )
        acc_ref[...] += jnp.dot(tall, mix, preferred_element_type=jnp.float32)
        if step + slots < len(steps):
            for copy in copies(step + slots):
                copy.start()
    if len(out_ref.shape) == 2:
        out_ref[...] = acc_ref[...]
        return
    share = out_ref.shape[2]
    for k in range(nv):
        turned = acc_ref[k * width : (k + 1) * width, :].T
        for r in range(occ // share):
            out_ref[r, order_ref[k]] = turned[r * share : (r + 1) * share, :].astype(out_ref.dtype)


def contract(order, xt, factors, sources, bounds, own, carry=None, aux_count=None):
    nv, occ, width = xt.shape
    carried = carry is not None
    slots = 3
    largest = max(high - low for low, high in bounds)
    count = sum(high - low for low, high in bounds)
    arrays, steps = [factors], []
    for low, high in bounds:
        places = [(0, 0)]
        for k in range(1, nv):
            start, array = next((a, x) for a, b, x in sources[k] if a <= low and high <= b)
            at = next((n for n, x in enumerate(arrays) if x is array), len(arrays))
            if at == len(arrays):
                arrays.append(array)
            places.append((at, low - start))
        steps.append((low, high, places))
    if aux_count is None:
        out = jax.ShapeDtypeStruct((nv * width, occ), jnp.float32)
    else:
        out = jax.ShapeDtypeStruct((aux_count, nv, occ // aux_count, width), jnp.bfloat16)
    in_vmem, in_hbm = pl.BlockSpec(memory_space=pltpu.VMEM), pl.BlockSpec(memory_space=pltpu.HBM)
    return pl.pallas_call(
        functools.partial(contract_body, nv, steps, own, carried, slots),
        in_specs=[pl.BlockSpec(memory_space=pltpu.SMEM)]
        + [in_vmem] * (1 + carried)
        + [in_hbm] * len(arrays),
        out_specs=in_vmem,
        out_shape=out,
        scratch_shapes=[
            pltpu.VMEM((nv * width, occ), jnp.float32),
            pltpu.VMEM((slots, nv, largest, width, occ), jnp.bfloat16),
            pltpu.SemaphoreType.DMA((slots, nv)),
        ],
        compiler_params=pltpu.CompilerParams(vmem_limit_bytes=40 * 2**20),
        cost_estimate=pl.CostEstimate(flops=0, bytes_accessed=0, transcendentals=0),
    )(order, xt, *([carry] if carried else []), *arrays)


def five_sums(trial, gap, coupling):
    rounded = trial.astype(jnp.bfloat16).astype(jnp.float32)
    image = gap * rounded + coupling
    scaled_trial = trial / gap
    scaled_diff = trial - image / gap

    def total(values):
        return jnp.sum(values, keepdims=True)

    sums = (
        total(trial * image),
        total(trial * trial),
        total(scaled_diff * scaled_diff),
        total(scaled_diff * scaled_trial),
        total(scaled_trial * scaled_trial),
    )
    return scaled_diff, scaled_trial, sums


def finish(scaled_diff, scaled_trial, sums, count):
    cross_sum, self_sum, diff_sum, mixed_sum, scaled_sum = sums
    shift = cross_sum / self_sum
    mean_square = (diff_sum + 2.0 * shift * mixed_sum + shift * shift * scaled_sum) / count
    return (scaled_diff + shift * scaled_trial) * lax.rsqrt(mean_square + 1e-06), shift


def step_whole(order, coupling_shares, trial, gap, aux_count):
    nv, occ, width = trial.shape
    share = occ // aux_count

    def body(order_ref, shares_ref, trial_ref, gap_ref, next_ref, xt_ref, shift_ref, coupling_ref):
        for r in range(aux_count):
            for v in range(nv):
                rows = shares_ref[r * nv + order_ref[v]].astype(jnp.float32)
                coupling_ref[v * occ + r * share : v * occ + (r + 1) * share, :] = rows
        diff, scaled, sums = five_sums(
            trial_ref[...].reshape(nv * occ, width), gap_ref[...].reshape(nv * occ, width), coupling_ref[...]
        )
        fresh, shift = finish(diff, scaled, sums, nv * occ * width)
        fresh = fresh.reshape(nv, occ, width)
        next_ref[...] = fresh
        xt_ref[...] = fresh.astype(jnp.bfloat16)
        shift_ref[...] = jnp.broadcast_to(shift, shift_ref.shape)

    return pl.pallas_call(
        body,
        out_shape=(
            jax.ShapeDtypeStruct(trial.shape, jnp.float32),
            jax.ShapeDtypeStruct(trial.shape, jnp.bfloat16),
            jax.ShapeDtypeStruct((1, 128), jnp.float32),
        ),
        in_specs=[pl.BlockSpec(memory_space=pltpu.SMEM)] + [pl.BlockSpec(memory_space=pltpu.VMEM)] * 3,
        scratch_shapes=[pltpu.VMEM((nv * occ, width), jnp.float32)],
        compiler_params=pltpu.CompilerParams(vmem_limit_bytes=24 * 2**20),
    )(order, coupling_shares, trial, gap)


def share_sums(terms, trial, gap):
    count = terms.shape[0]

    def body(terms_ref, trial_ref, gap_ref, diff_ref, scaled_ref, sums_ref):
        coupling = jnp.sum(terms_ref[...].astype(jnp.float32), axis=0)
        diff, scaled, sums = five_sums(trial_ref[...], gap_ref[...], coupling)
        diff_ref[...] = diff
        scaled_ref[...] = scaled
        lane = lax.broadcasted_iota(jnp.int32, (1, 128), 1)
        row = jnp.zeros((1, 128), jnp.float32)
        for at, value in enumerate(sums):
            row = jnp.where(lane == at, value, row)
        sums_ref[...] = jnp.broadcast_to(row[None], sums_ref.shape)

    like = jax.ShapeDtypeStruct(trial.shape, jnp.float32)
    return pl.pallas_call(
        body,
        out_shape=(like, like, jax.ShapeDtypeStruct((count, 1, 128), jnp.float32)),
        compiler_params=pltpu.CompilerParams(vmem_limit_bytes=24 * 2**20),
    )(terms, trial, gap)


def step_share(diff, scaled, all_sums, total):
    def body(diff_ref, scaled_ref, sums_ref, next_ref, shift_ref):
        row = jnp.sum(sums_ref[...], axis=0)
        fresh, shift = finish(
            diff_ref[...], scaled_ref[...], [row[:, at : at + 1] for at in range(5)], total
        )
        next_ref[...] = fresh
        shift_ref[...] = jnp.broadcast_to(shift, shift_ref.shape)

    return pl.pallas_call(
        body,
        out_shape=(
            jax.ShapeDtypeStruct(diff.shape, jnp.float32),
            jax.ShapeDtypeStruct((1, 128), jnp.float32),
        ),
    )(diff, scaled, all_sums)


def spread(share, count, axes=EVERY):
    copies = jnp.broadcast_to(share[None], (count,) + share.shape)
    return lax.all_to_all(copies, axes, 0, 0, tiled=True)


def local(factors, trials, occ_energy, vir_energy):
    na, nv = lax.axis_size("aux"), lax.axis_size("vir")
    count = na * nv
    aux_at, vir_at = lax.axis_index("aux"), lax.axis_index("vir")
    p_count, width, occ = factors.shape
    own = p_count // nv
    share = occ // na
    total = occ * width * nv
    paired = nv & (nv - 1) == 0

    def partner(at, k):
        return at ^ k if paired else (at + k) % nv

    def source(at, k):
        return at ^ k if paired else (at - k) % nv

    def send(value, k):
        return lax.ppermute(value, "vir", [(one, partner(one, k)) for one in range(nv)])

    order = [source(vir_at, k) for k in range(nv)] + [vir_at]
    order = jnp.stack(order).astype(jnp.int32)

    unit = own // 16
    cut_up = unit >= 4 and own % 16 == 0
    sources = {k: [] for k in range(1, nv)}

    def piece(k, low, high, whole=factors):
        return lax.dynamic_slice_in_dim(whole, partner(vir_at, k) * own + low, high - low, 0)

    def exchange(k, low, high, part):
        sources[k].append((low, high, send(part, k)))

    def after_newest(k, *values):
        low, high, array = sources[k][-1]
        *values, array = lax.optimization_barrier((*values, array))
        sources[k][-1] = (low, high, array)
        return values

    marks = [0, own]
    if cut_up:
        marks = [0, 12 * unit, 15 * unit, own]
    far = [k for k in range(nv) if k > 1] + [1]
    later_factors = factors
    for n, k in enumerate(far):
        cut = piece(k, *marks[:2], later_factors)
        if cut_up and n == 0:
            later_factors, cut = lax.optimization_barrier((factors, cut))
        exchange(k, *marks[:2], cut)
    if cut_up:
        later = [[piece(k, low, high, later_factors) for k in far] for low, high in zip(marks[1:], marks[2:])]
        later, trials = lax.optimization_barrier((later, *after_newest(2, trials)))

    gathered = spread(trials[0].T, na, "aux").reshape(occ, width)
    gathered = jnp.concatenate([gathered, vir_energy[None]], axis=0)
    if paired:
        state = {0: gathered}
        bit = nv // 2
        while bit:
            names = sorted(state)
            came = send(jnp.stack([state[k] for k in names]), bit)
            state.update({k ^ bit: came[at] for at, k in enumerate(names)})
            bit //= 2
    else:
        state = {k: send(gathered, k) if k else gathered for k in range(nv)}
    state = jnp.stack([state[k] for k in range(nv)])
    trial = state[:, :occ]
    gap_own = vir_energy[None, :] - lax.dynamic_slice_in_dim(occ_energy, aux_at * share, share)[:, None]
    xt = trial.astype(jnp.bfloat16)

    call = functools.partial(contract, order, xt, factors, sources)
    groups = [[(0, own)]]
    if cut_up:
        low, high, end = marks[1:]
        for k, cut in enumerate(later[0]):
            exchange(far[k], low, high, cut)
        groups = [[(n * 4 * unit, (n + 1) * 4 * unit) for n in range(3)], [(low, high)], [(high, end)]]
        carry = call(groups[0], own)
        cuts, carry = lax.optimization_barrier((later[1], carry))
        for k, cut in zip(far, cuts):
            exchange(k, high, end, cut)
        carry = call(groups[1], own, carry)

    shift_list = []
    for iteration in range(ITERS):
        last = iteration == ITERS - 1
        call = functools.partial(contract, order, xt, factors, sources)
        if cut_up and iteration == 0:
            partial = call(groups[-1], own, carry, na)
        else:
            partial = call(sum(groups, []), own, None, na)
        if not last:
            energy, partial = lax.optimization_barrier((occ_energy, partial))
            gap = state[:, occ:] - energy[None, :, None]
        terms = lax.all_to_all(partial.reshape(count, share, width), EVERY, 0, 0, tiled=True)
        if not last:
            coupling = jnp.sum(terms.astype(jnp.float32), axis=0).astype(jnp.bfloat16)
            coupling, gap = lax.optimization_barrier((coupling, gap))
            trial, xt, shift = step_whole(order, spread(coupling, count), trial, gap, na)
        else:
            trial_own = lax.dynamic_slice_in_dim(trial[0], aux_at * share, share, 0)
            diff, scaled, sums = share_sums(terms, trial_own, gap_own)
            sums = lax.all_to_all(sums, EVERY, 0, 0, tiled=True)
            fresh, shift = step_share(diff, scaled, sums, total)
        shift_list.append(shift[:, :1])
    return (fresh.T[None], jnp.concatenate(shift_list, axis=0))


def solution(mesh):
    placed = (P("aux", "vir", None), P(None, "vir", "aux"), P(), P("vir"))
    return jax.shard_map(
        local, mesh=mesh, in_specs=placed, out_specs=(P(None, "vir", "aux"), P()), check_vma=False
    )
```

```python
import functools

import jax
import jax.numpy as jnp
from jax import lax
from jax.experimental import pallas as pl
from jax.experimental.pallas import tpu as pltpu
from jax.sharding import PartitionSpec as P

EVERY = ("aux", "vir")


def diagonal(occ):
    rows = lax.broadcasted_iota(jnp.int32, (occ, occ), 0)
    return rows == lax.broadcasted_iota(jnp.int32, (occ, occ), 1)


def coulomb_and_exchange(pair, eye):
    density = jnp.sum(jnp.where(eye, pair, 0.0), keepdims=True)
    density = density.astype(jnp.bfloat16).astype(jnp.float32)
    pair = pair.astype(jnp.bfloat16).astype(jnp.float32)
    return (jnp.where(eye, 2.0 * density, 0.0) - pair).astype(jnp.bfloat16)


def side_by_side(blocks, count):
    return jnp.concatenate([blocks[q] for q in range(count)], axis=1)


def five_sums(trial, gap, coupling):
    rounded = trial.astype(jnp.bfloat16).astype(jnp.float32)
    image = gap * rounded + coupling
    scaled_trial = trial / gap
    scaled_diff = trial - image / gap

    def total(values):
        return jnp.sum(values, keepdims=True)

    sums = (
        total(trial * image),
        total(trial * trial),
        total(scaled_diff * scaled_diff),
        total(scaled_diff * scaled_trial),
        total(scaled_trial * scaled_trial),
    )
    return scaled_diff, scaled_trial, sums


def finish(scaled_diff, scaled_trial, sums, count):
    cross_sum, self_sum, diff_sum, mixed_sum, scaled_sum = sums
    shift = cross_sum / self_sum
    mean_square = (diff_sum + 2.0 * shift * mixed_sum + shift * shift * scaled_sum) / count
    return (scaled_diff + shift * scaled_trial) * lax.rsqrt(mean_square + 1e-06), shift


def contract_body(nv, blocks, size, own, carried, stepping, total, order_ref, *refs):
    first_refs, refs = refs[: 4 if stepping else 1], refs[4 if stepping else 1 :]
    carry_ref, f_refs = (refs[0], refs[1:]) if carried else (None, refs)
    f_count = 1 + max(at for block in blocks for _, _, places in block for at, _ in places)
    f_refs, refs = f_refs[:f_count], f_refs[f_count:]
    out_refs, (acc_ref, xt_ref, held, sems) = refs[:-4], refs[-4:]
    out_ref = out_refs[0]
    width, occ = held.shape[3:]
    near_start = order_ref[nv] * own

    for at, block in enumerate(blocks):
        for k in range(nv):
            into_at = 0
            for low, high, places in block:
                array, offset = places[k]
                start = near_start + low if k == 0 else offset
                count = high - low
                pltpu.make_async_copy(
                    f_refs[array].at[pl.ds(start, count)],
                    held.at[at, k, pl.ds(into_at, count)],
                    sems.at[at, k],
                ).start()
                into_at += count

    acc_ref[...] = carry_ref[...] if carried else jnp.zeros_like(acc_ref)
    if stepping:
        shares_ref, trial_ref, vir_ref, occ_ref = first_refs
        own_ref, shift_ref = out_refs[1:]
        share = own_ref.shape[0]
        coupling = jnp.concatenate(
            [
                shares_ref[r * nv + order_ref[k]].astype(jnp.float32)
                for k in range(nv)
                for r in range(occ // share)
            ],
            axis=0,
        )
        gap = jnp.concatenate([vir_ref[k] - occ_ref[...] for k in range(nv)], axis=0)
        diff, scaled, sums = five_sums(trial_ref[...].reshape(nv * occ, width), gap, coupling)
        fresh, shift = finish(diff, scaled, sums, total)
        shift_ref[...] = jnp.broadcast_to(shift, shift_ref.shape)
        for k in range(nv):
            rows = fresh[k * occ : (k + 1) * occ]
            xt_ref[:, k * width : (k + 1) * width] = rows.astype(jnp.bfloat16)
        mine = fresh[:share]
        for r in range(1, occ // share):
            rows = fresh[r * share : (r + 1) * share]
            mine = jnp.where(order_ref[nv + 1] == r, rows, mine)
        own_ref[...] = mine
    else:
        for k in range(nv):
            xt_ref[:, k * width : (k + 1) * width] = first_refs[0][k]
    eye = lax.broadcasted_iota(jnp.int32, (occ, occ), 0) == lax.broadcasted_iota(
        jnp.int32, (occ, occ), 1
    )

    def work(at, _):
        for k in range(nv):
            pltpu.make_async_copy(held.at[at, k], held.at[at, k], sems.at[at, k]).wait()
        tall = jnp.concatenate(
            [
                jnp.concatenate([held[at, k, q] for q in range(size)], axis=1)
                for k in range(nv)
            ],
            axis=0,
        )
        pairs = jnp.dot(xt_ref[...], tall, preferred_element_type=jnp.float32)
        mixes = []
        for q in range(size):
            pair = pairs[:, q * occ : (q + 1) * occ]
            density = jnp.sum(jnp.where(eye, pair, 0.0), keepdims=True)
            density = density.astype(jnp.bfloat16).astype(jnp.float32)
            pair = pair.astype(jnp.bfloat16).astype(jnp.float32)
            mixes.append((jnp.where(eye, 2.0 * density, 0.0) - pair).astype(jnp.bfloat16))
        mix = jnp.concatenate(mixes, axis=0)
        acc_ref[...] += jnp.dot(tall, mix, preferred_element_type=jnp.float32)
        return _

    lax.fori_loop(0, len(blocks), work, 0)
    if len(out_ref.shape) == 2:
        out_ref[...] = acc_ref[...]
        return
    share = out_ref.shape[2]
    for k in range(nv):
        turned = acc_ref[k * width : (k + 1) * width, :].T
        for r in range(occ // share):
            out_ref[r, order_ref[k]] = turned[r * share : (r + 1) * share, :].astype(out_ref.dtype)


def contract(order, first, factors, sources, blocks, own, carry=None, aux_count=None):
    p_count, width, occ = factors.shape
    nv = p_count // own
    carried, stepping = carry is not None, len(first) > 1
    size = sum(high - low for low, high in blocks[0])
    arrays, placed = [factors], []
    for block in blocks:
        placed.append([])
        for low, high in block:
            places = [(0, 0)]
            for k in range(1, nv):
                start, array = next((a, x) for a, b, x in sources[k] if a <= low and high <= b)
                at = next((n for n, x in enumerate(arrays) if x is array), len(arrays))
                if at == len(arrays):
                    arrays.append(array)
                places.append((at, low - start))
            placed[-1].append((low, high, places))
    if aux_count is None:
        out = [jax.ShapeDtypeStruct((nv * width, occ), jnp.float32)]
    else:
        out = [jax.ShapeDtypeStruct((aux_count, nv, occ // aux_count, width), jnp.bfloat16)]
    if stepping:
        out.append(jax.ShapeDtypeStruct((occ // aux_count, width), jnp.float32))
        out.append(jax.ShapeDtypeStruct((1, 128), jnp.float32))
    in_vmem, in_hbm = pl.BlockSpec(memory_space=pltpu.VMEM), pl.BlockSpec(memory_space=pltpu.HBM)
    body = functools.partial(
        contract_body, nv, placed, size, own, carried, stepping, nv * width * occ
    )
    return pl.pallas_call(
        body,
        in_specs=[pl.BlockSpec(memory_space=pltpu.SMEM)]
        + [in_vmem] * (len(first) + carried)
        + [in_hbm] * len(arrays),
        out_specs=[in_vmem] * len(out),
        out_shape=out,
        scratch_shapes=[
            pltpu.VMEM((nv * width, occ), jnp.float32),
            pltpu.VMEM((occ, nv * width), jnp.bfloat16),
            pltpu.VMEM((len(blocks), nv, size, width, occ), jnp.bfloat16),
            pltpu.SemaphoreType.DMA((len(blocks), nv)),
        ],
        compiler_params=pltpu.CompilerParams(vmem_limit_bytes=40 * 2**20),
        cost_estimate=pl.CostEstimate(flops=0, bytes_accessed=0, transcendentals=0),
    )(order, *first, *([carry] if carried else []), *arrays)


def share_sums(terms, trial, gap):
    count = terms.shape[0]

    def body(terms_ref, trial_ref, gap_ref, diff_ref, scaled_ref, sums_ref):
        coupling = jnp.sum(terms_ref[...].astype(jnp.float32), axis=0)
        diff, scaled, sums = five_sums(trial_ref[...], gap_ref[...], coupling)
        diff_ref[...] = diff
        scaled_ref[...] = scaled
        lane = lax.broadcasted_iota(jnp.int32, (1, 128), 1)
        row = jnp.zeros((1, 128), jnp.float32)
        for at, value in enumerate(sums):
            row = jnp.where(lane == at, value, row)
        sums_ref[...] = jnp.broadcast_to(row[None], sums_ref.shape)

    like = jax.ShapeDtypeStruct(trial.shape, jnp.float32)
    return pl.pallas_call(
        body,
        out_shape=(like, like, jax.ShapeDtypeStruct((count, 1, 128), jnp.float32)),
        compiler_params=pltpu.CompilerParams(vmem_limit_bytes=24 * 2**20),
    )(terms, trial, gap)


def step_share(diff, scaled, all_sums, before, total):
    def body(diff_ref, scaled_ref, sums_ref, before_ref, next_ref, shifts_ref):
        row = jnp.sum(sums_ref[...], axis=0)
        fresh, shift = finish(
            diff_ref[...], scaled_ref[...], [row[:, at : at + 1] for at in range(5)], total
        )
        next_ref[...] = fresh
        shifts_ref[...] = jnp.concatenate([before_ref[:, :1], shift], axis=1)

    return pl.pallas_call(
        body,
        out_shape=(
            jax.ShapeDtypeStruct(diff.shape, jnp.float32),
            jax.ShapeDtypeStruct((1, 2), jnp.float32),
        ),
    )(diff, scaled, all_sums, before)


def spread(share, count, axes=EVERY):
    copies = jnp.broadcast_to(share[None], (count,) + share.shape)
    return lax.all_to_all(copies, axes, 0, 0, tiled=True)


def local(factors, trials, occ_energy, vir_energy):
    na, nv = lax.axis_size("aux"), lax.axis_size("vir")
    count = na * nv
    aux_at, vir_at = lax.axis_index("aux"), lax.axis_index("vir")
    p_count, width, occ = factors.shape
    own = p_count // nv
    share = occ // na
    total = occ * width * nv
    paired = nv & (nv - 1) == 0

    def partner(at, k):
        return at ^ k if paired else (at + k) % nv

    def source(at, k):
        return at ^ k if paired else (at - k) % nv

    def send(value, k):
        return lax.ppermute(value, "vir", [(one, partner(one, k)) for one in range(nv)])

    order = [source(vir_at, k) for k in range(nv)] + [vir_at, aux_at]
    order = jnp.stack(order).astype(jnp.int32)

    unit = own // 16
    cut_up = unit >= 4 and own % 16 == 0
    sources = {k: [] for k in range(1, nv)}

    def piece(k, low, high, whole=factors):
        return lax.dynamic_slice_in_dim(whole, partner(vir_at, k) * own + low, high - low, 0)

    def exchange(k, low, high, part):
        sources[k].append((low, high, send(part, k)))

    def after_newest(k, *values):
        low, high, array = sources[k][-1]
        *values, array = lax.optimization_barrier((*values, array))
        sources[k][-1] = (low, high, array)
        return values

    marks = [0, own]
    if cut_up:
        marks = [0, 12 * unit, 15 * unit, own]
    far = [k for k in range(nv) if k > 1] + [1]
    later_factors = factors
    for n, k in enumerate(far):
        cut = piece(k, *marks[:2], later_factors)
        if cut_up and n == 0:
            later_factors, cut = lax.optimization_barrier((factors, cut))
        exchange(k, *marks[:2], cut)
    if cut_up:
        later = [[piece(k, low, high, later_factors) for k in far] for low, high in zip(marks[1:], marks[2:])]
        later, trials = lax.optimization_barrier((later, *after_newest(2, trials)))

    gathered = spread(trials[0].T, na, "aux").reshape(occ, width)
    gathered = jnp.concatenate([gathered, vir_energy[None]], axis=0)
    if paired:
        state = {0: gathered}
        bit = nv // 2
        while bit:
            names = sorted(state)
            came = send(jnp.stack([state[k] for k in names]), bit)
            state.update({k ^ bit: came[at] for at, k in enumerate(names)})
            bit //= 2
    else:
        state = {k: send(gathered, k) if k else gathered for k in range(nv)}
    state = jnp.stack([state[k] for k in range(nv)])
    trial = state[:, :occ]
    gap_own = vir_energy[None, :] - lax.dynamic_slice_in_dim(occ_energy, aux_at * share, share)[:, None]
    xt = trial.astype(jnp.bfloat16)

    def call(first, blocks, carry=None, aux_count=None):
        return contract(order, first, factors, sources, blocks, own, carry, aux_count)

    carry = None
    blocks = last_block = [[(0, own)]]
    if cut_up:
        low, high, end = marks[1:]
        for k, cut in enumerate(later[0]):
            exchange(far[k], low, high, cut)
        blocks = [[(n * 4 * unit, (n + 1) * 4 * unit)] for n in range(3)]
        last_block = [[(high, end)]]
        (carry,) = call([xt], blocks)
        cuts, carry = lax.optimization_barrier((later[1], carry))
        for k, cut in zip(far, cuts):
            exchange(k, high, end, cut)
        (carry,) = call([xt], [[(low, high)]], carry)
        blocks.append([(low, high), (high, end)])

    def sum_terms(partial):
        return lax.all_to_all(partial.reshape(count, share, width), EVERY, 0, 0, tiled=True)

    (partial,) = call([xt], last_block, carry, na)
    coupling = jnp.sum(sum_terms(partial).astype(jnp.float32), axis=0).astype(jnp.bfloat16)
    first = [spread(coupling, count), trial, state[:, occ:], occ_energy[:, None]]
    partial, trial_own, before = call(first, blocks, None, na)
    diff, scaled, sums = share_sums(sum_terms(partial), trial_own, gap_own)
    sums = lax.all_to_all(sums, EVERY, 0, 0, tiled=True)
    fresh, shifts = step_share(diff, scaled, sums, before, total)
    return (fresh.T[None], shifts.T)


def solution(mesh):
    placed = (P("aux", "vir", None), P(None, "vir", "aux"), P(), P("vir"))
    return jax.shard_map(
        local, mesh=mesh, in_specs=placed, out_specs=(P(None, "vir", "aux"), P()), check_vma=False
    )
```

```python
import functools

import jax
import jax.numpy as jnp
from jax import lax
from jax.experimental import pallas as pl
from jax.experimental.pallas import tpu as pltpu
from jax.sharding import PartitionSpec as P

EVERY = ("aux", "vir")


def diagonal(occ):
    rows = lax.broadcasted_iota(jnp.int32, (occ, occ), 0)
    return rows == lax.broadcasted_iota(jnp.int32, (occ, occ), 1)


def coulomb_and_exchange(pair, eye):
    density = jnp.sum(jnp.where(eye, pair, 0.0), keepdims=True)
    density = density.astype(jnp.bfloat16).astype(jnp.float32)
    pair = pair.astype(jnp.bfloat16).astype(jnp.float32)
    return (jnp.where(eye, 2.0 * density, 0.0) - pair).astype(jnp.bfloat16)


def side_by_side(blocks, count):
    return jnp.concatenate([blocks[q] for q in range(count)], axis=1)


def five_sums(trial, gap, coupling):
    rounded = trial.astype(jnp.bfloat16).astype(jnp.float32)
    image = gap * rounded + coupling
    scaled_trial = trial / gap
    scaled_diff = trial - image / gap

    def total(values):
        return jnp.sum(values, keepdims=True)

    sums = (
        total(trial * image),
        total(trial * trial),
        total(scaled_diff * scaled_diff),
        total(scaled_diff * scaled_trial),
        total(scaled_trial * scaled_trial),
    )
    return scaled_diff, scaled_trial, sums


def finish(scaled_diff, scaled_trial, sums, count):
    cross_sum, self_sum, diff_sum, mixed_sum, scaled_sum = sums
    shift = cross_sum / self_sum
    mean_square = (diff_sum + 2.0 * shift * mixed_sum + shift * shift * scaled_sum) / count
    return (scaled_diff + shift * scaled_trial) * lax.rsqrt(mean_square + 1e-06), shift


def contract_body(nv, blocks, size, own, carried, stepping, total, order_ref, *refs):
    first_refs, refs = refs[: 4 if stepping else 1], refs[4 if stepping else 1 :]
    carry_ref, f_refs = (refs[0], refs[1:]) if carried else (None, refs)
    f_count = 1 + max(at for block in blocks for _, _, places in block for at, _ in places)
    f_refs, refs = f_refs[:f_count], f_refs[f_count:]
    out_refs, (acc_ref, xt_ref, held, sems) = refs[:-4], refs[-4:]
    out_ref = out_refs[0]
    width, occ = held.shape[3:]
    near_start = order_ref[nv] * own

    for at, block in enumerate(blocks):
        for k in range(nv):
            into_at = 0
            for low, high, places in block:
                array, offset = places[k]
                start = near_start + low if k == 0 else offset
                count = high - low
                pltpu.make_async_copy(
                    f_refs[array].at[pl.ds(start, count)],
                    held.at[at, k, pl.ds(into_at, count)],
                    sems.at[at, k],
                ).start()
                into_at += count

    acc_ref[...] = carry_ref[...] if carried else jnp.zeros_like(acc_ref)
    if stepping:
        shares_ref, trial_ref, vir_ref, occ_ref = first_refs
        own_ref, shift_ref = out_refs[1:]
        share = own_ref.shape[0]
        coupling = jnp.concatenate(
            [
                shares_ref[r * nv + order_ref[k]].astype(jnp.float32)
                for k in range(nv)
                for r in range(occ // share)
            ],
            axis=0,
        )
        gap = jnp.concatenate([vir_ref[k] - occ_ref[...] for k in range(nv)], axis=0)
        diff, scaled, sums = five_sums(trial_ref[...].reshape(nv * occ, width), gap, coupling)
        fresh, shift = finish(diff, scaled, sums, total)
        shift_ref[...] = jnp.broadcast_to(shift, shift_ref.shape)
        for k in range(nv):
            rows = fresh[k * occ : (k + 1) * occ]
            xt_ref[:, k * width : (k + 1) * width] = rows.astype(jnp.bfloat16)
        mine = fresh[:share]
        for r in range(1, occ // share):
            rows = fresh[r * share : (r + 1) * share]
            mine = jnp.where(order_ref[nv + 1] == r, rows, mine)
        own_ref[...] = mine
    else:
        for k in range(nv):
            xt_ref[:, k * width : (k + 1) * width] = first_refs[0][k]
    eye = lax.broadcasted_iota(jnp.int32, (occ, occ), 0) == lax.broadcasted_iota(
        jnp.int32, (occ, occ), 1
    )

    def work(at, _):
        for k in range(nv):
            pltpu.make_async_copy(held.at[at, k], held.at[at, k], sems.at[at, k]).wait()
        tall = jnp.concatenate(
            [
                jnp.concatenate([held[at, k, q] for q in range(size)], axis=1)
                for k in range(nv)
            ],
            axis=0,
        )
        pairs = jnp.dot(xt_ref[...], tall, preferred_element_type=jnp.float32)
        mixes = []
        for q in range(size):
            pair = pairs[:, q * occ : (q + 1) * occ]
            density = jnp.sum(jnp.where(eye, pair, 0.0), keepdims=True)
            density = density.astype(jnp.bfloat16).astype(jnp.float32)
            pair = pair.astype(jnp.bfloat16).astype(jnp.float32)
            mixes.append((jnp.where(eye, 2.0 * density, 0.0) - pair).astype(jnp.bfloat16))
        mix = jnp.concatenate(mixes, axis=0)
        acc_ref[...] += jnp.dot(tall, mix, preferred_element_type=jnp.float32)
        return _

    lax.fori_loop(0, len(blocks), work, 0)
    if len(out_ref.shape) == 2:
        out_ref[...] = acc_ref[...]
        return
    share = out_ref.shape[2]
    for k in range(nv):
        turned = acc_ref[k * width : (k + 1) * width, :].T
        for r in range(occ // share):
            out_ref[r, order_ref[k]] = turned[r * share : (r + 1) * share, :].astype(out_ref.dtype)


def contract(order, first, factors, sources, blocks, own, carry=None, aux_count=None):
    p_count, width, occ = factors.shape
    nv = p_count // own
    carried, stepping = carry is not None, len(first) > 1
    size = sum(high - low for low, high in blocks[0])
    arrays, placed = [factors], []
    for block in blocks:
        placed.append([])
        for low, high in block:
            places = [(0, 0)]
            for k in range(1, nv):
                start, array = next((a, x) for a, b, x in sources[k] if a <= low and high <= b)
                at = next((n for n, x in enumerate(arrays) if x is array), len(arrays))
                if at == len(arrays):
                    arrays.append(array)
                places.append((at, low - start))
            placed[-1].append((low, high, places))
    if aux_count is None:
        out = [jax.ShapeDtypeStruct((nv * width, occ), jnp.float32)]
    else:
        out = [jax.ShapeDtypeStruct((aux_count, nv, occ // aux_count, width), jnp.bfloat16)]
    if stepping:
        out.append(jax.ShapeDtypeStruct((occ // aux_count, width), jnp.float32))
        out.append(jax.ShapeDtypeStruct((1, 128), jnp.float32))
    in_vmem, in_hbm = pl.BlockSpec(memory_space=pltpu.VMEM), pl.BlockSpec(memory_space=pltpu.HBM)
    body = functools.partial(
        contract_body, nv, placed, size, own, carried, stepping, nv * width * occ
    )
    return pl.pallas_call(
        body,
        in_specs=[pl.BlockSpec(memory_space=pltpu.SMEM)]
        + [in_vmem] * (len(first) + carried)
        + [in_hbm] * len(arrays),
        out_specs=[in_vmem] * len(out),
        out_shape=out,
        scratch_shapes=[
            pltpu.VMEM((nv * width, occ), jnp.float32),
            pltpu.VMEM((occ, nv * width), jnp.bfloat16),
            pltpu.VMEM((len(blocks), nv, size, width, occ), jnp.bfloat16),
            pltpu.SemaphoreType.DMA((len(blocks), nv)),
        ],
        compiler_params=pltpu.CompilerParams(vmem_limit_bytes=(58 if stepping else 24) * 2**20),
        cost_estimate=pl.CostEstimate(flops=0, bytes_accessed=0, transcendentals=0),
    )(order, *first, *([carry] if carried else []), *arrays)


def share_sums(terms, trial, gap):
    count = terms.shape[0]

    def body(terms_ref, trial_ref, gap_ref, diff_ref, scaled_ref, sums_ref):
        coupling = jnp.sum(terms_ref[...].astype(jnp.float32), axis=0)
        diff, scaled, sums = five_sums(trial_ref[...], gap_ref[...], coupling)
        diff_ref[...] = diff
        scaled_ref[...] = scaled
        lane = lax.broadcasted_iota(jnp.int32, (1, 128), 1)
        row = jnp.zeros((1, 128), jnp.float32)
        for at, value in enumerate(sums):
            row = jnp.where(lane == at, value, row)
        sums_ref[...] = jnp.broadcast_to(row[None], sums_ref.shape)

    like = jax.ShapeDtypeStruct(trial.shape, jnp.float32)
    return pl.pallas_call(
        body,
        out_shape=(like, like, jax.ShapeDtypeStruct((count, 1, 128), jnp.float32)),
        compiler_params=pltpu.CompilerParams(vmem_limit_bytes=24 * 2**20),
    )(terms, trial, gap)


def step_share(diff, scaled, all_sums, before, total):
    def body(diff_ref, scaled_ref, sums_ref, before_ref, next_ref, shifts_ref):
        row = jnp.sum(sums_ref[...], axis=0)
        fresh, shift = finish(
            diff_ref[...], scaled_ref[...], [row[:, at : at + 1] for at in range(5)], total
        )
        next_ref[...] = fresh
        shifts_ref[...] = jnp.concatenate([before_ref[:, :1], shift], axis=1)

    return pl.pallas_call(
        body,
        out_shape=(
            jax.ShapeDtypeStruct(diff.shape, jnp.float32),
            jax.ShapeDtypeStruct((1, 2), jnp.float32),
        ),
    )(diff, scaled, all_sums, before)


def share_copies(terms):
    def body(terms_ref, copies_ref):
        coupling = jnp.sum(terms_ref[...].astype(jnp.float32), axis=0).astype(jnp.bfloat16)
        copies_ref[...] = jnp.broadcast_to(coupling[None], copies_ref.shape)

    return pl.pallas_call(body, out_shape=jax.ShapeDtypeStruct(terms.shape, jnp.bfloat16))(terms)


def spread(share, count, axes=EVERY):
    copies = jnp.broadcast_to(share[None], (count,) + share.shape)
    return lax.all_to_all(copies, axes, 0, 0, tiled=True)


def local(factors, trials, occ_energy, vir_energy):
    na, nv = lax.axis_size("aux"), lax.axis_size("vir")
    count = na * nv
    aux_at, vir_at = lax.axis_index("aux"), lax.axis_index("vir")
    p_count, width, occ = factors.shape
    own = p_count // nv
    share = occ // na
    total = occ * width * nv
    paired = nv & (nv - 1) == 0

    def partner(at, k):
        return at ^ k if paired else (at + k) % nv

    def source(at, k):
        return at ^ k if paired else (at - k) % nv

    def send(value, k):
        return lax.ppermute(value, "vir", [(one, partner(one, k)) for one in range(nv)])

    order = [source(vir_at, k) for k in range(nv)] + [vir_at, aux_at]
    order = jnp.stack(order).astype(jnp.int32)

    unit = own // 16
    cut_up = unit >= 4 and own % 16 == 0
    sources = {k: [] for k in range(1, nv)}

    def piece(k, low, high, whole=factors):
        return lax.dynamic_slice_in_dim(whole, partner(vir_at, k) * own + low, high - low, 0)

    def exchange(k, low, high, part):
        sources[k].append((low, high, send(part, k)))

    def after_newest(k, *values):
        low, high, array = sources[k][-1]
        *values, array = lax.optimization_barrier((*values, array))
        sources[k][-1] = (low, high, array)
        return values

    marks = [0, own]
    if cut_up:
        marks = [0, 12 * unit, 15 * unit, own]
    far = [k for k in range(nv) if k > 1] + [1]
    later_factors = factors
    for n, k in enumerate(far):
        cut = piece(k, *marks[:2], later_factors)
        if cut_up and n == 0:
            later_factors, cut = lax.optimization_barrier((factors, cut))
        exchange(k, *marks[:2], cut)
    if cut_up:
        later = [[piece(k, low, high, later_factors) for k in far] for low, high in zip(marks[1:], marks[2:])]
        later, trials = lax.optimization_barrier((later, *after_newest(2, trials)))

    gathered = spread(trials[0].T, na, "aux").reshape(occ, width)
    gathered = jnp.concatenate([gathered, vir_energy[None]], axis=0)
    if paired:
        state = {0: gathered}
        bit = nv // 2
        while bit:
            names = sorted(state)
            came = send(jnp.stack([state[k] for k in names]), bit)
            state.update({k ^ bit: came[at] for at, k in enumerate(names)})
            bit //= 2
    else:
        state = {k: send(gathered, k) if k else gathered for k in range(nv)}
    state = jnp.stack([state[k] for k in range(nv)])
    trial = state[:, :occ]
    gap_own = vir_energy[None, :] - lax.dynamic_slice_in_dim(occ_energy, aux_at * share, share)[:, None]
    xt = trial.astype(jnp.bfloat16)

    def call(first, blocks, carry=None, aux_count=None):
        return contract(order, first, factors, sources, blocks, own, carry, aux_count)

    carry = None
    blocks = last_block = [[(0, own)]]
    if cut_up:
        low, high, end = marks[1:]
        for k, cut in enumerate(later[0]):
            exchange(far[k], low, high, cut)
        blocks = [[(n * 4 * unit, (n + 1) * 4 * unit)] for n in range(3)]
        last_block = [[(high, end)]]
        (carry,) = call([xt], blocks)
        cuts, carry = lax.optimization_barrier((later[1], carry))
        for k, cut in zip(far, cuts):
            exchange(k, high, end, cut)
        (carry,) = call([xt], [[(low, high)]], carry)
        blocks.append([(low, high), (high, end)])

    def sum_terms(partial):
        return lax.all_to_all(partial.reshape(count, share, width), EVERY, 0, 0, tiled=True)

    (partial,) = call([xt], last_block, carry, na)
    copies = share_copies(sum_terms(partial))
    first = [lax.all_to_all(copies, EVERY, 0, 0, tiled=True), trial, state[:, occ:], occ_energy[:, None]]
    partial, trial_own, before = call(first, blocks, None, na)
    diff, scaled, sums = share_sums(sum_terms(partial), trial_own, gap_own)
    sums = lax.all_to_all(sums, EVERY, 0, 0, tiled=True)
    fresh, shifts = step_share(diff, scaled, sums, before, total)
    return (fresh.T[None], shifts.T)


def solution(mesh):
    placed = (P("aux", "vir", None), P(None, "vir", "aux"), P(), P("vir"))
    return jax.shard_map(
        local, mesh=mesh, in_specs=placed, out_specs=(P(None, "vir", "aux"), P()), check_vma=False
    )
```

```python
import functools

import jax
import jax.numpy as jnp
from jax import lax
from jax.experimental import pallas as pl
from jax.experimental.pallas import tpu as pltpu
from jax.sharding import PartitionSpec as P

EVERY = ("aux", "vir")


def diagonal(occ):
    rows = lax.broadcasted_iota(jnp.int32, (occ, occ), 0)
    return rows == lax.broadcasted_iota(jnp.int32, (occ, occ), 1)


def coulomb_and_exchange(pair, eye):
    density = jnp.sum(jnp.where(eye, pair, 0.0), keepdims=True)
    density = density.astype(jnp.bfloat16).astype(jnp.float32)
    pair = pair.astype(jnp.bfloat16).astype(jnp.float32)
    return (jnp.where(eye, 2.0 * density, 0.0) - pair).astype(jnp.bfloat16)


def side_by_side(blocks, count):
    return jnp.concatenate([blocks[q] for q in range(count)], axis=1)


def five_sums(trial, gap, coupling):
    rounded = trial.astype(jnp.bfloat16).astype(jnp.float32)
    image = gap * rounded + coupling
    scaled_trial = trial / gap
    scaled_diff = trial - image / gap

    def total(values):
        return jnp.sum(values, keepdims=True)

    sums = (
        total(trial * image),
        total(trial * trial),
        total(scaled_diff * scaled_diff),
        total(scaled_diff * scaled_trial),
        total(scaled_trial * scaled_trial),
    )
    return scaled_diff, scaled_trial, sums


def finish(scaled_diff, scaled_trial, sums, count):
    cross_sum, self_sum, diff_sum, mixed_sum, scaled_sum = sums
    shift = cross_sum / self_sum
    mean_square = (diff_sum + 2.0 * shift * mixed_sum + shift * shift * scaled_sum) / count
    return (scaled_diff + shift * scaled_trial) * lax.rsqrt(mean_square + 1e-06), shift


def diagonal(occ):
    rows = lax.broadcasted_iota(jnp.int32, (occ, occ), 0)
    return rows == lax.broadcasted_iota(jnp.int32, (occ, occ), 1)


def coulomb_and_exchange(pair, eye):
    density = jnp.sum(jnp.where(eye, pair, 0.0), keepdims=True)
    density = density.astype(jnp.bfloat16).astype(jnp.float32)
    pair = pair.astype(jnp.bfloat16).astype(jnp.float32)
    return (jnp.where(eye, 2.0 * density, 0.0) - pair).astype(jnp.bfloat16)


def side_by_side(blocks, count):
    return jnp.concatenate([blocks[q] for q in range(count)], axis=1)


def contract_body(nv, blocks, size, own, carried, stepping, total, order_ref, *refs):
    first_refs, refs = refs[: 4 if stepping else 1], refs[4 if stepping else 1 :]
    carry_ref, f_refs = (refs[0], refs[1:]) if carried else (None, refs)
    f_count = 1 + max(at for block in blocks for _, _, places in block for at, _ in places)
    f_refs, refs = f_refs[:f_count], f_refs[f_count:]
    out_refs, (acc_ref, xt_ref, held, sems) = refs[:-4], refs[-4:]
    out_ref = out_refs[0]
    width, occ = held.shape[3:]
    near_start = order_ref[nv] * own

    for at, block in enumerate(blocks):
        for k in range(nv):
            into_at = 0
            for low, high, places in block:
                array, offset = places[k]
                start = near_start + low if k == 0 else offset
                count = high - low
                pltpu.make_async_copy(
                    f_refs[array].at[pl.ds(start, count)],
                    held.at[at, k, pl.ds(into_at, count)],
                    sems.at[at, k],
                ).start()
                into_at += count

    acc_ref[...] = carry_ref[...] if carried else jnp.zeros_like(acc_ref)
    if stepping:
        shares_ref, trial_ref, vir_ref, occ_ref = first_refs
        own_ref, shift_ref, next_ref = out_refs[1:]
        share = own_ref.shape[0]
        coupling = jnp.concatenate(
            [
                shares_ref[r * nv + order_ref[k]].astype(jnp.float32)
                for k in range(nv)
                for r in range(occ // share)
            ],
            axis=0,
        )
        gap = jnp.concatenate([vir_ref[k] - occ_ref[...] for k in range(nv)], axis=0)
        diff, scaled, sums = five_sums(trial_ref[...].reshape(nv * occ, width), gap, coupling)
        fresh, shift = finish(diff, scaled, sums, total)
        shift_ref[...] = jnp.broadcast_to(shift, shift_ref.shape)
        for k in range(nv):
            rows = fresh[k * occ : (k + 1) * occ]
            xt_ref[:, k * width : (k + 1) * width] = rows.astype(jnp.bfloat16)
            next_ref[k] = rows.astype(jnp.bfloat16)
        mine = fresh[:share]
        for r in range(1, occ // share):
            rows = fresh[r * share : (r + 1) * share]
            mine = jnp.where(order_ref[nv + 1] == r, rows, mine)
        own_ref[...] = mine
    else:
        for k in range(nv):
            xt_ref[:, k * width : (k + 1) * width] = first_refs[0][k]
    eye = diagonal(occ)

    def work(at, _):
        for k in range(nv):
            pltpu.make_async_copy(held.at[at, k], held.at[at, k], sems.at[at, k]).wait()
        tall = jnp.concatenate(
            [
                jnp.concatenate([held[at, k, q] for q in range(size)], axis=1)
                for k in range(nv)
            ],
            axis=0,
        )
        pairs = jnp.dot(xt_ref[...], tall, preferred_element_type=jnp.float32)
        mix = jnp.concatenate(
            [coulomb_and_exchange(pairs[:, q * occ : (q + 1) * occ], eye) for q in range(size)],
            axis=0,
        )
        acc_ref[...] += jnp.dot(tall, mix, preferred_element_type=jnp.float32)
        return _

    lax.fori_loop(0, len(blocks), work, 0)
    if len(out_ref.shape) == 2:
        out_ref[...] = acc_ref[...]
        return
    share = out_ref.shape[2]
    for k in range(nv):
        turned = acc_ref[k * width : (k + 1) * width, :].T
        for r in range(occ // share):
            out_ref[r, order_ref[k]] = turned[r * share : (r + 1) * share, :].astype(out_ref.dtype)


def contract(order, first, factors, sources, blocks, own, share, carry=None, aux_count=None):
    p_count, width, occ = factors.shape
    nv = p_count // own
    carried, stepping = carry is not None, len(first) > 1
    size = sum(high - low for low, high in blocks[0])
    arrays, placed = [factors], []
    for block in blocks:
        placed.append([])
        for low, high in block:
            places = [(0, 0)]
            for k in range(1, nv):
                start, array = next((a, x) for a, b, x in sources[k] if a <= low and high <= b)
                at = next((n for n, x in enumerate(arrays) if x is array), len(arrays))
                if at == len(arrays):
                    arrays.append(array)
                places.append((at, low - start))
            placed[-1].append((low, high, places))
    if aux_count is None:
        out = [jax.ShapeDtypeStruct((nv * width, occ), jnp.float32)]
    else:
        out = [jax.ShapeDtypeStruct((aux_count, nv, occ // aux_count, width), jnp.bfloat16)]
    if stepping:
        out.append(jax.ShapeDtypeStruct((share, width), jnp.float32))
        out.append(jax.ShapeDtypeStruct((1, 128), jnp.float32))
        out.append(jax.ShapeDtypeStruct((nv, occ, width), jnp.bfloat16))
    in_vmem, in_hbm = pl.BlockSpec(memory_space=pltpu.VMEM), pl.BlockSpec(memory_space=pltpu.HBM)
    body = functools.partial(
        contract_body, nv, placed, size, own, carried, stepping, nv * width * occ
    )
    return pl.pallas_call(
        body,
        in_specs=[pl.BlockSpec(memory_space=pltpu.SMEM)]
        + [in_vmem] * (len(first) + carried)
        + [in_hbm] * len(arrays),
        out_specs=[in_vmem] * len(out),
        out_shape=out,
        scratch_shapes=[
            pltpu.VMEM((nv * width, occ), jnp.float32),
            pltpu.VMEM((occ, nv * width), jnp.bfloat16),
            pltpu.VMEM((len(blocks), nv, size, width, occ), jnp.bfloat16),
            pltpu.SemaphoreType.DMA((len(blocks), nv)),
        ],
        compiler_params=pltpu.CompilerParams(vmem_limit_bytes=(58 if stepping else 24) * 2**20),
        cost_estimate=pl.CostEstimate(
            flops=4 * own * nv * width * occ * occ * stepping,
            bytes_accessed=2 * own * nv * width * occ * stepping,
            transcendentals=0,
        ),
    )(order, *first, *([carry] if carried else []), *arrays)


def partial_pairs(factors, xt_own, own, kept, unit):
    p_count, width, occ = factors.shape
    nv, per = p_count // own, kept // unit

    def body(xt_ref, f_ref, out_ref):
        wide = side_by_side(f_ref, unit)
        pairs = jnp.dot(xt_ref[...], wide, preferred_element_type=jnp.float32)
        for q in range(unit):
            out_ref[q] = pairs[:, q * occ : (q + 1) * occ].astype(jnp.bfloat16)

    return pl.pallas_call(
        body,
        grid=(nv, per),
        in_specs=[
            pl.BlockSpec((occ, width), lambda b, t: (0, 0)),
            pl.BlockSpec((unit, width, occ), lambda b, t: (b * (own // unit) + (own - kept) // unit + t, 0, 0)),
        ],
        out_specs=pl.BlockSpec((unit, occ, occ), lambda b, t: (b * per + t, 0, 0)),
        out_shape=jax.ShapeDtypeStruct((nv * kept, occ, occ), jnp.bfloat16),
        cost_estimate=pl.CostEstimate(flops=0, bytes_accessed=0, transcendentals=0),
    )(xt_own, factors)


def contract_pairs(order, factors, mine, other, carry, own, kept, unit):
    p_count, width, occ = factors.shape
    nv, per = p_count // own, kept // unit
    half = nv * per // 2

    def body(order_ref, mine_ref, other_ref, f_ref, carry_ref, out_ref):
        step = pl.program_id(0)

        @pl.when(step == 0)
        def _():
            out_ref[...] = carry_ref[...]

        eye = diagonal(occ)
        is_mine = step < half
        mix = jnp.concatenate(
            [
                coulomb_and_exchange(
                    jnp.where(is_mine, mine_ref[q].astype(jnp.float32), other_ref[q].astype(jnp.float32)), eye
                )
                for q in range(unit)
            ],
            axis=0,
        )
        wide = side_by_side(f_ref, unit)
        out_ref[0:width, :] += jnp.dot(wide, mix, preferred_element_type=jnp.float32)

    def place(g, order):
        core = order[nv + 2]
        at = jnp.where(g < half, core * half + g, (1 - core) * half + g - half)
        return (lax.div(at, per) * (own // unit) + (own - kept) // unit + lax.rem(at, per), 0, 0)

    whole = pl.BlockSpec((nv * width, occ), lambda g, order: (0, 0))
    return pl.pallas_call(
        body,
        grid_spec=pltpu.PrefetchScalarGridSpec(
            num_scalar_prefetch=1,
            grid=(2 * half,),
            in_specs=[
                pl.BlockSpec((unit, occ, occ), lambda g, order: (jnp.minimum(g, half - 1), 0, 0)),
                pl.BlockSpec((unit, occ, occ), lambda g, order: (jnp.maximum(g - half, 0), 0, 0)),
                pl.BlockSpec((unit, width, occ), place),
                whole,
            ],
            out_specs=whole,
        ),
        out_shape=jax.ShapeDtypeStruct((nv * width, occ), jnp.float32),
        cost_estimate=pl.CostEstimate(flops=0, bytes_accessed=0, transcendentals=0),
    )(order, mine, other, factors, carry)


def share_sums(terms, trial, gap):
    count = terms.shape[0]

    def body(terms_ref, trial_ref, gap_ref, diff_ref, scaled_ref, sums_ref):
        coupling = jnp.sum(terms_ref[...].astype(jnp.float32), axis=0)
        diff, scaled, sums = five_sums(trial_ref[...], gap_ref[...], coupling)
        diff_ref[...] = diff
        scaled_ref[...] = scaled
        lane = lax.broadcasted_iota(jnp.int32, (1, 128), 1)
        row = jnp.zeros((1, 128), jnp.float32)
        for at, value in enumerate(sums):
            row = jnp.where(lane == at, value, row)
        sums_ref[...] = jnp.broadcast_to(row[None], sums_ref.shape)

    like = jax.ShapeDtypeStruct(trial.shape, jnp.float32)
    return pl.pallas_call(
        body,
        out_shape=(like, like, jax.ShapeDtypeStruct((count, 1, 128), jnp.float32)),
        compiler_params=pltpu.CompilerParams(vmem_limit_bytes=24 * 2**20),
    )(terms, trial, gap)


def step_share(diff, scaled, all_sums, before, total):
    def body(diff_ref, scaled_ref, sums_ref, before_ref, next_ref, shifts_ref):
        row = jnp.sum(sums_ref[...], axis=0)
        fresh, shift = finish(
            diff_ref[...], scaled_ref[...], [row[:, at : at + 1] for at in range(5)], total
        )
        next_ref[...] = fresh
        shifts_ref[...] = jnp.concatenate([before_ref[:, :1], shift], axis=1)

    return pl.pallas_call(
        body,
        out_shape=(
            jax.ShapeDtypeStruct(diff.shape, jnp.float32),
            jax.ShapeDtypeStruct((1, 2), jnp.float32),
        ),
    )(diff, scaled, all_sums, before)


def share_copies(terms):
    def body(terms_ref, copies_ref):
        coupling = jnp.sum(terms_ref[...].astype(jnp.float32), axis=0).astype(jnp.bfloat16)
        copies_ref[...] = jnp.broadcast_to(coupling[None], copies_ref.shape)

    return pl.pallas_call(body, out_shape=jax.ShapeDtypeStruct(terms.shape, jnp.bfloat16))(terms)


def spread(share, count, axes=EVERY):
    copies = jnp.broadcast_to(share[None], (count,) + share.shape)
    return lax.all_to_all(copies, axes, 0, 0, tiled=True)


def local(factors, trials, occ_energy, vir_energy):
    na, nv = lax.axis_size("aux"), lax.axis_size("vir")
    count = na * nv
    aux_at, vir_at = lax.axis_index("aux"), lax.axis_index("vir")
    p_count, width, occ = factors.shape
    own = p_count // nv
    share = occ // na
    total = occ * width * nv
    paired = nv & (nv - 1) == 0

    def partner(at, k):
        return at ^ k if paired else (at + k) % nv

    def source(at, k):
        return at ^ k if paired else (at - k) % nv

    def send(value, k):
        return lax.ppermute(value, "vir", [(one, partner(one, k)) for one in range(nv)])

    order = [source(vir_at, k) for k in range(nv)] + [vir_at, aux_at, vir_at & 1]
    order = jnp.stack(order).astype(jnp.int32)

    unit = own // 16
    cut_up = paired and nv >= 4 and unit >= 4 and own % 16 == 0
    sources = {k: [] for k in range(1, nv)}

    def piece(k, low, high, whole=factors):
        return lax.dynamic_slice_in_dim(whole, partner(vir_at, k) * own + low, high - low, 0)

    def exchange(k, low, high, part):
        sources[k].append((low, high, send(part, k)))

    def after_newest(k, *values):
        low, high, array = sources[k][-1]
        *values, array = lax.optimization_barrier((*values, array))
        sources[k][-1] = (low, high, array)
        return values

    low, high, end = 11 * unit, 13 * unit, 14 * unit
    far = [k for k in range(nv) if k > 1] + [1]
    starts = {k: high if cut_up else own for k in far}
    if cut_up:
        starts[2] = low
    later_factors = factors
    for n, k in enumerate(far):
        cut = piece(k, 0, starts[k], later_factors)
        if cut_up and n == 0:
            later_factors, cut = lax.optimization_barrier((factors, cut))
        exchange(k, 0, starts[k], cut)
    if cut_up:
        middle = piece(2, low, high, later_factors)
        ending = [piece(k, high, end, later_factors) for k in far]
        middle, ending, trials = lax.optimization_barrier((middle, ending, *after_newest(2, trials)))

    gathered = spread(trials[0].T, na, "aux").reshape(occ, width)
    gathered = jnp.concatenate([gathered, vir_energy[None]], axis=0)
    if paired:
        state = {0: gathered}
        bit = nv // 2
        while bit:
            names = sorted(state)
            came = send(jnp.stack([state[k] for k in names]), bit)
            if cut_up and bit == 2:
                middle, came = lax.optimization_barrier((middle, came))
                exchange(2, low, high, middle)
            state.update({k ^ bit: came[at] for at, k in enumerate(names)})
            bit //= 2
    else:
        state = {k: send(gathered, k) if k else gathered for k in range(nv)}
    state = jnp.stack([state[k] for k in range(nv)])
    trial = state[:, :occ]
    gap_own = vir_energy[None, :] - lax.dynamic_slice_in_dim(occ_energy, aux_at * share, share)[:, None]
    xt = trial.astype(jnp.bfloat16)

    def call(first, blocks, carry=None, aux_count=None):
        return contract(order, first, factors, sources, blocks, own, share, carry, aux_count)

    carry = None
    blocks = last_block = [[(0, own)]]
    if cut_up:
        kept = own - end
        half, core = nv * kept // 2, vir_at & 1
        sums = partial_pairs(factors, xt[0], own, kept, kept)
        mine = lax.dynamic_slice_in_dim(sums, core * half, half, 0)
        other = lax.dynamic_slice_in_dim(sums, (1 - core) * half, half, 0)

        def add(one, two):
            return (one.astype(jnp.float32) + two.astype(jnp.float32)).astype(jnp.bfloat16)

        (carry,) = call([xt], [[(n * low // 4, (n + 1) * low // 4)] for n in range(4)])
        other, carry = after_newest(2, other, carry)
        mine = add(mine, send(other, 1))
        cuts, mine = lax.optimization_barrier((ending, mine))
        bit = 2
        while bit < nv:
            mine = add(mine, send(mine, bit))
            bit *= 2
        for k, cut in zip(far, cuts):
            exchange(k, high, end, cut)
        (carry,) = call([xt], [[(low, high)]], carry)
        carry = contract_pairs(order, factors, mine, send(mine, 1), carry, own, kept, kept)
        last_block = [[(high, end)]]
        size = end // 4
        blocks = [[(n * size, (n + 1) * size)] for n in range(3)]
        blocks.append([(3 * size, low), (low, high), (high, end)])

    def sum_terms(partial):
        return lax.all_to_all(partial.reshape(count, share, width), EVERY, 0, 0, tiled=True)

    (partial,) = call([xt], last_block, carry, na)
    copies = share_copies(sum_terms(partial))
    if cut_up:
        whole, copies = lax.optimization_barrier((factors, copies))
        for k in far:
            exchange(k, end, own, piece(k, end, own, whole))
    first = [lax.all_to_all(copies, EVERY, 0, 0, tiled=True), trial, state[:, occ:], occ_energy[:, None]]
    if cut_up:
        carry, trial_own, before, xt = call(first, blocks)
        (partial,) = call([xt], [[(end, own)]], carry, na)
    else:
        partial, trial_own, before, xt = call(first, blocks, None, na)
    diff, scaled, sums = share_sums(sum_terms(partial), trial_own, gap_own)
    sums = lax.all_to_all(sums, EVERY, 0, 0, tiled=True)
    fresh, shifts = step_share(diff, scaled, sums, before, total)
    return (fresh.T[None], shifts.T)


def solution(mesh):
    placed = (P("aux", "vir", None), P(None, "vir", "aux"), P(), P("vir"))
    return jax.shard_map(
        local, mesh=mesh, in_specs=placed, out_specs=(P(None, "vir", "aux"), P()), check_vma=False
    )
```

```python
import functools

import jax
import jax.numpy as jnp
from jax import lax
from jax.experimental import pallas as pl
from jax.experimental.pallas import tpu as pltpu
from jax.sharding import PartitionSpec as P

EVERY = ("aux", "vir")


def diagonal(occ):
    rows = lax.broadcasted_iota(jnp.int32, (occ, occ), 0)
    return rows == lax.broadcasted_iota(jnp.int32, (occ, occ), 1)


def coulomb_and_exchange(pair, eye):
    density = jnp.sum(jnp.where(eye, pair, 0.0), keepdims=True)
    density = density.astype(jnp.bfloat16).astype(jnp.float32)
    pair = pair.astype(jnp.bfloat16).astype(jnp.float32)
    return (jnp.where(eye, 2.0 * density, 0.0) - pair).astype(jnp.bfloat16)


def side_by_side(blocks, count):
    return jnp.concatenate([blocks[q] for q in range(count)], axis=1)


def five_sums(trial, gap, coupling):
    rounded = trial.astype(jnp.bfloat16).astype(jnp.float32)
    image = gap * rounded + coupling
    scaled_trial = trial / gap
    scaled_diff = trial - image / gap

    def total(values):
        return jnp.sum(values, keepdims=True)

    sums = (
        total(trial * image),
        total(trial * trial),
        total(scaled_diff * scaled_diff),
        total(scaled_diff * scaled_trial),
        total(scaled_trial * scaled_trial),
    )
    return scaled_diff, scaled_trial, sums


def finish(scaled_diff, scaled_trial, sums, count):
    cross_sum, self_sum, diff_sum, mixed_sum, scaled_sum = sums
    shift = cross_sum / self_sum
    mean_square = (diff_sum + 2.0 * shift * mixed_sum + shift * shift * scaled_sum) / count
    return (scaled_diff + shift * scaled_trial) * lax.rsqrt(mean_square + 1e-06), shift


def contract_body(nv, blocks, size, own, carried, stepping, total, order_ref, *refs):
    first_refs, refs = refs[: 4 if stepping else 1], refs[4 if stepping else 1 :]
    carry_ref, f_refs = (refs[0], refs[1:]) if carried else (None, refs)
    f_count = 1 + max(at for block in blocks for _, _, places in block for at, _ in places)
    f_refs, refs = f_refs[:f_count], f_refs[f_count:]
    out_refs, (acc_ref, xt_ref, held, sems) = refs[:-4], refs[-4:]
    out_ref = out_refs[0]
    width, occ = held.shape[3:]
    near_start = order_ref[nv] * own

    for at, block in enumerate(blocks):
        for k in range(nv):
            into_at = 0
            for low, high, places in block:
                array, offset = places[k]
                start = near_start + low if k == 0 else offset
                count = high - low
                pltpu.make_async_copy(
                    f_refs[array].at[pl.ds(start, count)],
                    held.at[at, k, pl.ds(into_at, count)],
                    sems.at[at, k],
                ).start()
                into_at += count

    acc_ref[...] = carry_ref[...] if carried else jnp.zeros_like(acc_ref)
    if stepping:
        shares_ref, trial_ref, vir_ref, occ_ref = first_refs
        own_ref, shift_ref = out_refs[1:]
        share = own_ref.shape[0]
        coupling = jnp.concatenate(
            [
                shares_ref[r * nv + order_ref[k]].astype(jnp.float32)
                for k in range(nv)
                for r in range(occ // share)
            ],
            axis=0,
        )
        gap = jnp.concatenate([vir_ref[k] - occ_ref[...] for k in range(nv)], axis=0)
        diff, scaled, sums = five_sums(trial_ref[...].reshape(nv * occ, width), gap, coupling)
        fresh, shift = finish(diff, scaled, sums, total)
        shift_ref[...] = jnp.broadcast_to(shift, shift_ref.shape)
        for k in range(nv):
            rows = fresh[k * occ : (k + 1) * occ]
            xt_ref[:, k * width : (k + 1) * width] = rows.astype(jnp.bfloat16)
        mine = fresh[:share]
        for r in range(1, occ // share):
            rows = fresh[r * share : (r + 1) * share]
            mine = jnp.where(order_ref[nv + 1] == r, rows, mine)
        own_ref[...] = mine
    else:
        for k in range(nv):
            xt_ref[:, k * width : (k + 1) * width] = first_refs[0][k]
    eye = lax.broadcasted_iota(jnp.int32, (occ, occ), 0) == lax.broadcasted_iota(
        jnp.int32, (occ, occ), 1
    )

    def work(at, _):
        for k in range(nv):
            pltpu.make_async_copy(held.at[at, k], held.at[at, k], sems.at[at, k]).wait()
        tall = jnp.concatenate(
            [
                jnp.concatenate([held[at, k, q] for q in range(size)], axis=1)
                for k in range(nv)
            ],
            axis=0,
        )
        pairs = jnp.dot(xt_ref[...], tall, preferred_element_type=jnp.float32)
        mixes = []
        for q in range(size):
            pair = pairs[:, q * occ : (q + 1) * occ]
            density = jnp.sum(jnp.where(eye, pair, 0.0), keepdims=True)
            density = density.astype(jnp.bfloat16).astype(jnp.float32)
            pair = pair.astype(jnp.bfloat16).astype(jnp.float32)
            mixes.append((jnp.where(eye, 2.0 * density, 0.0) - pair).astype(jnp.bfloat16))
        mix = jnp.concatenate(mixes, axis=0)
        acc_ref[...] += jnp.dot(tall, mix, preferred_element_type=jnp.float32)
        return _

    lax.fori_loop(0, len(blocks), work, 0)
    if len(out_ref.shape) == 2:
        out_ref[...] = acc_ref[...]
        return
    share = out_ref.shape[2]
    for k in range(nv):
        turned = acc_ref[k * width : (k + 1) * width, :].T
        for r in range(occ // share):
            out_ref[r, order_ref[k]] = turned[r * share : (r + 1) * share, :].astype(out_ref.dtype)


def contract(order, first, factors, sources, blocks, own, carry=None, aux_count=None):
    p_count, width, occ = factors.shape
    nv = p_count // own
    carried, stepping = carry is not None, len(first) > 1
    size = sum(high - low for low, high in blocks[0])
    arrays, placed = [factors], []
    for block in blocks:
        placed.append([])
        for low, high in block:
            places = [(0, 0)]
            for k in range(1, nv):
                start, array = next((a, x) for a, b, x in sources[k] if a <= low and high <= b)
                at = next((n for n, x in enumerate(arrays) if x is array), len(arrays))
                if at == len(arrays):
                    arrays.append(array)
                places.append((at, low - start))
            placed[-1].append((low, high, places))
    if aux_count is None:
        out = [jax.ShapeDtypeStruct((nv * width, occ), jnp.float32)]
    else:
        out = [jax.ShapeDtypeStruct((aux_count, nv, occ // aux_count, width), jnp.bfloat16)]
    if stepping:
        out.append(jax.ShapeDtypeStruct((occ // aux_count, width), jnp.float32))
        out.append(jax.ShapeDtypeStruct((1, 128), jnp.float32))
    in_vmem, in_hbm = pl.BlockSpec(memory_space=pltpu.VMEM), pl.BlockSpec(memory_space=pltpu.HBM)
    body = functools.partial(
        contract_body, nv, placed, size, own, carried, stepping, nv * width * occ
    )
    return pl.pallas_call(
        body,
        in_specs=[pl.BlockSpec(memory_space=pltpu.SMEM)]
        + [in_vmem] * (len(first) + carried)
        + [in_hbm] * len(arrays),
        out_specs=[in_vmem] * len(out),
        out_shape=out,
        scratch_shapes=[
            pltpu.VMEM((nv * width, occ), jnp.float32),
            pltpu.VMEM((occ, nv * width), jnp.bfloat16),
            pltpu.VMEM((len(blocks), nv, size, width, occ), jnp.bfloat16),
            pltpu.SemaphoreType.DMA((len(blocks), nv)),
        ],
        compiler_params=pltpu.CompilerParams(vmem_limit_bytes=46 * 2**20),
        cost_estimate=pl.CostEstimate(flops=0, bytes_accessed=0, transcendentals=0),
    )(order, *first, *([carry] if carried else []), *arrays)


def share_sums(terms, trial, gap):
    count = terms.shape[0]

    def body(terms_ref, trial_ref, gap_ref, ratios_ref, sums_ref):
        coupling = jnp.sum(terms_ref[...].astype(jnp.float32), axis=0)
        diff, scaled, sums = five_sums(trial_ref[...], gap_ref[...], coupling)
        ratios_ref[0] = diff
        ratios_ref[1] = scaled
        lane = lax.broadcasted_iota(jnp.int32, (1, 128), 1)
        row = jnp.zeros((1, 128), jnp.float32)
        for at, value in enumerate(sums):
            row = jnp.where(lane == at, value, row)
        sums_ref[...] = jnp.broadcast_to(row[None], sums_ref.shape)

    ratios = jax.ShapeDtypeStruct((2, *trial.shape), jnp.float32)
    return pl.pallas_call(
        body,
        out_shape=(ratios, jax.ShapeDtypeStruct((count, 1, 128), jnp.float32)),
        compiler_params=pltpu.CompilerParams(vmem_limit_bytes=24 * 2**20),
    )(terms, trial, gap)


def step_share(ratios, all_sums, before, total):
    def body(ratios_ref, sums_ref, before_ref, next_ref, shifts_ref):
        row = jnp.sum(sums_ref[...], axis=0)
        fresh, shift = finish(
            ratios_ref[0], ratios_ref[1], [row[:, at : at + 1] for at in range(5)], total
        )
        next_ref[...] = fresh
        shifts_ref[...] = jnp.concatenate([before_ref[:, :1], shift], axis=1)

    return pl.pallas_call(
        body,
        out_shape=(
            jax.ShapeDtypeStruct(ratios.shape[1:], jnp.float32),
            jax.ShapeDtypeStruct((1, 2), jnp.float32),
        ),
    )(ratios, all_sums, before)


def share_copies(terms):
    def body(terms_ref, copies_ref):
        coupling = jnp.sum(terms_ref[...].astype(jnp.float32), axis=0).astype(jnp.bfloat16)
        copies_ref[...] = jnp.broadcast_to(coupling[None], copies_ref.shape)

    return pl.pallas_call(body, out_shape=jax.ShapeDtypeStruct(terms.shape, jnp.bfloat16))(terms)


def spread(share, count, axes=EVERY):
    copies = jnp.broadcast_to(share[None], (count,) + share.shape)
    return lax.all_to_all(copies, axes, 0, 0, tiled=True)


def local(factors, trials, occ_energy, vir_energy):
    na, nv = lax.axis_size("aux"), lax.axis_size("vir")
    count = na * nv
    aux_at, vir_at = lax.axis_index("aux"), lax.axis_index("vir")
    p_count, width, occ = factors.shape
    own = p_count // nv
    share = occ // na
    total = occ * width * nv
    paired = nv & (nv - 1) == 0

    def partner(at, k):
        return at ^ k if paired else (at + k) % nv

    def source(at, k):
        return at ^ k if paired else (at - k) % nv

    def send(value, k):
        return lax.ppermute(value, "vir", [(one, partner(one, k)) for one in range(nv)])

    order = [source(vir_at, k) for k in range(nv)] + [vir_at, aux_at]
    order = jnp.stack(order).astype(jnp.int32)

    unit = own // 16
    cut_up = unit >= 4 and own % 16 == 0
    sources = {k: [] for k in range(1, nv)}

    def piece(k, low, high, whole=factors):
        return lax.dynamic_slice_in_dim(whole, partner(vir_at, k) * own + low, high - low, 0)

    def exchange(k, low, high, part):
        sources[k].append((low, high, send(part, k)))

    def after_newest(k, *values):
        low, high, array = sources[k][-1]
        *values, array = lax.optimization_barrier((*values, array))
        sources[k][-1] = (low, high, array)
        return values

    marks = [0, own]
    if cut_up:
        marks = [0, 12 * unit, 15 * unit, own]
    far = [k for k in range(nv) if k > 1] + [1]
    later_factors = factors
    for n, k in enumerate(far):
        cut = piece(k, *marks[:2], later_factors)
        if cut_up and n == 0:
            later_factors, cut = lax.optimization_barrier((factors, cut))
        exchange(k, *marks[:2], cut)
    if cut_up:
        later = [[piece(k, low, high, later_factors) for k in far] for low, high in zip(marks[1:], marks[2:])]
        later, trials = lax.optimization_barrier((later, *after_newest(2, trials)))

    gathered = spread(trials[0].T, na, "aux").reshape(occ, width)
    gathered = jnp.concatenate([gathered, vir_energy[None]], axis=0)
    if paired:
        state = {0: gathered}
        bit = nv // 2
        while bit:
            names = sorted(state)
            came = send(jnp.stack([state[k] for k in names]), bit)
            state.update({k ^ bit: came[at] for at, k in enumerate(names)})
            bit //= 2
    else:
        state = {k: send(gathered, k) if k else gathered for k in range(nv)}
    state = jnp.stack([state[k] for k in range(nv)])
    trial = state[:, :occ]
    gap_own = vir_energy[None, :] - lax.dynamic_slice_in_dim(occ_energy, aux_at * share, share)[:, None]
    xt = trial.astype(jnp.bfloat16)

    def call(first, blocks, carry=None, aux_count=None):
        return contract(order, first, factors, sources, blocks, own, carry, aux_count)

    carry = None
    blocks = last_block = [[(0, own)]]
    if cut_up:
        low, high, end = marks[1:]
        for k, cut in enumerate(later[0]):
            exchange(far[k], low, high, cut)
        blocks = [[(n * 4 * unit, (n + 1) * 4 * unit)] for n in range(3)]
        last_block = [[(high, end)]]
        (carry,) = call([xt], blocks)
        cuts, carry = lax.optimization_barrier((later[1], carry))
        for k, cut in zip(far, cuts):
            exchange(k, high, end, cut)
        (carry,) = call([xt], [[(low, high)]], carry)
        blocks.append([(low, high), (high, end)])

    def sum_terms(partial):
        return lax.all_to_all(partial.reshape(count, share, width), EVERY, 0, 0, tiled=True)

    (partial,) = call([xt], last_block, carry, na)
    copies = share_copies(sum_terms(partial))
    first = [lax.all_to_all(copies, EVERY, 0, 0, tiled=True), trial, state[:, occ:], occ_energy[:, None]]
    partial, trial_own, before = call(first, blocks, None, na)
    ratios, sums = share_sums(sum_terms(partial), trial_own, gap_own)
    sums = lax.all_to_all(sums, EVERY, 0, 0, tiled=True)
    fresh, shifts = step_share(ratios, sums, before, total)
    return (fresh.T[None], shifts.T)


def solution(mesh):
    placed = (P("aux", "vir", None), P(None, "vir", "aux"), P(), P("vir"))
    return jax.shard_map(
        local, mesh=mesh, in_specs=placed, out_specs=(P(None, "vir", "aux"), P()), check_vma=False
    )
```

```python
import functools

import jax
import jax.numpy as jnp
from jax import lax
from jax.experimental import pallas as pl
from jax.experimental.pallas import tpu as pltpu
from jax.sharding import PartitionSpec as P

EVERY = ("aux", "vir")


def diagonal(occ):
    rows = lax.broadcasted_iota(jnp.int32, (occ, occ), 0)
    return rows == lax.broadcasted_iota(jnp.int32, (occ, occ), 1)


def coulomb_and_exchange(pair, eye):
    density = jnp.sum(jnp.where(eye, pair, 0.0), keepdims=True)
    density = density.astype(jnp.bfloat16).astype(jnp.float32)
    pair = pair.astype(jnp.bfloat16).astype(jnp.float32)
    return (jnp.where(eye, 2.0 * density, 0.0) - pair).astype(jnp.bfloat16)


def side_by_side(blocks, count):
    return jnp.concatenate([blocks[q] for q in range(count)], axis=1)


def five_sums(trial, gap, coupling):
    rounded = trial.astype(jnp.bfloat16).astype(jnp.float32)
    image = gap * rounded + coupling
    scaled_trial = trial / gap
    scaled_diff = trial - image / gap

    def total(values):
        return jnp.sum(values, keepdims=True)

    sums = (
        total(trial * image),
        total(trial * trial),
        total(scaled_diff * scaled_diff),
        total(scaled_diff * scaled_trial),
        total(scaled_trial * scaled_trial),
    )
    return scaled_diff, scaled_trial, sums


def finish(scaled_diff, scaled_trial, sums, count):
    cross_sum, self_sum, diff_sum, mixed_sum, scaled_sum = sums
    shift = cross_sum / self_sum
    mean_square = (diff_sum + 2.0 * shift * mixed_sum + shift * shift * scaled_sum) / count
    return (scaled_diff + shift * scaled_trial) * lax.rsqrt(mean_square + 1e-06), shift


def contract_body(nv, blocks, size, own, carried, stepping, total, order_ref, *refs):
    first_refs, refs = refs[: 4 if stepping else 1], refs[4 if stepping else 1 :]
    carry_ref, f_refs = (refs[0], refs[1:]) if carried else (None, refs)
    f_count = 1 + max(at for block in blocks for _, _, places in block for at, _ in places)
    f_refs, refs = f_refs[:f_count], f_refs[f_count:]
    out_refs, (acc_ref, xt_ref, held, sems) = refs[:-4], refs[-4:]
    out_ref = out_refs[0]
    width, occ = held.shape[3:]
    near_start = order_ref[nv] * own

    for at, block in enumerate(blocks):
        for k in range(nv):
            into_at = 0
            for low, high, places in block:
                array, offset = places[k]
                start = near_start + low if k == 0 else offset
                count = high - low
                pltpu.make_async_copy(
                    f_refs[array].at[pl.ds(start, count)],
                    held.at[at, k, pl.ds(into_at, count)],
                    sems.at[at, k],
                ).start()
                into_at += count

    acc_ref[...] = carry_ref[...] if carried else jnp.zeros_like(acc_ref)
    if stepping:
        shares_ref, trial_ref, vir_ref, occ_ref = first_refs
        own_ref, shift_ref = out_refs[1:]
        share = own_ref.shape[0]
        coupling = jnp.concatenate(
            [
                shares_ref[r * nv + order_ref[k]].astype(jnp.float32)
                for k in range(nv)
                for r in range(occ // share)
            ],
            axis=0,
        )
        gap = jnp.concatenate([vir_ref[k] - occ_ref[...] for k in range(nv)], axis=0)
        diff, scaled, sums = five_sums(trial_ref[...].reshape(nv * occ, width), gap, coupling)
        fresh, shift = finish(diff, scaled, sums, total)
        shift_ref[...] = jnp.broadcast_to(shift, shift_ref.shape)
        for k in range(nv):
            rows = fresh[k * occ : (k + 1) * occ]
            xt_ref[:, k * width : (k + 1) * width] = rows.astype(jnp.bfloat16)
        mine = fresh[:share]
        for r in range(1, occ // share):
            rows = fresh[r * share : (r + 1) * share]
            mine = jnp.where(order_ref[nv + 1] == r, rows, mine)
        own_ref[...] = mine
    else:
        for k in range(nv):
            xt_ref[:, k * width : (k + 1) * width] = first_refs[0][k]
    eye = lax.broadcasted_iota(jnp.int32, (occ, occ), 0) == lax.broadcasted_iota(
        jnp.int32, (occ, occ), 1
    )

    def work(at, _):
        for k in range(nv):
            pltpu.make_async_copy(held.at[at, k], held.at[at, k], sems.at[at, k]).wait()
        tall = jnp.concatenate(
            [
                jnp.concatenate([held[at, k, q] for q in range(size)], axis=1)
                for k in range(nv)
            ],
            axis=0,
        )
        pairs = jnp.dot(xt_ref[...], tall, preferred_element_type=jnp.float32)
        mixes = []
        for q in range(size):
            pair = pairs[:, q * occ : (q + 1) * occ]
            density = jnp.sum(jnp.where(eye, pair, 0.0), keepdims=True)
            density = density.astype(jnp.bfloat16).astype(jnp.float32)
            pair = pair.astype(jnp.bfloat16).astype(jnp.float32)
            mixes.append((jnp.where(eye, 2.0 * density, 0.0) - pair).astype(jnp.bfloat16))
        mix = jnp.concatenate(mixes, axis=0)
        acc_ref[...] += jnp.dot(tall, mix, preferred_element_type=jnp.float32)
        return _

    lax.fori_loop(0, len(blocks), work, 0)
    if len(out_ref.shape) == 2:
        out_ref[...] = acc_ref[...]
        return
    share = out_ref.shape[2]
    for k in range(nv):
        turned = acc_ref[k * width : (k + 1) * width, :].T
        for r in range(occ // share):
            out_ref[r, order_ref[k]] = turned[r * share : (r + 1) * share, :].astype(out_ref.dtype)


def contract(order, first, factors, sources, blocks, own, carry=None, aux_count=None):
    p_count, width, occ = factors.shape
    nv = p_count // own
    carried, stepping = carry is not None, len(first) > 1
    size = sum(high - low for low, high in blocks[0])
    arrays, placed = [factors], []
    for block in blocks:
        placed.append([])
        for low, high in block:
            places = [(0, 0)]
            for k in range(1, nv):
                start, array = next((a, x) for a, b, x in sources[k] if a <= low and high <= b)
                at = next((n for n, x in enumerate(arrays) if x is array), len(arrays))
                if at == len(arrays):
                    arrays.append(array)
                places.append((at, low - start))
            placed[-1].append((low, high, places))
    if aux_count is None:
        out = [jax.ShapeDtypeStruct((nv * width, occ), jnp.float32)]
    else:
        out = [jax.ShapeDtypeStruct((aux_count, nv, occ // aux_count, width), jnp.bfloat16)]
    if stepping:
        out.append(jax.ShapeDtypeStruct((occ // aux_count, width), jnp.float32))
        out.append(jax.ShapeDtypeStruct((1, 128), jnp.float32))
    in_vmem, in_hbm = pl.BlockSpec(memory_space=pltpu.VMEM), pl.BlockSpec(memory_space=pltpu.HBM)
    body = functools.partial(
        contract_body, nv, placed, size, own, carried, stepping, nv * width * occ
    )
    return pl.pallas_call(
        body,
        in_specs=[pl.BlockSpec(memory_space=pltpu.SMEM)]
        + [in_vmem] * (len(first) + carried)
        + [in_hbm] * len(arrays),
        out_specs=[in_vmem] * len(out),
        out_shape=out,
        scratch_shapes=[
            pltpu.VMEM((nv * width, occ), jnp.float32),
            pltpu.VMEM((occ, nv * width), jnp.bfloat16),
            pltpu.VMEM((len(blocks), nv, size, width, occ), jnp.bfloat16),
            pltpu.SemaphoreType.DMA((len(blocks), nv)),
        ],
        compiler_params=pltpu.CompilerParams(vmem_limit_bytes=46 * 2**20),
        cost_estimate=pl.CostEstimate(flops=0, bytes_accessed=0, transcendentals=0),
    )(order, *first, *([carry] if carried else []), *arrays)


def share_sums(terms, trial, gap):
    count = terms.shape[0]

    def body(terms_ref, trial_ref, gap_ref, ratios_ref, sums_ref):
        coupling = jnp.sum(terms_ref[...].astype(jnp.float32), axis=0)
        diff, scaled, sums = five_sums(trial_ref[...], gap_ref[...], coupling)
        ratios_ref[0] = diff
        ratios_ref[1] = scaled
        lane = lax.broadcasted_iota(jnp.int32, (1, 128), 1)
        row = jnp.zeros((1, 128), jnp.float32)
        for at, value in enumerate(sums):
            row = jnp.where(lane == at, value, row)
        sums_ref[...] = jnp.broadcast_to(row[None], sums_ref.shape)

    ratios = jax.ShapeDtypeStruct((2, *trial.shape), jnp.float32)
    return pl.pallas_call(
        body,
        out_shape=(ratios, jax.ShapeDtypeStruct((count, 1, 128), jnp.float32)),
        compiler_params=pltpu.CompilerParams(vmem_limit_bytes=24 * 2**20),
    )(terms, trial, gap)


def step_share(ratios, all_sums, before, total):
    def body(ratios_ref, sums_ref, before_ref, next_ref, shifts_ref):
        row = jnp.sum(sums_ref[...], axis=0)
        fresh, shift = finish(
            ratios_ref[0], ratios_ref[1], [row[:, at : at + 1] for at in range(5)], total
        )
        next_ref[...] = fresh
        shifts_ref[...] = jnp.concatenate([before_ref[:, :1], shift], axis=1)

    return pl.pallas_call(
        body,
        out_shape=(
            jax.ShapeDtypeStruct(ratios.shape[1:], jnp.float32),
            jax.ShapeDtypeStruct((1, 2), jnp.float32),
        ),
    )(ratios, all_sums, before)


def share_copies(terms):
    def body(terms_ref, copies_ref):
        coupling = jnp.sum(terms_ref[...].astype(jnp.float32), axis=0).astype(jnp.bfloat16)
        copies_ref[...] = jnp.broadcast_to(coupling[None], copies_ref.shape)

    return pl.pallas_call(body, out_shape=jax.ShapeDtypeStruct(terms.shape, jnp.bfloat16))(terms)


def cut_out(whole, start, count):
    parts = 4
    rows = count // parts

    def body(start_ref, whole_ref, out_ref, sems):
        copies = []
        for n in range(parts):
            place = pl.ds(start_ref[0] + n * rows, rows)
            copies.append(
                pltpu.make_async_copy(whole_ref.at[place], out_ref.at[pl.ds(n * rows, rows)], sems.at[n])
            )
        for copy in copies:
            copy.start()
        for copy in copies:
            copy.wait()

    return pl.pallas_call(
        body,
        in_specs=[pl.BlockSpec(memory_space=pltpu.SMEM), pl.BlockSpec(memory_space=pltpu.HBM)],
        out_specs=pl.BlockSpec(memory_space=pltpu.VMEM),
        out_shape=jax.ShapeDtypeStruct((count, *whole.shape[1:]), whole.dtype),
        scratch_shapes=[pltpu.SemaphoreType.DMA((parts,))],
        compiler_params=pltpu.CompilerParams(vmem_limit_bytes=46 * 2**20),
    )(start.astype(jnp.int32)[None], whole)


def spread(share, count, axes=EVERY):
    copies = jnp.broadcast_to(share[None], (count,) + share.shape)
    return lax.all_to_all(copies, axes, 0, 0, tiled=True)


def local(factors, trials, occ_energy, vir_energy):
    na, nv = lax.axis_size("aux"), lax.axis_size("vir")
    count = na * nv
    aux_at, vir_at = lax.axis_index("aux"), lax.axis_index("vir")
    p_count, width, occ = factors.shape
    own = p_count // nv
    share = occ // na
    total = occ * width * nv
    paired = nv & (nv - 1) == 0

    def partner(at, k):
        return at ^ k if paired else (at + k) % nv

    def source(at, k):
        return at ^ k if paired else (at - k) % nv

    def send(value, k):
        return lax.ppermute(value, "vir", [(one, partner(one, k)) for one in range(nv)])

    order = [source(vir_at, k) for k in range(nv)] + [vir_at, aux_at]
    order = jnp.stack(order).astype(jnp.int32)

    unit = own // 16
    cut_up = unit >= 4 and own % 16 == 0
    sources = {k: [] for k in range(1, nv)}

    def piece(k, low, high, whole=factors):
        return lax.dynamic_slice_in_dim(whole, partner(vir_at, k) * own + low, high - low, 0)

    def exchange(k, low, high, part):
        sources[k].append((low, high, send(part, k)))

    def after_newest(k, *values):
        low, high, array = sources[k][-1]
        *values, array = lax.optimization_barrier((*values, array))
        sources[k][-1] = (low, high, array)
        return values

    marks = [0, own]
    if cut_up:
        marks = [0, 9 * unit, 15 * unit, own]
    far = [k for k in range(nv) if k > 1] + [1]
    later_factors = factors
    for n, k in enumerate(far):
        if cut_up and n == 0:
            cut = cut_out(factors, partner(vir_at, k) * own, marks[1])
        else:
            cut = piece(k, *marks[:2], later_factors)
        if cut_up and n == 0:
            later_factors, cut = lax.optimization_barrier((factors, cut))
        exchange(k, *marks[:2], cut)
    if cut_up:
        later = [[piece(k, low, high, later_factors) for k in far] for low, high in zip(marks[1:], marks[2:])]
        later, trials = lax.optimization_barrier((later, *after_newest(2, trials)))

    gathered = spread(trials[0].T, na, "aux").reshape(occ, width)
    gathered = jnp.concatenate([gathered, vir_energy[None]], axis=0)
    if paired:
        state = {0: gathered}
        bit = nv // 2
        while bit:
            names = sorted(state)
            came = send(jnp.stack([state[k] for k in names]), bit)
            state.update({k ^ bit: came[at] for at, k in enumerate(names)})
            bit //= 2
    else:
        state = {k: send(gathered, k) if k else gathered for k in range(nv)}
    state = jnp.stack([state[k] for k in range(nv)])
    trial = state[:, :occ]
    gap_own = vir_energy[None, :] - lax.dynamic_slice_in_dim(occ_energy, aux_at * share, share)[:, None]
    xt = trial.astype(jnp.bfloat16)

    def call(first, blocks, carry=None, aux_count=None):
        return contract(order, first, factors, sources, blocks, own, carry, aux_count)

    carry = None
    blocks = last_block = [[(0, own)]]
    if cut_up:
        low, high, end = marks[1:]
        for k, cut in enumerate(later[0]):
            exchange(far[k], low, high, cut)
        parts = [(n * low // 4, (n + 1) * low // 4) for n in range(4)]
        middle = (low + high) // 2
        last_block = [[(high, end)]]
        (carry,) = call([xt], [[part] for part in parts])
        cuts, carry = lax.optimization_barrier((later[1], carry))
        for k, cut in zip(far, cuts):
            exchange(k, high, end, cut)
        (carry,) = call([xt], [[(low, middle)], [(middle, high)]], carry)
        blocks = []
        for start in range(0, own, 4 * unit):
            points = [start] + [m for m in marks if start < m < start + 4 * unit] + [start + 4 * unit]
            blocks.append(list(zip(points, points[1:])))

    def sum_terms(partial):
        return lax.all_to_all(partial.reshape(count, share, width), EVERY, 0, 0, tiled=True)

    (partial,) = call([xt], last_block, carry, na)
    copies = share_copies(sum_terms(partial))
    first = [lax.all_to_all(copies, EVERY, 0, 0, tiled=True), trial, state[:, occ:], occ_energy[:, None]]
    partial, trial_own, before = call(first, blocks, None, na)
    ratios, sums = share_sums(sum_terms(partial), trial_own, gap_own)
    sums = lax.all_to_all(sums, EVERY, 0, 0, tiled=True)
    fresh, shifts = step_share(ratios, sums, before, total)
    return (fresh.T[None], shifts.T)


def solution(mesh):
    placed = (P("aux", "vir", None), P(None, "vir", "aux"), P(), P("vir"))
    return jax.shard_map(
        local, mesh=mesh, in_specs=placed, out_specs=(P(None, "vir", "aux"), P()), check_vma=False
    )
```

```python
import functools

import jax
import jax.numpy as jnp
from jax import lax
from jax.experimental import pallas as pl
from jax.experimental.pallas import tpu as pltpu
from jax.sharding import PartitionSpec as P

EVERY = ("aux", "vir")


def diagonal(occ):
    rows = lax.broadcasted_iota(jnp.int32, (occ, occ), 0)
    return rows == lax.broadcasted_iota(jnp.int32, (occ, occ), 1)


def coulomb_and_exchange(pair, eye):
    density = jnp.sum(jnp.where(eye, pair, 0.0), keepdims=True)
    density = density.astype(jnp.bfloat16).astype(jnp.float32)
    pair = pair.astype(jnp.bfloat16).astype(jnp.float32)
    return (jnp.where(eye, 2.0 * density, 0.0) - pair).astype(jnp.bfloat16)


def side_by_side(blocks, count):
    return jnp.concatenate([blocks[q] for q in range(count)], axis=1)


def five_sums(trial, gap, coupling):
    rounded = trial.astype(jnp.bfloat16).astype(jnp.float32)
    image = gap * rounded + coupling
    scaled_trial = trial / gap
    scaled_diff = trial - image / gap

    def total(values):
        return jnp.sum(values, keepdims=True)

    sums = (
        total(trial * image),
        total(trial * trial),
        total(scaled_diff * scaled_diff),
        total(scaled_diff * scaled_trial),
        total(scaled_trial * scaled_trial),
    )
    return scaled_diff, scaled_trial, sums


def finish(scaled_diff, scaled_trial, sums, count):
    cross_sum, self_sum, diff_sum, mixed_sum, scaled_sum = sums
    shift = cross_sum / self_sum
    mean_square = (diff_sum + 2.0 * shift * mixed_sum + shift * shift * scaled_sum) / count
    return (scaled_diff + shift * scaled_trial) * lax.rsqrt(mean_square + 1e-06), shift


def contract_body(nv, blocks, size, own, carried, stepping, total, order_ref, *refs):
    first_refs, refs = refs[: 4 if stepping else 1], refs[4 if stepping else 1 :]
    carry_ref, f_refs = (refs[0], refs[1:]) if carried else (None, refs)
    f_count = 1 + max(at for block in blocks for _, _, places in block for at, _ in places)
    f_refs, refs = f_refs[:f_count], f_refs[f_count:]
    out_refs, (acc_ref, xt_ref, held, sems) = refs[:-4], refs[-4:]
    out_ref = out_refs[0]
    width, occ = held.shape[3:]
    near_start = order_ref[nv] * own

    for at, block in enumerate(blocks):
        for k in range(nv):
            into_at = 0
            for low, high, places in block:
                array, offset = places[k]
                start = near_start + low if k == 0 else offset
                count = high - low
                pltpu.make_async_copy(
                    f_refs[array].at[pl.ds(start, count)],
                    held.at[at, k, pl.ds(into_at, count)],
                    sems.at[at, k],
                ).start()
                into_at += count

    acc_ref[...] = carry_ref[...] if carried else jnp.zeros_like(acc_ref)
    if stepping:
        shares_ref, trial_ref, vir_ref, occ_ref = first_refs
        own_ref = out_refs[1]
        share = own_ref.shape[0] - 1
        coupling = jnp.concatenate(
            [
                shares_ref[r * nv + order_ref[k]].astype(jnp.float32)
                for k in range(nv)
                for r in range(occ // share)
            ],
            axis=0,
        )
        gap = jnp.concatenate([vir_ref[k] - occ_ref[...] for k in range(nv)], axis=0)
        diff, scaled, sums = five_sums(trial_ref[...].reshape(nv * occ, width), gap, coupling)
        fresh, shift = finish(diff, scaled, sums, total)
        own_ref[share:, :] = jnp.broadcast_to(shift, (1, width))
        for k in range(nv):
            rows = fresh[k * occ : (k + 1) * occ]
            xt_ref[:, k * width : (k + 1) * width] = rows.astype(jnp.bfloat16)
        mine = fresh[:share]
        for r in range(1, occ // share):
            rows = fresh[r * share : (r + 1) * share]
            mine = jnp.where(order_ref[nv + 1] == r, rows, mine)
        own_ref[:share, :] = mine
    else:
        for k in range(nv):
            xt_ref[:, k * width : (k + 1) * width] = first_refs[0][k]
    eye = lax.broadcasted_iota(jnp.int32, (occ, occ), 0) == lax.broadcasted_iota(
        jnp.int32, (occ, occ), 1
    )

    def work(at, _):
        for k in range(nv):
            pltpu.make_async_copy(held.at[at, k], held.at[at, k], sems.at[at, k]).wait()
        tall = jnp.concatenate(
            [
                jnp.concatenate([held[at, k, q] for q in range(size)], axis=1)
                for k in range(nv)
            ],
            axis=0,
        )
        pairs = jnp.dot(xt_ref[...], tall, preferred_element_type=jnp.float32)
        mixes = []
        for q in range(size):
            pair = pairs[:, q * occ : (q + 1) * occ]
            density = jnp.sum(jnp.where(eye, pair, 0.0), keepdims=True)
            density = density.astype(jnp.bfloat16).astype(jnp.float32)
            pair = pair.astype(jnp.bfloat16).astype(jnp.float32)
            mixes.append((jnp.where(eye, 2.0 * density, 0.0) - pair).astype(jnp.bfloat16))
        mix = jnp.concatenate(mixes, axis=0)
        acc_ref[...] += jnp.dot(tall, mix, preferred_element_type=jnp.float32)
        return _

    lax.fori_loop(0, len(blocks), work, 0)
    if len(out_ref.shape) == 2:
        out_ref[...] = acc_ref[...]
        return
    share = out_ref.shape[2]
    for k in range(nv):
        turned = acc_ref[k * width : (k + 1) * width, :].T
        for r in range(occ // share):
            out_ref[r, order_ref[k]] = turned[r * share : (r + 1) * share, :].astype(out_ref.dtype)


def contract(order, first, factors, sources, blocks, own, carry=None, aux_count=None):
    p_count, width, occ = factors.shape
    nv = p_count // own
    carried, stepping = carry is not None, len(first) > 1
    size = sum(high - low for low, high in blocks[0])
    arrays, placed = [factors], []
    for block in blocks:
        placed.append([])
        for low, high in block:
            places = [(0, 0)]
            for k in range(1, nv):
                start, array = next((a, x) for a, b, x in sources[k] if a <= low and high <= b)
                at = next((n for n, x in enumerate(arrays) if x is array), len(arrays))
                if at == len(arrays):
                    arrays.append(array)
                places.append((at, low - start))
            placed[-1].append((low, high, places))
    if aux_count is None:
        out = [jax.ShapeDtypeStruct((nv * width, occ), jnp.float32)]
    else:
        out = [jax.ShapeDtypeStruct((aux_count, nv, occ // aux_count, width), jnp.bfloat16)]
    if stepping:
        out.append(jax.ShapeDtypeStruct((occ // aux_count + 1, width), jnp.float32))
    in_vmem, in_hbm = pl.BlockSpec(memory_space=pltpu.VMEM), pl.BlockSpec(memory_space=pltpu.HBM)
    body = functools.partial(
        contract_body, nv, placed, size, own, carried, stepping, nv * width * occ
    )
    return pl.pallas_call(
        body,
        in_specs=[pl.BlockSpec(memory_space=pltpu.SMEM)]
        + [in_vmem] * (len(first) + carried)
        + [in_hbm] * len(arrays),
        out_specs=[in_vmem] * len(out),
        out_shape=out,
        scratch_shapes=[
            pltpu.VMEM((nv * width, occ), jnp.float32),
            pltpu.VMEM((occ, nv * width), jnp.bfloat16),
            pltpu.VMEM((len(blocks), nv, size, width, occ), jnp.bfloat16),
            pltpu.SemaphoreType.DMA((len(blocks), nv)),
        ],
        compiler_params=pltpu.CompilerParams(vmem_limit_bytes=46 * 2**20),
        cost_estimate=pl.CostEstimate(flops=0, bytes_accessed=0, transcendentals=0),
    )(order, *first, *([carry] if carried else []), *arrays)


def share_sums(terms, trial, gap):
    count = terms.shape[0]

    def body(terms_ref, trial_ref, gap_ref, ratios_ref, sums_ref):
        coupling = jnp.sum(terms_ref[...].astype(jnp.float32), axis=0)
        share = gap_ref.shape[0]
        diff, scaled, sums = five_sums(trial_ref[:share, :], gap_ref[...], coupling)
        ratios_ref[0] = diff
        ratios_ref[1] = scaled
        ratios_ref[2] = jnp.broadcast_to(trial_ref[share:, :], diff.shape)
        lane = lax.broadcasted_iota(jnp.int32, (1, 128), 1)
        row = jnp.zeros((1, 128), jnp.float32)
        for at, value in enumerate(sums):
            row = jnp.where(lane == at, value, row)
        sums_ref[...] = jnp.broadcast_to(row[None], sums_ref.shape)

    ratios = jax.ShapeDtypeStruct((3, *gap.shape), jnp.float32)
    return pl.pallas_call(
        body,
        out_shape=(ratios, jax.ShapeDtypeStruct((count, 1, 128), jnp.float32)),
        compiler_params=pltpu.CompilerParams(vmem_limit_bytes=24 * 2**20),
    )(terms, trial, gap)


def step_share(ratios, all_sums, total):
    def body(ratios_ref, sums_ref, next_ref, shifts_ref):
        row = jnp.sum(sums_ref[...], axis=0)
        fresh, shift = finish(
            ratios_ref[0], ratios_ref[1], [row[:, at : at + 1] for at in range(5)], total
        )
        next_ref[...] = fresh
        shifts_ref[...] = jnp.concatenate([ratios_ref[2, :1, :1], shift], axis=1)

    return pl.pallas_call(
        body,
        out_shape=(
            jax.ShapeDtypeStruct(ratios.shape[1:], jnp.float32),
            jax.ShapeDtypeStruct((1, 2), jnp.float32),
        ),
    )(ratios, all_sums)


def share_copies(terms):
    def body(terms_ref, copies_ref):
        coupling = jnp.sum(terms_ref[...].astype(jnp.float32), axis=0).astype(jnp.bfloat16)
        copies_ref[...] = jnp.broadcast_to(coupling[None], copies_ref.shape)

    return pl.pallas_call(body, out_shape=jax.ShapeDtypeStruct(terms.shape, jnp.bfloat16))(terms)


def cut_out(whole, start, count):
    parts = 4
    rows = count // parts

    def body(start_ref, whole_ref, out_ref, sems):
        copies = []
        for n in range(parts):
            place = pl.ds(start_ref[0] + n * rows, rows)
            copies.append(
                pltpu.make_async_copy(whole_ref.at[place], out_ref.at[pl.ds(n * rows, rows)], sems.at[n])
            )
        for copy in copies:
            copy.start()
        for copy in copies:
            copy.wait()

    return pl.pallas_call(
        body,
        in_specs=[pl.BlockSpec(memory_space=pltpu.SMEM), pl.BlockSpec(memory_space=pltpu.HBM)],
        out_specs=pl.BlockSpec(memory_space=pltpu.VMEM),
        out_shape=jax.ShapeDtypeStruct((count, *whole.shape[1:]), whole.dtype),
        scratch_shapes=[pltpu.SemaphoreType.DMA((parts,))],
        compiler_params=pltpu.CompilerParams(vmem_limit_bytes=46 * 2**20),
    )(start.astype(jnp.int32)[None], whole)


def spread(share, count, axes=EVERY):
    copies = jnp.broadcast_to(share[None], (count,) + share.shape)
    return lax.all_to_all(copies, axes, 0, 0, tiled=True)


def local(factors, trials, occ_energy, vir_energy):
    na, nv = lax.axis_size("aux"), lax.axis_size("vir")
    count = na * nv
    aux_at, vir_at = lax.axis_index("aux"), lax.axis_index("vir")
    p_count, width, occ = factors.shape
    own = p_count // nv
    share = occ // na
    total = occ * width * nv
    paired = nv & (nv - 1) == 0

    def partner(at, k):
        return at ^ k if paired else (at + k) % nv

    def source(at, k):
        return at ^ k if paired else (at - k) % nv

    def send(value, k):
        return lax.ppermute(value, "vir", [(one, partner(one, k)) for one in range(nv)])

    order = [source(vir_at, k) for k in range(nv)] + [vir_at, aux_at]
    order = jnp.stack(order).astype(jnp.int32)

    unit = own // 16
    cut_up = unit >= 4 and own % 16 == 0
    sources = {k: [] for k in range(1, nv)}

    def piece(k, low, high, whole=factors):
        return lax.dynamic_slice_in_dim(whole, partner(vir_at, k) * own + low, high - low, 0)

    def exchange(k, low, high, part):
        sources[k].append((low, high, send(part, k)))

    def after_newest(k, *values):
        low, high, array = sources[k][-1]
        *values, array = lax.optimization_barrier((*values, array))
        sources[k][-1] = (low, high, array)
        return values

    marks = [0, own]
    if cut_up:
        marks = [0, 9 * unit, 15 * unit, own]
    far = [k for k in range(nv) if k > 1] + [1]
    later_factors = factors
    for n, k in enumerate(far):
        if cut_up and n == 0:
            cut = cut_out(factors, partner(vir_at, k) * own, marks[1])
        else:
            cut = piece(k, *marks[:2], later_factors)
        if cut_up and n == 0:
            later_factors, cut = lax.optimization_barrier((factors, cut))
        exchange(k, *marks[:2], cut)
    if cut_up:
        later = [[piece(k, low, high, later_factors) for k in far] for low, high in zip(marks[1:], marks[2:])]
        later, trials = lax.optimization_barrier((later, *after_newest(2, trials)))

    gathered = spread(trials[0].T, na, "aux").reshape(occ, width)
    gathered = jnp.concatenate([gathered, vir_energy[None]], axis=0)
    if paired:
        state = {0: gathered}
        bit = nv // 2
        while bit:
            names = sorted(state)
            came = send(jnp.stack([state[k] for k in names]), bit)
            state.update({k ^ bit: came[at] for at, k in enumerate(names)})
            bit //= 2
    else:
        state = {k: send(gathered, k) if k else gathered for k in range(nv)}
    state = jnp.stack([state[k] for k in range(nv)])
    trial = state[:, :occ]
    gap_own = vir_energy[None, :] - lax.dynamic_slice_in_dim(occ_energy, aux_at * share, share)[:, None]
    xt = trial.astype(jnp.bfloat16)

    def call(first, blocks, carry=None, aux_count=None):
        return contract(order, first, factors, sources, blocks, own, carry, aux_count)

    carry = None
    blocks = last_block = [[(0, own)]]
    if cut_up:
        low, high, end = marks[1:]
        for k, cut in enumerate(later[0]):
            exchange(far[k], low, high, cut)
        parts = [(n * low // 4, (n + 1) * low // 4) for n in range(4)]
        middle = (low + high) // 2
        last_block = [[(high, end)]]
        (carry,) = call([xt], [[part] for part in parts])
        cuts, carry = after_newest(2, later[1], carry)
        for k, cut in zip(far, cuts):
            exchange(k, high, end, cut)
        (carry,) = call([xt], [[(low, middle)], [(middle, high)]], carry)
        blocks = []
        for start in range(0, own, 4 * unit):
            points = [start] + [m for m in marks if start < m < start + 4 * unit] + [start + 4 * unit]
            blocks.append(list(zip(points, points[1:])))

    def sum_terms(partial):
        return lax.all_to_all(partial.reshape(count, share, width), EVERY, 0, 0, tiled=True)

    (partial,) = call([xt], last_block, carry, na)
    copies = share_copies(sum_terms(partial))
    first = [lax.all_to_all(copies, EVERY, 0, 0, tiled=True), trial, state[:, occ:], occ_energy[:, None]]
    partial, trial_own = call(first, blocks, None, na)
    ratios, sums = share_sums(sum_terms(partial), trial_own, gap_own)
    sums = lax.all_to_all(sums, EVERY, 0, 0, tiled=True)
    fresh, shifts = step_share(ratios, sums, total)
    return (fresh.T[None], shifts.T)


def solution(mesh):
    placed = (P("aux", "vir", None), P(None, "vir", "aux"), P(), P("vir"))
    return jax.shard_map(
        local, mesh=mesh, in_specs=placed, out_specs=(P(None, "vir", "aux"), P()), check_vma=False
    )
```

```python
import functools

import jax
import jax.numpy as jnp
from jax import lax
from jax.experimental import pallas as pl
from jax.experimental.pallas import tpu as pltpu
from jax.sharding import PartitionSpec as P

EVERY = ("aux", "vir")


def diagonal(occ):
    rows = lax.broadcasted_iota(jnp.int32, (occ, occ), 0)
    return rows == lax.broadcasted_iota(jnp.int32, (occ, occ), 1)


def coulomb_and_exchange(pair, eye):
    density = jnp.sum(jnp.where(eye, pair, 0.0), keepdims=True)
    density = density.astype(jnp.bfloat16).astype(jnp.float32)
    pair = pair.astype(jnp.bfloat16).astype(jnp.float32)
    return (jnp.where(eye, 2.0 * density, 0.0) - pair).astype(jnp.bfloat16)


def side_by_side(blocks, count):
    return jnp.concatenate([blocks[q] for q in range(count)], axis=1)


def five_sums(trial, gap, coupling):
    rounded = trial.astype(jnp.bfloat16).astype(jnp.float32)
    image = gap * rounded + coupling
    scaled_trial = trial / gap
    scaled_diff = trial - image / gap

    def total(values):
        return jnp.sum(values, keepdims=True)

    sums = (
        total(trial * image),
        total(trial * trial),
        total(scaled_diff * scaled_diff),
        total(scaled_diff * scaled_trial),
        total(scaled_trial * scaled_trial),
    )
    return scaled_diff, scaled_trial, sums


def finish(scaled_diff, scaled_trial, sums, count):
    cross_sum, self_sum, diff_sum, mixed_sum, scaled_sum = sums
    shift = cross_sum / self_sum
    mean_square = (diff_sum + 2.0 * shift * mixed_sum + shift * shift * scaled_sum) / count
    return (scaled_diff + shift * scaled_trial) * lax.rsqrt(mean_square + 1e-06), shift


def contract_body(nv, blocks, size, own, carried, stepping, total, order_ref, *refs):
    first_refs, refs = refs[: 4 if stepping else 1], refs[4 if stepping else 1 :]
    carry_ref, f_refs = (refs[0], refs[1:]) if carried else (None, refs)
    f_count = 1 + max(at for block in blocks for _, _, places in block for at, _ in places)
    f_refs, refs = f_refs[:f_count], f_refs[f_count:]
    out_refs, (acc_ref, xt_ref, held, sems) = refs[:-4], refs[-4:]
    out_ref = out_refs[0]
    width, occ = held.shape[3:]
    near_start = order_ref[nv] * own

    for at, block in enumerate(blocks):
        for k in range(nv):
            into_at = 0
            for low, high, places in block:
                array, offset = places[k]
                start = near_start + low if k == 0 else offset
                count = high - low
                pltpu.make_async_copy(
                    f_refs[array].at[pl.ds(start, count)],
                    held.at[at, k, pl.ds(into_at, count)],
                    sems.at[at, k],
                ).start()
                into_at += count

    acc_ref[...] = carry_ref[...] if carried else jnp.zeros_like(acc_ref)
    if stepping:
        shares_ref, trial_ref, vir_ref, occ_ref = first_refs
        own_ref = out_refs[1]
        share = own_ref.shape[0] - 1
        coupling = jnp.concatenate(
            [
                shares_ref[r * nv + order_ref[k]].astype(jnp.float32)
                for k in range(nv)
                for r in range(occ // share)
            ],
            axis=0,
        )
        gap = jnp.concatenate([vir_ref[k] - occ_ref[...] for k in range(nv)], axis=0)
        diff, scaled, sums = five_sums(trial_ref[...].reshape(nv * occ, width), gap, coupling)
        fresh, shift = finish(diff, scaled, sums, total)
        own_ref[share:, :] = jnp.broadcast_to(shift, (1, width))
        for k in range(nv):
            rows = fresh[k * occ : (k + 1) * occ]
            xt_ref[:, k * width : (k + 1) * width] = rows.astype(jnp.bfloat16)
        mine = fresh[:share]
        for r in range(1, occ // share):
            rows = fresh[r * share : (r + 1) * share]
            mine = jnp.where(order_ref[nv + 1] == r, rows, mine)
        own_ref[:share, :] = mine
    else:
        for k in range(nv):
            xt_ref[:, k * width : (k + 1) * width] = first_refs[0][k]
    eye = lax.broadcasted_iota(jnp.int32, (occ, occ), 0) == lax.broadcasted_iota(
        jnp.int32, (occ, occ), 1
    )

    def work(at, _):
        for k in range(nv):
            pltpu.make_async_copy(held.at[at, k], held.at[at, k], sems.at[at, k]).wait()
        tall = jnp.concatenate(
            [
                jnp.concatenate([held[at, k, q] for q in range(size)], axis=1)
                for k in range(nv)
            ],
            axis=0,
        )
        pairs = jnp.dot(xt_ref[...], tall, preferred_element_type=jnp.float32)
        mixes = []
        for q in range(size):
            pair = pairs[:, q * occ : (q + 1) * occ]
            density = jnp.sum(jnp.where(eye, pair, 0.0), keepdims=True)
            density = density.astype(jnp.bfloat16).astype(jnp.float32)
            pair = pair.astype(jnp.bfloat16).astype(jnp.float32)
            mixes.append((jnp.where(eye, 2.0 * density, 0.0) - pair).astype(jnp.bfloat16))
        mix = jnp.concatenate(mixes, axis=0)
        acc_ref[...] += jnp.dot(tall, mix, preferred_element_type=jnp.float32)
        return _

    lax.fori_loop(0, len(blocks), work, 0)
    if len(out_ref.shape) == 2:
        out_ref[...] = acc_ref[...]
        return
    share = out_ref.shape[2]
    for k in range(nv):
        turned = acc_ref[k * width : (k + 1) * width, :].T
        for r in range(occ // share):
            out_ref[r, order_ref[k]] = turned[r * share : (r + 1) * share, :].astype(out_ref.dtype)


def contract(order, first, factors, sources, blocks, own, carry=None, aux_count=None):
    p_count, width, occ = factors.shape
    nv = p_count // own
    carried, stepping = carry is not None, len(first) > 1
    size = sum(high - low for low, high in blocks[0])
    arrays, placed = [factors], []
    for block in blocks:
        placed.append([])
        for low, high in block:
            places = [(0, 0)]
            for k in range(1, nv):
                start, array = next((a, x) for a, b, x in sources[k] if a <= low and high <= b)
                at = next((n for n, x in enumerate(arrays) if x is array), len(arrays))
                if at == len(arrays):
                    arrays.append(array)
                places.append((at, low - start))
            placed[-1].append((low, high, places))
    if aux_count is None:
        out = [jax.ShapeDtypeStruct((nv * width, occ), jnp.float32)]
    else:
        out = [jax.ShapeDtypeStruct((aux_count, nv, occ // aux_count, width), jnp.bfloat16)]
    if stepping:
        out.append(jax.ShapeDtypeStruct((occ // aux_count + 1, width), jnp.float32))
    in_vmem, in_hbm = pl.BlockSpec(memory_space=pltpu.VMEM), pl.BlockSpec(memory_space=pltpu.HBM)
    body = functools.partial(
        contract_body, nv, placed, size, own, carried, stepping, nv * width * occ
    )
    return pl.pallas_call(
        body,
        in_specs=[pl.BlockSpec(memory_space=pltpu.SMEM)]
        + [in_vmem] * (len(first) + carried)
        + [in_hbm] * len(arrays),
        out_specs=[in_vmem] * len(out),
        out_shape=out,
        scratch_shapes=[
            pltpu.VMEM((nv * width, occ), jnp.float32),
            pltpu.VMEM((occ, nv * width), jnp.bfloat16),
            pltpu.VMEM((len(blocks), nv, size, width, occ), jnp.bfloat16),
            pltpu.SemaphoreType.DMA((len(blocks), nv)),
        ],
        compiler_params=pltpu.CompilerParams(vmem_limit_bytes=46 * 2**20),
        cost_estimate=pl.CostEstimate(flops=0, bytes_accessed=0, transcendentals=0),
    )(order, *first, *([carry] if carried else []), *arrays)


def share_sums(terms, trial, gap):
    count = terms.shape[0]

    def body(terms_ref, trial_ref, gap_ref, ratios_ref, sums_ref):
        coupling = jnp.sum(terms_ref[...].astype(jnp.float32), axis=0)
        share = gap_ref.shape[0]
        diff, scaled, sums = five_sums(trial_ref[:share, :], gap_ref[...], coupling)
        ratios_ref[0] = diff
        ratios_ref[1] = scaled
        ratios_ref[2] = jnp.broadcast_to(trial_ref[share:, :], diff.shape)
        lane = lax.broadcasted_iota(jnp.int32, (1, 128), 1)
        row = jnp.zeros((1, 128), jnp.float32)
        for at, value in enumerate(sums):
            row = jnp.where(lane == at, value, row)
        sums_ref[...] = jnp.broadcast_to(row[None], sums_ref.shape)

    ratios = jax.ShapeDtypeStruct((3, *gap.shape), jnp.float32)
    return pl.pallas_call(
        body,
        out_shape=(ratios, jax.ShapeDtypeStruct((count, 1, 128), jnp.float32)),
        compiler_params=pltpu.CompilerParams(vmem_limit_bytes=24 * 2**20),
    )(terms, trial, gap)


def step_share(ratios, all_sums, total):
    def body(ratios_ref, sums_ref, next_ref, shifts_ref):
        row = jnp.sum(sums_ref[...], axis=0)
        fresh, shift = finish(
            ratios_ref[0], ratios_ref[1], [row[:, at : at + 1] for at in range(5)], total
        )
        next_ref[...] = fresh
        shifts_ref[...] = jnp.concatenate([ratios_ref[2, :1, :1], shift], axis=1)

    return pl.pallas_call(
        body,
        out_shape=(
            jax.ShapeDtypeStruct(ratios.shape[1:], jnp.float32),
            jax.ShapeDtypeStruct((1, 2), jnp.float32),
        ),
    )(ratios, all_sums)


def share_copies(terms):
    def body(terms_ref, copies_ref):
        coupling = jnp.sum(terms_ref[...].astype(jnp.float32), axis=0).astype(jnp.bfloat16)
        copies_ref[...] = jnp.broadcast_to(coupling[None], copies_ref.shape)

    return pl.pallas_call(body, out_shape=jax.ShapeDtypeStruct(terms.shape, jnp.bfloat16))(terms)


def cut_out(whole, start, count):
    parts = next(n for n in (12, 9, 8, 4, 2, 1) if count % n == 0)
    rows = count // parts

    def body(start_ref, whole_ref, out_ref, sems):
        copies = []
        for n in range(parts):
            place = pl.ds(start_ref[0] + n * rows, rows)
            copies.append(
                pltpu.make_async_copy(whole_ref.at[place], out_ref.at[pl.ds(n * rows, rows)], sems.at[n])
            )
        for copy in copies:
            copy.start()
        for copy in copies:
            copy.wait()

    return pl.pallas_call(
        body,
        in_specs=[pl.BlockSpec(memory_space=pltpu.SMEM), pl.BlockSpec(memory_space=pltpu.HBM)],
        out_specs=pl.BlockSpec(memory_space=pltpu.VMEM),
        out_shape=jax.ShapeDtypeStruct((count, *whole.shape[1:]), whole.dtype),
        scratch_shapes=[pltpu.SemaphoreType.DMA((parts,))],
        compiler_params=pltpu.CompilerParams(vmem_limit_bytes=46 * 2**20),
    )(start.astype(jnp.int32)[None], whole)


def spread(share, count, axes=EVERY):
    copies = jnp.broadcast_to(share[None], (count,) + share.shape)
    return lax.all_to_all(copies, axes, 0, 0, tiled=True)


def local(factors, trials, occ_energy, vir_energy):
    na, nv = lax.axis_size("aux"), lax.axis_size("vir")
    count = na * nv
    aux_at, vir_at = lax.axis_index("aux"), lax.axis_index("vir")
    p_count, width, occ = factors.shape
    own = p_count // nv
    share = occ // na
    total = occ * width * nv
    paired = nv & (nv - 1) == 0

    def partner(at, k):
        return at ^ k if paired else (at + k) % nv

    def source(at, k):
        return at ^ k if paired else (at - k) % nv

    def send(value, k):
        return lax.ppermute(value, "vir", [(one, partner(one, k)) for one in range(nv)])

    order = [source(vir_at, k) for k in range(nv)] + [vir_at, aux_at]
    order = jnp.stack(order).astype(jnp.int32)

    unit = own // 16
    cut_up = unit >= 4 and own % 16 == 0
    sources = {k: [] for k in range(1, nv)}

    def piece(k, low, high, whole=factors):
        return lax.dynamic_slice_in_dim(whole, partner(vir_at, k) * own + low, high - low, 0)

    def exchange(k, low, high, part):
        sources[k].append((low, high, send(part, k)))

    def after_newest(k, *values):
        low, high, array = sources[k][-1]
        *values, array = lax.optimization_barrier((*values, array))
        sources[k][-1] = (low, high, array)
        return values

    marks = [0, own]
    if cut_up:
        marks = [0, 9 * unit, 15 * unit, own]
    far = [k for k in range(nv) if k > 1] + [1]
    later_factors = factors
    for n, k in enumerate(far):
        if cut_up and n == 0:
            cut = cut_out(factors, partner(vir_at, k) * own, marks[1])
        else:
            cut = piece(k, *marks[:2], later_factors)
        if cut_up and n == 0:
            later_factors, cut = lax.optimization_barrier((factors, cut))
        exchange(k, *marks[:2], cut)
    if cut_up:
        later = [[piece(k, low, high, later_factors) for k in far] for low, high in zip(marks[1:], marks[2:])]
        later, trials = lax.optimization_barrier((later, *after_newest(2, trials)))

    gathered = spread(trials[0].T, na, "aux").reshape(occ, width)
    gathered = jnp.concatenate([gathered, vir_energy[None]], axis=0)
    if paired:
        state = {0: gathered}
        bit = nv // 2
        while bit:
            names = sorted(state)
            came = send(jnp.stack([state[k] for k in names]), bit)
            state.update({k ^ bit: came[at] for at, k in enumerate(names)})
            bit //= 2
    else:
        state = {k: send(gathered, k) if k else gathered for k in range(nv)}
    state = jnp.stack([state[k] for k in range(nv)])
    trial = state[:, :occ]
    gap_own = vir_energy[None, :] - lax.dynamic_slice_in_dim(occ_energy, aux_at * share, share)[:, None]
    xt = trial.astype(jnp.bfloat16)

    def call(first, blocks, carry=None, aux_count=None):
        return contract(order, first, factors, sources, blocks, own, carry, aux_count)

    carry = None
    blocks = last_block = [[(0, own)]]
    if cut_up:
        low, high, end = marks[1:]
        for k, cut in enumerate(later[0]):
            exchange(far[k], low, high, cut)
        parts = [(n * low // 4, (n + 1) * low // 4) for n in range(4)]
        middle = (low + high) // 2
        last_block = [[(high, end)]]
        (carry,) = call([xt], [[part] for part in parts])
        cuts, carry = after_newest(2, later[1], carry)
        for k, cut in zip(far, cuts):
            exchange(k, high, end, cut)
        (carry,) = call([xt], [[(low, middle)], [(middle, high)]], carry)
        blocks = []
        for start in range(0, own, 4 * unit):
            points = [start] + [m for m in marks if start < m < start + 4 * unit] + [start + 4 * unit]
            blocks.append(list(zip(points, points[1:])))

    def sum_terms(partial):
        return lax.all_to_all(partial.reshape(count, share, width), EVERY, 0, 0, tiled=True)

    (partial,) = call([xt], last_block, carry, na)
    copies = share_copies(sum_terms(partial))
    first = [lax.all_to_all(copies, EVERY, 0, 0, tiled=True), trial, state[:, occ:], occ_energy[:, None]]
    partial, trial_own = call(first, blocks, None, na)
    ratios, sums = share_sums(sum_terms(partial), trial_own, gap_own)
    sums = lax.all_to_all(sums, EVERY, 0, 0, tiled=True)
    fresh, shifts = step_share(ratios, sums, total)
    return (fresh.T[None], shifts.T)


def solution(mesh):
    placed = (P("aux", "vir", None), P(None, "vir", "aux"), P(), P("vir"))
    return jax.shard_map(
        local, mesh=mesh, in_specs=placed, out_specs=(P(None, "vir", "aux"), P()), check_vma=False
    )
```

```python
import functools

import jax
import jax.numpy as jnp
from jax import lax
from jax.experimental import pallas as pl
from jax.experimental.pallas import tpu as pltpu
from jax.sharding import PartitionSpec as P

EVERY = ("aux", "vir")


def diagonal(occ):
    rows = lax.broadcasted_iota(jnp.int32, (occ, occ), 0)
    return rows == lax.broadcasted_iota(jnp.int32, (occ, occ), 1)


def coulomb_and_exchange(pair, eye):
    density = jnp.sum(jnp.where(eye, pair, 0.0), keepdims=True)
    density = density.astype(jnp.bfloat16).astype(jnp.float32)
    pair = pair.astype(jnp.bfloat16).astype(jnp.float32)
    return (jnp.where(eye, 2.0 * density, 0.0) - pair).astype(jnp.bfloat16)


def side_by_side(blocks, count):
    return jnp.concatenate([blocks[q] for q in range(count)], axis=1)


def five_sums(trial, gap, coupling):
    rounded = trial.astype(jnp.bfloat16).astype(jnp.float32)
    image = gap * rounded + coupling
    scaled_trial = trial / gap
    scaled_diff = trial - image / gap

    def total(values):
        return jnp.sum(values, keepdims=True)

    sums = (
        total(trial * image),
        total(trial * trial),
        total(scaled_diff * scaled_diff),
        total(scaled_diff * scaled_trial),
        total(scaled_trial * scaled_trial),
    )
    return scaled_diff, scaled_trial, sums


def finish(scaled_diff, scaled_trial, sums, count):
    cross_sum, self_sum, diff_sum, mixed_sum, scaled_sum = sums
    shift = cross_sum / self_sum
    mean_square = (diff_sum + 2.0 * shift * mixed_sum + shift * shift * scaled_sum) / count
    return (scaled_diff + shift * scaled_trial) * lax.rsqrt(mean_square + 1e-06), shift


def contract_body(nv, blocks, size, own, carried, stepping, total, order_ref, *refs):
    first_refs, refs = refs[: 4 if stepping else 1], refs[4 if stepping else 1 :]
    carry_ref, f_refs = (refs[0], refs[1:]) if carried else (None, refs)
    f_count = 1 + max(at for block in blocks for _, _, places in block for at, _ in places)
    f_refs, refs = f_refs[:f_count], f_refs[f_count:]
    out_refs, (acc_ref, xt_ref, held, sems) = refs[:-4], refs[-4:]
    out_ref = out_refs[0]
    width, occ = held.shape[3:]
    near_start = order_ref[nv] * own

    for at, block in enumerate(blocks):
        for k in range(nv):
            into_at = 0
            for low, high, places in block:
                array, offset = places[k]
                start = near_start + low if k == 0 else offset
                count = high - low
                pltpu.make_async_copy(
                    f_refs[array].at[pl.ds(start, count)],
                    held.at[at, k, pl.ds(into_at, count)],
                    sems.at[at, k],
                ).start()
                into_at += count

    acc_ref[...] = carry_ref[...] if carried else jnp.zeros_like(acc_ref)
    if stepping:
        shares_ref, trial_ref, vir_ref, occ_ref = first_refs
        own_ref = out_refs[1]
        share = own_ref.shape[0] - 1
        coupling = jnp.concatenate(
            [
                shares_ref[r * nv + order_ref[k]].astype(jnp.float32)
                for k in range(nv)
                for r in range(occ // share)
            ],
            axis=0,
        )
        gap = jnp.concatenate([vir_ref[k] - occ_ref[...] for k in range(nv)], axis=0)
        diff, scaled, sums = five_sums(trial_ref[...].reshape(nv * occ, width), gap, coupling)
        fresh, shift = finish(diff, scaled, sums, total)
        own_ref[share:, :] = jnp.broadcast_to(shift, (1, width))
        for k in range(nv):
            rows = fresh[k * occ : (k + 1) * occ]
            xt_ref[:, k * width : (k + 1) * width] = rows.astype(jnp.bfloat16)
        mine = fresh[:share]
        for r in range(1, occ // share):
            rows = fresh[r * share : (r + 1) * share]
            mine = jnp.where(order_ref[nv + 1] == r, rows, mine)
        own_ref[:share, :] = mine
    else:
        for k in range(nv):
            xt_ref[:, k * width : (k + 1) * width] = first_refs[0][k]
    eye = lax.broadcasted_iota(jnp.int32, (occ, occ), 0) == lax.broadcasted_iota(
        jnp.int32, (occ, occ), 1
    )

    def work(at, _):
        for k in range(nv):
            pltpu.make_async_copy(held.at[at, k], held.at[at, k], sems.at[at, k]).wait()
        tall = jnp.concatenate(
            [
                jnp.concatenate([held[at, k, q] for q in range(size)], axis=1)
                for k in range(nv)
            ],
            axis=0,
        )
        pairs = jnp.dot(xt_ref[...], tall, preferred_element_type=jnp.float32)
        mixes = []
        for q in range(size):
            pair = pairs[:, q * occ : (q + 1) * occ]
            density = jnp.sum(jnp.where(eye, pair, 0.0), keepdims=True)
            density = density.astype(jnp.bfloat16).astype(jnp.float32)
            pair = pair.astype(jnp.bfloat16).astype(jnp.float32)
            mixes.append((jnp.where(eye, 2.0 * density, 0.0) - pair).astype(jnp.bfloat16))
        mix = jnp.concatenate(mixes, axis=0)
        acc_ref[...] += jnp.dot(tall, mix, preferred_element_type=jnp.float32)
        return _

    lax.fori_loop(0, len(blocks), work, 0)
    if len(out_ref.shape) == 2:
        out_ref[...] = acc_ref[...]
        return
    share = out_ref.shape[2]
    for k in range(nv):
        turned = acc_ref[k * width : (k + 1) * width, :].T
        for r in range(occ // share):
            out_ref[r, order_ref[k]] = turned[r * share : (r + 1) * share, :].astype(out_ref.dtype)


def contract(order, first, factors, sources, blocks, own, carry=None, aux_count=None):
    p_count, width, occ = factors.shape
    nv = p_count // own
    carried, stepping = carry is not None, len(first) > 1
    size = sum(high - low for low, high in blocks[0])
    arrays, placed = [factors], []
    for block in blocks:
        placed.append([])
        for low, high in block:
            places = [(0, 0)]
            for k in range(1, nv):
                start, array = next((a, x) for a, b, x in sources[k] if a <= low and high <= b)
                at = next((n for n, x in enumerate(arrays) if x is array), len(arrays))
                if at == len(arrays):
                    arrays.append(array)
                places.append((at, low - start))
            placed[-1].append((low, high, places))
    if aux_count is None:
        out = [jax.ShapeDtypeStruct((nv * width, occ), jnp.float32)]
    else:
        out = [jax.ShapeDtypeStruct((aux_count, nv, occ // aux_count, width), jnp.bfloat16)]
    if stepping:
        out.append(jax.ShapeDtypeStruct((occ // aux_count + 1, width), jnp.float32))
    in_vmem, in_hbm = pl.BlockSpec(memory_space=pltpu.VMEM), pl.BlockSpec(memory_space=pltpu.HBM)
    body = functools.partial(
        contract_body, nv, placed, size, own, carried, stepping, nv * width * occ
    )
    return pl.pallas_call(
        body,
        in_specs=[pl.BlockSpec(memory_space=pltpu.SMEM)]
        + [in_vmem] * (len(first) + carried)
        + [in_hbm] * len(arrays),
        out_specs=[in_vmem] * len(out),
        out_shape=out,
        scratch_shapes=[
            pltpu.VMEM((nv * width, occ), jnp.float32),
            pltpu.VMEM((occ, nv * width), jnp.bfloat16),
            pltpu.VMEM((len(blocks), nv, size, width, occ), jnp.bfloat16),
            pltpu.SemaphoreType.DMA((len(blocks), nv)),
        ],
        compiler_params=pltpu.CompilerParams(vmem_limit_bytes=46 * 2**20),
        cost_estimate=pl.CostEstimate(flops=0, bytes_accessed=0, transcendentals=0),
    )(order, *first, *([carry] if carried else []), *arrays)


def share_sums(terms, trial, gap):
    count = terms.shape[0]

    def body(terms_ref, trial_ref, gap_ref, ratios_ref, sums_ref):
        coupling = jnp.sum(terms_ref[...].astype(jnp.float32), axis=0)
        share = gap_ref.shape[0]
        diff, scaled, sums = five_sums(trial_ref[:share, :], gap_ref[...], coupling)
        ratios_ref[0] = diff
        ratios_ref[1] = scaled
        ratios_ref[2] = jnp.broadcast_to(trial_ref[share:, :], diff.shape)
        lane = lax.broadcasted_iota(jnp.int32, (1, 128), 1)
        row = jnp.zeros((1, 128), jnp.float32)
        for at, value in enumerate(sums):
            row = jnp.where(lane == at, value, row)
        sums_ref[...] = jnp.broadcast_to(row[None], sums_ref.shape)

    ratios = jax.ShapeDtypeStruct((3, *gap.shape), jnp.float32)
    return pl.pallas_call(
        body,
        out_shape=(ratios, jax.ShapeDtypeStruct((count, 1, 128), jnp.float32)),
        compiler_params=pltpu.CompilerParams(vmem_limit_bytes=24 * 2**20),
    )(terms, trial, gap)


def step_share(ratios, all_sums, total):
    def body(ratios_ref, sums_ref, next_ref, shifts_ref):
        row = jnp.sum(sums_ref[...], axis=0)
        fresh, shift = finish(
            ratios_ref[0], ratios_ref[1], [row[:, at : at + 1] for at in range(5)], total
        )
        next_ref[...] = fresh
        shifts_ref[...] = jnp.concatenate([ratios_ref[2, :1, :1], shift], axis=1)

    return pl.pallas_call(
        body,
        out_shape=(
            jax.ShapeDtypeStruct(ratios.shape[1:], jnp.float32),
            jax.ShapeDtypeStruct((1, 2), jnp.float32),
        ),
    )(ratios, all_sums)


def share_copies(terms):
    def body(terms_ref, copies_ref):
        coupling = jnp.sum(terms_ref[...].astype(jnp.float32), axis=0).astype(jnp.bfloat16)
        copies_ref[...] = jnp.broadcast_to(coupling[None], copies_ref.shape)

    return pl.pallas_call(body, out_shape=jax.ShapeDtypeStruct(terms.shape, jnp.bfloat16))(terms)


def cut_out(whole, start, count):
    parts = 4
    rows = count // parts

    def body(start_ref, whole_ref, out_ref, sems):
        copies = []
        for n in range(parts):
            place = pl.ds(start_ref[0] + n * rows, rows)
            copies.append(
                pltpu.make_async_copy(whole_ref.at[place], out_ref.at[pl.ds(n * rows, rows)], sems.at[n])
            )
        for copy in copies:
            copy.start()
        for copy in copies:
            copy.wait()

    return pl.pallas_call(
        body,
        in_specs=[pl.BlockSpec(memory_space=pltpu.SMEM), pl.BlockSpec(memory_space=pltpu.HBM)],
        out_specs=pl.BlockSpec(memory_space=pltpu.VMEM),
        out_shape=jax.ShapeDtypeStruct((count, *whole.shape[1:]), whole.dtype),
        scratch_shapes=[pltpu.SemaphoreType.DMA((parts,))],
        compiler_params=pltpu.CompilerParams(vmem_limit_bytes=46 * 2**20),
    )(start.astype(jnp.int32)[None], whole)


def spread(share, count, axes=EVERY):
    copies = jnp.broadcast_to(share[None], (count,) + share.shape)
    return lax.all_to_all(copies, axes, 0, 0, tiled=True)


def local(factors, trials, occ_energy, vir_energy):
    na, nv = lax.axis_size("aux"), lax.axis_size("vir")
    count = na * nv
    aux_at, vir_at = lax.axis_index("aux"), lax.axis_index("vir")
    p_count, width, occ = factors.shape
    own = p_count // nv
    share = occ // na
    total = occ * width * nv
    paired = nv & (nv - 1) == 0

    def partner(at, k):
        return at ^ k if paired else (at + k) % nv

    def source(at, k):
        return at ^ k if paired else (at - k) % nv

    def send(value, k):
        return lax.ppermute(value, "vir", [(one, partner(one, k)) for one in range(nv)])

    order = [source(vir_at, k) for k in range(nv)] + [vir_at, aux_at]
    order = jnp.stack(order).astype(jnp.int32)

    unit = own // 16
    cut_up = unit >= 4 and own % 16 == 0
    sources = {k: [] for k in range(1, nv)}

    def piece(k, low, high, whole=factors):
        return lax.dynamic_slice_in_dim(whole, partner(vir_at, k) * own + low, high - low, 0)

    def exchange(k, low, high, part):
        sources[k].append((low, high, send(part, k)))

    def after_newest(k, *values):
        low, high, array = sources[k][-1]
        *values, array = lax.optimization_barrier((*values, array))
        sources[k][-1] = (low, high, array)
        return values

    marks = [0, own]
    if cut_up:
        marks = [0, 9 * unit, 15 * unit, own]
    far = [k for k in range(nv) if k > 1] + [1]
    later_factors = factors
    for n, k in enumerate(far):
        if cut_up and n == 0:
            cut = cut_out(factors, partner(vir_at, k) * own, marks[1])
        else:
            cut = piece(k, *marks[:2], later_factors)
        if cut_up and n == 0:
            later_factors, cut = lax.optimization_barrier((factors, cut))
        exchange(k, *marks[:2], cut)
    if cut_up:
        later = [[piece(k, low, high, later_factors) for k in far] for low, high in zip(marks[1:], marks[2:])]
        later, trials = lax.optimization_barrier((later, *after_newest(2, trials)))

    gathered = spread(trials[0].T, na, "aux").reshape(occ, width)
    gathered = jnp.concatenate([gathered, vir_energy[None]], axis=0)
    if paired:
        state = {0: gathered}
        bit = nv // 2
        while bit:
            names = sorted(state)
            came = send(jnp.stack([state[k] for k in names]), bit)
            state.update({k ^ bit: came[at] for at, k in enumerate(names)})
            bit //= 2
    else:
        state = {k: send(gathered, k) if k else gathered for k in range(nv)}
    state = jnp.stack([state[k] for k in range(nv)])
    trial = state[:, :occ]
    gap_own = vir_energy[None, :] - lax.dynamic_slice_in_dim(occ_energy, aux_at * share, share)[:, None]
    xt = trial.astype(jnp.bfloat16)

    def call(first, blocks, carry=None, aux_count=None):
        return contract(order, first, factors, sources, blocks, own, carry, aux_count)

    carry = None
    blocks = last_block = [[(0, own)]]
    if cut_up:
        low, high, end = marks[1:]
        for k, cut in enumerate(later[0]):
            exchange(far[k], low, high, cut)
        parts = [(n * low // 4, (n + 1) * low // 4) for n in range(4)]
        middle = (low + high) // 2
        last_block = [[(high, end)]]
        (carry,) = call([xt], [[part] for part in parts])
        cuts, carry = after_newest(2, later[1], carry)
        for k, cut in zip(far, cuts):
            exchange(k, high, end, cut)
        (carry,) = call([xt], [[(low, middle)], [(middle, high)]], carry)
        blocks = []
        for start in range(0, own, 8 * unit):
            stop = start + 8 * unit
            points = [start] + [m for m in marks if start < m < stop] + [stop]
            blocks.append(list(zip(points, points[1:])))

    def sum_terms(partial):
        return lax.all_to_all(partial.reshape(count, share, width), EVERY, 0, 0, tiled=True)

    (partial,) = call([xt], last_block, carry, na)
    copies = share_copies(sum_terms(partial))
    first = [lax.all_to_all(copies, EVERY, 0, 0, tiled=True), trial, state[:, occ:], occ_energy[:, None]]
    partial, trial_own = call(first, blocks, None, na)
    ratios, sums = share_sums(sum_terms(partial), trial_own, gap_own)
    sums = lax.all_to_all(sums, EVERY, 0, 0, tiled=True)
    fresh, shifts = step_share(ratios, sums, total)
    return (fresh.T[None], shifts.T)


def solution(mesh):
    placed = (P("aux", "vir", None), P(None, "vir", "aux"), P(), P("vir"))
    return jax.shard_map(
        local, mesh=mesh, in_specs=placed, out_specs=(P(None, "vir", "aux"), P()), check_vma=False
    )
```

```python
import functools

import jax
import jax.numpy as jnp
from jax import lax
from jax.experimental import pallas as pl
from jax.experimental.pallas import tpu as pltpu
from jax.sharding import PartitionSpec as P

EVERY = ("aux", "vir")


def diagonal(occ):
    rows = lax.broadcasted_iota(jnp.int32, (occ, occ), 0)
    return rows == lax.broadcasted_iota(jnp.int32, (occ, occ), 1)


def coulomb_and_exchange(pair, eye):
    density = jnp.sum(jnp.where(eye, pair, 0.0), keepdims=True)
    density = density.astype(jnp.bfloat16).astype(jnp.float32)
    pair = pair.astype(jnp.bfloat16).astype(jnp.float32)
    return (jnp.where(eye, 2.0 * density, 0.0) - pair).astype(jnp.bfloat16)


def side_by_side(blocks, count):
    return jnp.concatenate([blocks[q] for q in range(count)], axis=1)


def five_sums(trial, gap, coupling):
    rounded = trial.astype(jnp.bfloat16).astype(jnp.float32)
    image = gap * rounded + coupling
    scaled_trial = trial / gap
    scaled_diff = trial - image / gap

    def total(values):
        return jnp.sum(values, keepdims=True)

    sums = (
        total(trial * image),
        total(trial * trial),
        total(scaled_diff * scaled_diff),
        total(scaled_diff * scaled_trial),
        total(scaled_trial * scaled_trial),
    )
    return scaled_diff, scaled_trial, sums


def finish(scaled_diff, scaled_trial, sums, count):
    cross_sum, self_sum, diff_sum, mixed_sum, scaled_sum = sums
    shift = cross_sum / self_sum
    mean_square = (diff_sum + 2.0 * shift * mixed_sum + shift * shift * scaled_sum) / count
    return (scaled_diff + shift * scaled_trial) * lax.rsqrt(mean_square + 1e-06), shift


def contract_body(nv, blocks, size, own, carried, stepping, total, order_ref, *refs):
    first_refs, refs = refs[: 4 if stepping else 1], refs[4 if stepping else 1 :]
    carry_ref, f_refs = (refs[0], refs[1:]) if carried else (None, refs)
    f_count = 1 + max(at for block in blocks for _, _, places in block for at, _ in places)
    f_refs, refs = f_refs[:f_count], f_refs[f_count:]
    out_refs, (acc_ref, xt_ref, held, sems) = refs[:-4], refs[-4:]
    out_ref = out_refs[0]
    width, occ = held.shape[3:]
    near_start = order_ref[nv] * own

    for at, block in enumerate(blocks):
        for k in range(nv):
            into_at = 0
            for low, high, places in block:
                array, offset = places[k]
                start = near_start + low if k == 0 else offset
                count = high - low
                pltpu.make_async_copy(
                    f_refs[array].at[pl.ds(start, count)],
                    held.at[at, k, pl.ds(into_at, count)],
                    sems.at[at, k],
                ).start()
                into_at += count

    acc_ref[...] = carry_ref[...] if carried else jnp.zeros_like(acc_ref)
    if stepping:
        shares_ref, trial_ref, vir_ref, occ_ref = first_refs
        own_ref = out_refs[1]
        share = own_ref.shape[0] - 1
        coupling = jnp.concatenate(
            [
                shares_ref[r * nv + order_ref[k]].astype(jnp.float32)
                for k in range(nv)
                for r in range(occ // share)
            ],
            axis=0,
        )
        gap = jnp.concatenate([vir_ref[k] - occ_ref[...] for k in range(nv)], axis=0)
        diff, scaled, sums = five_sums(trial_ref[...].reshape(nv * occ, width), gap, coupling)
        fresh, shift = finish(diff, scaled, sums, total)
        own_ref[share:, :] = jnp.broadcast_to(shift, (1, width))
        for k in range(nv):
            rows = fresh[k * occ : (k + 1) * occ]
            xt_ref[:, k * width : (k + 1) * width] = rows.astype(jnp.bfloat16)
        mine = fresh[:share]
        for r in range(1, occ // share):
            rows = fresh[r * share : (r + 1) * share]
            mine = jnp.where(order_ref[nv + 1] == r, rows, mine)
        own_ref[:share, :] = mine
    else:
        for k in range(nv):
            xt_ref[:, k * width : (k + 1) * width] = first_refs[0][k]
    eye = lax.broadcasted_iota(jnp.int32, (occ, occ), 0) == lax.broadcasted_iota(
        jnp.int32, (occ, occ), 1
    )

    def work(at, _):
        for k in range(nv):
            pltpu.make_async_copy(held.at[at, k], held.at[at, k], sems.at[at, k]).wait()
        tall = jnp.concatenate(
            [
                jnp.concatenate([held[at, k, q] for q in range(size)], axis=1)
                for k in range(nv)
            ],
            axis=0,
        )
        pairs = jnp.dot(xt_ref[...], tall, preferred_element_type=jnp.float32)
        mixes = []
        for q in range(size):
            pair = pairs[:, q * occ : (q + 1) * occ]
            density = jnp.sum(jnp.where(eye, pair, 0.0), keepdims=True)
            density = density.astype(jnp.bfloat16).astype(jnp.float32)
            pair = pair.astype(jnp.bfloat16).astype(jnp.float32)
            mixes.append((jnp.where(eye, 2.0 * density, 0.0) - pair).astype(jnp.bfloat16))
        mix = jnp.concatenate(mixes, axis=0)
        acc_ref[...] += jnp.dot(tall, mix, preferred_element_type=jnp.float32)
        return _

    lax.fori_loop(0, len(blocks), work, 0)
    if len(out_ref.shape) == 2:
        out_ref[...] = acc_ref[...]
        return
    share = out_ref.shape[2]
    for k in range(nv):
        turned = acc_ref[k * width : (k + 1) * width, :].T
        for r in range(occ // share):
            out_ref[r, order_ref[k]] = turned[r * share : (r + 1) * share, :].astype(out_ref.dtype)


def contract(order, first, factors, sources, blocks, own, carry=None, aux_count=None):
    p_count, width, occ = factors.shape
    nv = p_count // own
    carried, stepping = carry is not None, len(first) > 1
    size = sum(high - low for low, high in blocks[0])
    arrays, placed = [factors], []
    for block in blocks:
        placed.append([])
        for low, high in block:
            places = [(0, 0)]
            for k in range(1, nv):
                start, array = next((a, x) for a, b, x in sources[k] if a <= low and high <= b)
                at = next((n for n, x in enumerate(arrays) if x is array), len(arrays))
                if at == len(arrays):
                    arrays.append(array)
                places.append((at, low - start))
            placed[-1].append((low, high, places))
    if aux_count is None:
        out = [jax.ShapeDtypeStruct((nv * width, occ), jnp.float32)]
    else:
        out = [jax.ShapeDtypeStruct((aux_count, nv, occ // aux_count, width), jnp.bfloat16)]
    if stepping:
        out.append(jax.ShapeDtypeStruct((occ // aux_count + 1, width), jnp.float32))
    in_vmem, in_hbm = pl.BlockSpec(memory_space=pltpu.VMEM), pl.BlockSpec(memory_space=pltpu.HBM)
    body = functools.partial(
        contract_body, nv, placed, size, own, carried, stepping, nv * width * occ
    )
    return pl.pallas_call(
        body,
        in_specs=[pl.BlockSpec(memory_space=pltpu.SMEM)]
        + [in_vmem] * (len(first) + carried)
        + [in_hbm] * len(arrays),
        out_specs=[in_vmem] * len(out),
        out_shape=out,
        scratch_shapes=[
            pltpu.VMEM((nv * width, occ), jnp.float32),
            pltpu.VMEM((occ, nv * width), jnp.bfloat16),
            pltpu.VMEM((len(blocks), nv, size, width, occ), jnp.bfloat16),
            pltpu.SemaphoreType.DMA((len(blocks), nv)),
        ],
        compiler_params=pltpu.CompilerParams(vmem_limit_bytes=46 * 2**20),
        cost_estimate=pl.CostEstimate(flops=0, bytes_accessed=0, transcendentals=0),
    )(order, *first, *([carry] if carried else []), *arrays)


def share_sums(terms, trial, gap):
    count = terms.shape[0]

    def body(terms_ref, trial_ref, gap_ref, ratios_ref, sums_ref):
        coupling = jnp.sum(terms_ref[...].astype(jnp.float32), axis=0)
        share = gap_ref.shape[0]
        diff, scaled, sums = five_sums(trial_ref[:share, :], gap_ref[...], coupling)
        ratios_ref[0] = diff
        ratios_ref[1] = scaled
        ratios_ref[2] = jnp.broadcast_to(trial_ref[share:, :], diff.shape)
        lane = lax.broadcasted_iota(jnp.int32, (1, 128), 1)
        row = jnp.zeros((1, 128), jnp.float32)
        for at, value in enumerate(sums):
            row = jnp.where(lane == at, value, row)
        sums_ref[...] = jnp.broadcast_to(row[None], sums_ref.shape)

    ratios = jax.ShapeDtypeStruct((3, *gap.shape), jnp.float32)
    return pl.pallas_call(
        body,
        out_shape=(ratios, jax.ShapeDtypeStruct((count, 1, 128), jnp.float32)),
        compiler_params=pltpu.CompilerParams(vmem_limit_bytes=24 * 2**20),
    )(terms, trial, gap)


def step_share(ratios, all_sums, total):
    def body(ratios_ref, sums_ref, next_ref, shifts_ref):
        row = jnp.sum(sums_ref[...], axis=0)
        fresh, shift = finish(
            ratios_ref[0], ratios_ref[1], [row[:, at : at + 1] for at in range(5)], total
        )
        next_ref[...] = fresh
        shifts_ref[...] = jnp.concatenate([ratios_ref[2, :1, :1], shift], axis=1)

    return pl.pallas_call(
        body,
        out_shape=(
            jax.ShapeDtypeStruct(ratios.shape[1:], jnp.float32),
            jax.ShapeDtypeStruct((1, 2), jnp.float32),
        ),
    )(ratios, all_sums)


def share_copies(terms):
    def body(terms_ref, copies_ref):
        coupling = jnp.sum(terms_ref[...].astype(jnp.float32), axis=0).astype(jnp.bfloat16)
        copies_ref[...] = jnp.broadcast_to(coupling[None], copies_ref.shape)

    return pl.pallas_call(body, out_shape=jax.ShapeDtypeStruct(terms.shape, jnp.bfloat16))(terms)


def cut_out(whole, start, count):
    parts = 4
    rows = count // parts

    def body(start_ref, whole_ref, out_ref, sems):
        copies = []
        for n in range(parts):
            place = pl.ds(start_ref[0] + n * rows, rows)
            copies.append(
                pltpu.make_async_copy(whole_ref.at[place], out_ref.at[pl.ds(n * rows, rows)], sems.at[n])
            )
        for copy in copies:
            copy.start()
        for copy in copies:
            copy.wait()

    return pl.pallas_call(
        body,
        in_specs=[pl.BlockSpec(memory_space=pltpu.SMEM), pl.BlockSpec(memory_space=pltpu.HBM)],
        out_specs=pl.BlockSpec(memory_space=pltpu.VMEM),
        out_shape=jax.ShapeDtypeStruct((count, *whole.shape[1:]), whole.dtype),
        scratch_shapes=[pltpu.SemaphoreType.DMA((parts,))],
        compiler_params=pltpu.CompilerParams(vmem_limit_bytes=46 * 2**20),
    )(start.astype(jnp.int32)[None], whole)


def spread(share, count, axes=EVERY):
    copies = jnp.broadcast_to(share[None], (count,) + share.shape)
    return lax.all_to_all(copies, axes, 0, 0, tiled=True)


def local(factors, trials, occ_energy, vir_energy):
    na, nv = lax.axis_size("aux"), lax.axis_size("vir")
    count = na * nv
    aux_at, vir_at = lax.axis_index("aux"), lax.axis_index("vir")
    p_count, width, occ = factors.shape
    own = p_count // nv
    share = occ // na
    total = occ * width * nv
    paired = nv & (nv - 1) == 0

    def partner(at, k):
        return at ^ k if paired else (at + k) % nv

    def source(at, k):
        return at ^ k if paired else (at - k) % nv

    def send(value, k):
        return lax.ppermute(value, "vir", [(one, partner(one, k)) for one in range(nv)])

    order = [source(vir_at, k) for k in range(nv)] + [vir_at, aux_at]
    order = jnp.stack(order).astype(jnp.int32)

    unit = own // 16
    cut_up = unit >= 4 and own % 16 == 0
    sources = {k: [] for k in range(1, nv)}

    def piece(k, low, high, whole=factors):
        return lax.dynamic_slice_in_dim(whole, partner(vir_at, k) * own + low, high - low, 0)

    def exchange(k, low, high, part):
        sources[k].append((low, high, send(part, k)))

    def after_newest(k, *values):
        low, high, array = sources[k][-1]
        *values, array = lax.optimization_barrier((*values, array))
        sources[k][-1] = (low, high, array)
        return values

    marks = [0, own]
    if cut_up:
        marks = [0, 9 * unit, 15 * unit, own]
    far = [k for k in range(nv) if k > 1] + [1]
    first = {k: marks[1] for k in far}
    if cut_up:
        first[2] = 6 * unit
    later_factors = factors
    for n, k in enumerate(far):
        if cut_up and n == 0:
            cut = cut_out(factors, partner(vir_at, k) * own, first[k])
        else:
            cut = piece(k, 0, first[k], later_factors)
        if cut_up and n == 0:
            later_factors, cut = lax.optimization_barrier((factors, cut))
        exchange(k, 0, first[k], cut)
    if cut_up:
        later = [[piece(k, first[k], marks[2], later_factors) for k in far]]
        later += [[piece(k, marks[2], own, later_factors) for k in far]]
        later, trials = lax.optimization_barrier((later, *after_newest(2, trials)))

    gathered = spread(trials[0].T, na, "aux").reshape(occ, width)
    gathered = jnp.concatenate([gathered, vir_energy[None]], axis=0)
    if paired:
        state = {0: gathered}
        bit = nv // 2
        while bit:
            names = sorted(state)
            came = send(jnp.stack([state[k] for k in names]), bit)
            state.update({k ^ bit: came[at] for at, k in enumerate(names)})
            bit //= 2
    else:
        state = {k: send(gathered, k) if k else gathered for k in range(nv)}
    state = jnp.stack([state[k] for k in range(nv)])
    trial = state[:, :occ]
    gap_own = vir_energy[None, :] - lax.dynamic_slice_in_dim(occ_energy, aux_at * share, share)[:, None]
    xt = trial.astype(jnp.bfloat16)

    def call(first, blocks, carry=None, aux_count=None):
        return contract(order, first, factors, sources, blocks, own, carry, aux_count)

    carry = None
    blocks = last_block = [[(0, own)]]
    if cut_up:
        low, (high, end) = first[2], marks[2:]
        for k, cut in zip(far, later[0]):
            exchange(k, first[k], high, cut)
        last_block = [[(high, end)]]
        (carry,) = call([xt], [[(0, low // 2)], [(low // 2, low)]])
        cuts, carry = after_newest(2, later[1], carry)
        for k, cut in zip(far, cuts):
            exchange(k, high, end, cut)
        parts = [(low + n * (high - low) // 3, low + (n + 1) * (high - low) // 3) for n in range(3)]
        (carry,) = call([xt], [[part] for part in parts], carry)
        marks.insert(1, low)
        blocks = []
        for start in range(0, own, 4 * unit):
            points = [start] + [m for m in marks if start < m < start + 4 * unit] + [start + 4 * unit]
            blocks.append(list(zip(points, points[1:])))

    def sum_terms(partial):
        return lax.all_to_all(partial.reshape(count, share, width), EVERY, 0, 0, tiled=True)

    (partial,) = call([xt], last_block, carry, na)
    copies = share_copies(sum_terms(partial))
    first = [lax.all_to_all(copies, EVERY, 0, 0, tiled=True), trial, state[:, occ:], occ_energy[:, None]]
    partial, trial_own = call(first, blocks, None, na)
    ratios, sums = share_sums(sum_terms(partial), trial_own, gap_own)
    sums = lax.all_to_all(sums, EVERY, 0, 0, tiled=True)
    fresh, shifts = step_share(ratios, sums, total)
    return (fresh.T[None], shifts.T)


def solution(mesh):
    placed = (P("aux", "vir", None), P(None, "vir", "aux"), P(), P("vir"))
    return jax.shard_map(
        local, mesh=mesh, in_specs=placed, out_specs=(P(None, "vir", "aux"), P()), check_vma=False
    )
```

```python
import functools

import jax
import jax.numpy as jnp
from jax import lax
from jax.experimental import pallas as pl
from jax.experimental.pallas import tpu as pltpu
from jax.sharding import PartitionSpec as P

EVERY = ("aux", "vir")


def diagonal(occ):
    rows = lax.broadcasted_iota(jnp.int32, (occ, occ), 0)
    return rows == lax.broadcasted_iota(jnp.int32, (occ, occ), 1)


def coulomb_and_exchange(pair, eye):
    density = jnp.sum(jnp.where(eye, pair, 0.0), keepdims=True)
    density = density.astype(jnp.bfloat16).astype(jnp.float32)
    pair = pair.astype(jnp.bfloat16).astype(jnp.float32)
    return (jnp.where(eye, 2.0 * density, 0.0) - pair).astype(jnp.bfloat16)


def side_by_side(blocks, count):
    return jnp.concatenate([blocks[q] for q in range(count)], axis=1)


def five_sums(trial, gap, coupling):
    rounded = trial.astype(jnp.bfloat16).astype(jnp.float32)
    image = gap * rounded + coupling
    scaled_trial = trial / gap
    scaled_diff = trial - image / gap

    def total(values):
        return jnp.sum(values, keepdims=True)

    sums = (
        total(trial * image),
        total(trial * trial),
        total(scaled_diff * scaled_diff),
        total(scaled_diff * scaled_trial),
        total(scaled_trial * scaled_trial),
    )
    return scaled_diff, scaled_trial, sums


def finish(scaled_diff, scaled_trial, sums, count):
    cross_sum, self_sum, diff_sum, mixed_sum, scaled_sum = sums
    shift = cross_sum / self_sum
    mean_square = (diff_sum + 2.0 * shift * mixed_sum + shift * shift * scaled_sum) / count
    return (scaled_diff + shift * scaled_trial) * lax.rsqrt(mean_square + 1e-06), shift


def contract_body(nv, blocks, size, own, carried, stepping, total, order_ref, *refs):
    first_refs, refs = refs[: 4 if stepping else 1], refs[4 if stepping else 1 :]
    carry_ref, f_refs = (refs[0], refs[1:]) if carried else (None, refs)
    f_count = 1 + max(at for block in blocks for _, _, places in block for at, _ in places)
    f_refs, refs = f_refs[:f_count], f_refs[f_count:]
    out_refs, (acc_ref, xt_ref, held, sems) = refs[:-4], refs[-4:]
    out_ref = out_refs[0]
    width, occ = held.shape[3:]
    near_start = order_ref[nv] * own

    for at, block in enumerate(blocks):
        for k in range(nv):
            into_at = 0
            for low, high, places in block:
                array, offset = places[k]
                start = near_start + low if k == 0 else offset
                count = high - low
                pltpu.make_async_copy(
                    f_refs[array].at[pl.ds(start, count)],
                    held.at[at, k, pl.ds(into_at, count)],
                    sems.at[at, k],
                ).start()
                into_at += count

    acc_ref[...] = carry_ref[...] if carried else jnp.zeros_like(acc_ref)
    if stepping:
        shares_ref, trial_ref, vir_ref, occ_ref = first_refs
        own_ref = out_refs[1]
        share = own_ref.shape[0] - 1
        coupling = jnp.concatenate(
            [
                shares_ref[r * nv + order_ref[k]].astype(jnp.float32)
                for k in range(nv)
                for r in range(occ // share)
            ],
            axis=0,
        )
        gap = jnp.concatenate([vir_ref[k] - occ_ref[...] for k in range(nv)], axis=0)
        diff, scaled, sums = five_sums(trial_ref[...].reshape(nv * occ, width), gap, coupling)
        fresh, shift = finish(diff, scaled, sums, total)
        own_ref[share:, :] = jnp.broadcast_to(shift, (1, width))
        for k in range(nv):
            rows = fresh[k * occ : (k + 1) * occ]
            xt_ref[:, k * width : (k + 1) * width] = rows.astype(jnp.bfloat16)
        mine = fresh[:share]
        for r in range(1, occ // share):
            rows = fresh[r * share : (r + 1) * share]
            mine = jnp.where(order_ref[nv + 1] == r, rows, mine)
        own_ref[:share, :] = mine
    else:
        for k in range(nv):
            xt_ref[:, k * width : (k + 1) * width] = first_refs[0][k]
    eye = lax.broadcasted_iota(jnp.int32, (occ, occ), 0) == lax.broadcasted_iota(
        jnp.int32, (occ, occ), 1
    )

    def work(at, _):
        for k in range(nv):
            pltpu.make_async_copy(held.at[at, k], held.at[at, k], sems.at[at, k]).wait()
        tall = jnp.concatenate(
            [
                jnp.concatenate([held[at, k, q] for q in range(size)], axis=1)
                for k in range(nv)
            ],
            axis=0,
        )
        pairs = jnp.dot(xt_ref[...], tall, preferred_element_type=jnp.float32)
        mixes = []
        for q in range(size):
            pair = pairs[:, q * occ : (q + 1) * occ]
            density = jnp.sum(jnp.where(eye, pair, 0.0), keepdims=True)
            density = density.astype(jnp.bfloat16).astype(jnp.float32)
            pair = pair.astype(jnp.bfloat16).astype(jnp.float32)
            mixes.append((jnp.where(eye, 2.0 * density, 0.0) - pair).astype(jnp.bfloat16))
        mix = jnp.concatenate(mixes, axis=0)
        acc_ref[...] += jnp.dot(tall, mix, preferred_element_type=jnp.float32)
        return _

    lax.fori_loop(0, len(blocks), work, 0)
    if len(out_ref.shape) == 2:
        out_ref[...] = acc_ref[...]
        return
    share = out_ref.shape[2]
    for k in range(nv):
        turned = acc_ref[k * width : (k + 1) * width, :].T
        for r in range(occ // share):
            out_ref[r, order_ref[k]] = turned[r * share : (r + 1) * share, :].astype(out_ref.dtype)


def contract(order, first, factors, sources, blocks, own, carry=None, aux_count=None):
    p_count, width, occ = factors.shape
    nv = p_count // own
    carried, stepping = carry is not None, len(first) > 1
    size = sum(high - low for low, high in blocks[0])
    arrays, placed = [factors], []
    for block in blocks:
        placed.append([])
        for low, high in block:
            places = [(0, 0)]
            for k in range(1, nv):
                start, array = next((a, x) for a, b, x in sources[k] if a <= low and high <= b)
                at = next((n for n, x in enumerate(arrays) if x is array), len(arrays))
                if at == len(arrays):
                    arrays.append(array)
                places.append((at, low - start))
            placed[-1].append((low, high, places))
    if aux_count is None:
        out = [jax.ShapeDtypeStruct((nv * width, occ), jnp.float32)]
    else:
        out = [jax.ShapeDtypeStruct((aux_count, nv, occ // aux_count, width), jnp.bfloat16)]
    if stepping:
        out.append(jax.ShapeDtypeStruct((occ // aux_count + 1, width), jnp.float32))
    in_vmem, in_hbm = pl.BlockSpec(memory_space=pltpu.VMEM), pl.BlockSpec(memory_space=pltpu.HBM)
    body = functools.partial(
        contract_body, nv, placed, size, own, carried, stepping, nv * width * occ
    )
    return pl.pallas_call(
        body,
        in_specs=[pl.BlockSpec(memory_space=pltpu.SMEM)]
        + [in_vmem] * (len(first) + carried)
        + [in_hbm] * len(arrays),
        out_specs=[in_vmem] * len(out),
        out_shape=out,
        scratch_shapes=[
            pltpu.VMEM((nv * width, occ), jnp.float32),
            pltpu.VMEM((occ, nv * width), jnp.bfloat16),
            pltpu.VMEM((len(blocks), nv, size, width, occ), jnp.bfloat16),
            pltpu.SemaphoreType.DMA((len(blocks), nv)),
        ],
        compiler_params=pltpu.CompilerParams(vmem_limit_bytes=46 * 2**20),
        cost_estimate=pl.CostEstimate(flops=0, bytes_accessed=0, transcendentals=0),
    )(order, *first, *([carry] if carried else []), *arrays)


def share_sums(terms, trial, gap):
    count = terms.shape[0]

    def body(terms_ref, trial_ref, gap_ref, ratios_ref, sums_ref):
        coupling = jnp.sum(terms_ref[...].astype(jnp.float32), axis=0)
        share = gap_ref.shape[0]
        diff, scaled, sums = five_sums(trial_ref[:share, :], gap_ref[...], coupling)
        ratios_ref[0] = diff
        ratios_ref[1] = scaled
        ratios_ref[2] = jnp.broadcast_to(trial_ref[share:, :], diff.shape)
        lane = lax.broadcasted_iota(jnp.int32, (1, 128), 1)
        row = jnp.zeros((1, 128), jnp.float32)
        for at, value in enumerate(sums):
            row = jnp.where(lane == at, value, row)
        sums_ref[...] = jnp.broadcast_to(row[None], sums_ref.shape)

    ratios = jax.ShapeDtypeStruct((3, *gap.shape), jnp.float32)
    return pl.pallas_call(
        body,
        out_shape=(ratios, jax.ShapeDtypeStruct((count, 1, 128), jnp.float32)),
        compiler_params=pltpu.CompilerParams(vmem_limit_bytes=24 * 2**20),
    )(terms, trial, gap)


def step_share(ratios, all_sums, total):
    def body(ratios_ref, sums_ref, next_ref, shifts_ref):
        row = jnp.sum(sums_ref[...], axis=0)
        fresh, shift = finish(
            ratios_ref[0], ratios_ref[1], [row[:, at : at + 1] for at in range(5)], total
        )
        next_ref[...] = fresh
        shifts_ref[...] = jnp.concatenate([ratios_ref[2, :1, :1], shift], axis=1)

    return pl.pallas_call(
        body,
        out_shape=(
            jax.ShapeDtypeStruct(ratios.shape[1:], jnp.float32),
            jax.ShapeDtypeStruct((1, 2), jnp.float32),
        ),
    )(ratios, all_sums)


def share_copies(terms):
    def body(terms_ref, copies_ref):
        coupling = jnp.sum(terms_ref[...].astype(jnp.float32), axis=0).astype(jnp.bfloat16)
        copies_ref[...] = jnp.broadcast_to(coupling[None], copies_ref.shape)

    return pl.pallas_call(body, out_shape=jax.ShapeDtypeStruct(terms.shape, jnp.bfloat16))(terms)


def cut_out(whole, start, count):
    parts = 4
    rows = count // parts

    def body(start_ref, whole_ref, out_ref, sems):
        copies = []
        for n in range(parts):
            place = pl.ds(start_ref[0] + n * rows, rows)
            copies.append(
                pltpu.make_async_copy(whole_ref.at[place], out_ref.at[pl.ds(n * rows, rows)], sems.at[n])
            )
        for copy in copies:
            copy.start()
        for copy in copies:
            copy.wait()

    return pl.pallas_call(
        body,
        in_specs=[pl.BlockSpec(memory_space=pltpu.SMEM), pl.BlockSpec(memory_space=pltpu.HBM)],
        out_specs=pl.BlockSpec(memory_space=pltpu.VMEM),
        out_shape=jax.ShapeDtypeStruct((count, *whole.shape[1:]), whole.dtype),
        scratch_shapes=[pltpu.SemaphoreType.DMA((parts,))],
        compiler_params=pltpu.CompilerParams(vmem_limit_bytes=46 * 2**20),
    )(start.astype(jnp.int32)[None], whole)


def spread(share, count, axes=EVERY):
    copies = jnp.broadcast_to(share[None], (count,) + share.shape)
    return lax.all_to_all(copies, axes, 0, 0, tiled=True)


def local(factors, trials, occ_energy, vir_energy):
    na, nv = lax.axis_size("aux"), lax.axis_size("vir")
    count = na * nv
    aux_at, vir_at = lax.axis_index("aux"), lax.axis_index("vir")
    p_count, width, occ = factors.shape
    own = p_count // nv
    share = occ // na
    total = occ * width * nv
    paired = nv & (nv - 1) == 0

    def partner(at, k):
        return at ^ k if paired else (at + k) % nv

    def source(at, k):
        return at ^ k if paired else (at - k) % nv

    def send(value, k):
        return lax.ppermute(value, "vir", [(one, partner(one, k)) for one in range(nv)])

    order = [source(vir_at, k) for k in range(nv)] + [vir_at, aux_at]
    order = jnp.stack(order).astype(jnp.int32)

    unit = own // 16
    cut_up = unit >= 4 and own % 16 == 0
    sources = {k: [] for k in range(1, nv)}

    def piece(k, low, high, whole=factors):
        return lax.dynamic_slice_in_dim(whole, partner(vir_at, k) * own + low, high - low, 0)

    def exchange(k, low, high, part):
        sources[k].append((low, high, send(part, k)))

    def after_newest(k, *values):
        low, high, array = sources[k][-1]
        *values, array = lax.optimization_barrier((*values, array))
        sources[k][-1] = (low, high, array)
        return values

    marks = [0, own]
    if cut_up:
        marks = [0, 9 * unit, own - unit // 2, own]
    far = [k for k in range(nv) if k > 1] + [1]
    later_factors = factors
    for n, k in enumerate(far):
        if cut_up and n == 0:
            cut = cut_out(factors, partner(vir_at, k) * own, marks[1])
        else:
            cut = piece(k, *marks[:2], later_factors)
        if cut_up and n == 0:
            later_factors, cut = lax.optimization_barrier((factors, cut))
        exchange(k, *marks[:2], cut)
    if cut_up:
        later = [[piece(k, low, high, later_factors) for k in far] for low, high in zip(marks[1:], marks[2:])]
        later, trials = lax.optimization_barrier((later, *after_newest(2, trials)))

    gathered = spread(trials[0].T, na, "aux").reshape(occ, width)
    gathered = jnp.concatenate([gathered, vir_energy[None]], axis=0)
    if paired:
        state = {0: gathered}
        bit = nv // 2
        while bit:
            names = sorted(state)
            came = send(jnp.stack([state[k] for k in names]), bit)
            state.update({k ^ bit: came[at] for at, k in enumerate(names)})
            bit //= 2
    else:
        state = {k: send(gathered, k) if k else gathered for k in range(nv)}
    state = jnp.stack([state[k] for k in range(nv)])
    trial = state[:, :occ]
    gap_own = vir_energy[None, :] - lax.dynamic_slice_in_dim(occ_energy, aux_at * share, share)[:, None]
    xt = trial.astype(jnp.bfloat16)

    def call(first, blocks, carry=None, aux_count=None):
        return contract(order, first, factors, sources, blocks, own, carry, aux_count)

    carry = None
    blocks = last_block = [[(0, own)]]
    if cut_up:
        low, high, end = marks[1:]
        for k, cut in enumerate(later[0]):
            exchange(far[k], low, high, cut)
        parts = [(n * low // 4, (n + 1) * low // 4) for n in range(4)]
        middle = (low + high) // 2
        last_block = [[(high, end)]]
        (carry,) = call([xt], [[part] for part in parts])
        cuts, carry = after_newest(2, later[1], carry)
        for k, cut in zip(far, cuts):
            exchange(k, high, end, cut)
        (carry,) = call([xt], [[(low, middle)], [(middle, high)]], carry)
        blocks = []
        for start in range(0, own, 4 * unit):
            points = [start] + [m for m in marks if start < m < start + 4 * unit] + [start + 4 * unit]
            blocks.append(list(zip(points, points[1:])))

    def sum_terms(partial):
        return lax.all_to_all(partial.reshape(count, share, width), EVERY, 0, 0, tiled=True)

    (partial,) = call([xt], last_block, carry, na)
    copies = share_copies(sum_terms(partial))
    first = [lax.all_to_all(copies, EVERY, 0, 0, tiled=True), trial, state[:, occ:], occ_energy[:, None]]
    partial, trial_own = call(first, blocks, None, na)
    ratios, sums = share_sums(sum_terms(partial), trial_own, gap_own)
    sums = lax.all_to_all(sums, EVERY, 0, 0, tiled=True)
    fresh, shifts = step_share(ratios, sums, total)
    return (fresh.T[None], shifts.T)


def solution(mesh):
    placed = (P("aux", "vir", None), P(None, "vir", "aux"), P(), P("vir"))
    return jax.shard_map(
        local, mesh=mesh, in_specs=placed, out_specs=(P(None, "vir", "aux"), P()), check_vma=False
    )
```
